256 devices in a mesh: seq: 32 (over y, z), kvh: 8 (over x, core).
Axes of the slice: x: 4, y: 4, z: 8, core: 2. Of those that a mesh axis runs over, the one named last changes fastest.
Arguments:
- queries: bfloat16 [512, 8192], P(('seq', 'kvh')), may hold values from -47 to 47
- keys: bfloat16 [32768, 1024], P(('seq', 'kvh')), may hold values from -6 to 6
- omega: bfloat16 [32768, 4096], P('seq', 'kvh'), may hold values from -6 to 6
- block_offsets: int32 [4], replicated, may hold values from 0 to 255, as said below
Outputs:
- basis_out: float32 [512, 4096], P('seq', 'kvh')
- projection: float32 [4096, 32768], P('kvh', 'seq')
The draws below stay inside these ranges and needn't reach their ends.
Inputs may be any that keep to these rules, and one draw needn't show every extreme that they name: `block_offsets`: block i lies in [i * s, (i + 1) * s) with s = 64; the first block is 0 and the last is 255.
All inputs are finite; a program needn't handle non-finite values.
Results may differ from the reference program's by a relative error of at most 0.012.
The reference program's roundings to bfloat16 on the way count: a program that leaves them out, or rounds other values in their place, can miss the bound.
Values may be sent and summed in bfloat16 or wider, within the bound.
A program may use at most 64 MiB of HBM per device.

```python
import math
import jax
import jax.numpy as jnp
from jax import lax

HD = 128
HQG = 8
R = 64
POWER = 2
QBLK = 128
QBLOCKS = 4
NQ = 512
NK = 32768
KEY_BLOCKS = 256
KV_HEADS = 8
Q_HEADS = 64


def draw_queries(key, part):
    values = 3.0 * jnp.clip(jax.random.normal(jax.random.fold_in(key, 24), (NQ, Q_HEADS * HD)), -6.0, 6.0)
    return values.astype(jnp.bfloat16)


def draw_keys(key, part):
    values = jnp.clip(jax.random.normal(jax.random.fold_in(key, 33), (NK, KV_HEADS * HD)), -6.0, 6.0)
    return values.astype(jnp.bfloat16)


def draw_block_offsets(key, part):
    stride = KEY_BLOCKS // QBLOCKS
    jitter = jax.random.randint(jax.random.fold_in(key, 41), (QBLOCKS,), 0, stride)
    positions = jnp.arange(QBLOCKS, dtype=jnp.int32)
    offsets = positions * stride + jitter
    offsets = jnp.where(positions == 0, 0, offsets)
    offsets = jnp.where(positions == QBLOCKS - 1, KEY_BLOCKS - 1, offsets)
    return offsets.astype(jnp.int32)


def steps_of(stream_key, dims, split, least, largest):
    def one(dim, blocks):
        heights = jax.random.uniform(jax.random.fold_in(jax.random.fold_in(stream_key, 6), dim), (blocks,), jnp.float32, least / len(split), largest / len(split))
        return jnp.repeat(jnp.exp(heights), dims[dim] // blocks).reshape((-1,) + (1,) * (len(dims) - dim - 1))

    gain = one(*split[0])
    for cut in split[1:]:
        gain = gain * one(*cut)
    return gain


def normal_values(own_key, extent, deviation, reach, shards=(), held_as=jnp.bfloat16):
    loudness = steps_of(own_key, extent, shards, -0.22, 0.18) if shards else 1.0
    values = jax.random.normal(own_key, extent, jnp.float32) * deviation * loudness
    return jnp.minimum(jnp.maximum(values, -reach), reach).astype(held_as)


def setup_inputs(seed: int = 0) -> dict:
    splits = jax.random.split(jax.random.key(seed), 5)
    queries = draw_queries(jax.random.fold_in(splits[4], 71), 0)
    keys = draw_keys(jax.random.fold_in(splits[4], 71), 0)
    omega = normal_values(splits[2], (NK, Q_HEADS * R), 1.0, 6.0, ((0, 32), (1, 8)))
    block_offsets = draw_block_offsets(jax.random.fold_in(splits[4], 71), 0)
    return {"queries": queries, "keys": keys, "omega": omega, "block_offsets": block_offsets}


def orthonormal(sketch):
    gram_total = jnp.dot(sketch.T.astype(jnp.float32), sketch.astype(jnp.float32), precision=lax.Precision.HIGHEST, preferred_element_type=jnp.float32)
    factor = jnp.linalg.cholesky(gram_total)
    return jax.scipy.linalg.solve_triangular(factor, sketch.T, lower=True).T

def reference(queries, keys, omega, block_offsets):
    row_ids = jnp.arange(NQ, dtype=jnp.int32)
    query_pos = block_offsets[row_ids // QBLK] * QBLK + row_ids % QBLK
    key_pos = jnp.arange(NK, dtype=jnp.int32)
    allowed = key_pos[None, :] <= query_pos[:, None]
    inverse_root = 1.0 / math.sqrt(HD)

    def one_head(head_index):
        query_cols = lax.dynamic_slice_in_dim(queries, head_index * HD, HD, 1)
        key_cols = lax.dynamic_slice_in_dim(keys, head_index // HQG * HD, HD, 1)
        omega_cols = lax.dynamic_slice_in_dim(omega, head_index * R, R, 1)
        scores = jnp.dot(query_cols.astype(jnp.float32), key_cols.T.astype(jnp.float32), preferred_element_type=jnp.float32) * inverse_root
        maxima = lax.optimization_barrier(jnp.max(jnp.where(allowed, scores, -1e+30), axis=1, keepdims=True))
        weights = jnp.where(allowed, jnp.exp(scores - maxima), 0.0)
        probabilities = (weights / lax.optimization_barrier(jnp.sum(weights, axis=1, keepdims=True))).astype(jnp.bfloat16)
        basis = orthonormal(jnp.dot(probabilities.astype(jnp.float32), omega_cols.astype(jnp.float32), preferred_element_type=jnp.float32))
        for power_step in range(POWER):
            key_side = jnp.dot(probabilities.T.astype(jnp.float32), basis.astype(jnp.bfloat16).astype(jnp.float32), preferred_element_type=jnp.float32)
            basis = orthonormal(jnp.dot(probabilities.astype(jnp.float32), key_side.astype(jnp.bfloat16).astype(jnp.float32), preferred_element_type=jnp.float32))
        projected = jnp.dot(basis.astype(jnp.bfloat16).T.astype(jnp.float32), probabilities.astype(jnp.float32), preferred_element_type=jnp.float32)
        return (basis, projected)
    bases, projections = lax.map(one_head, jnp.arange(Q_HEADS, dtype=jnp.int32))
    basis_out = jnp.transpose(bases, (1, 0, 2)).reshape(NQ, Q_HEADS * R) * math.sqrt(NQ)
    return (basis_out, projections.reshape(Q_HEADS * R, NK) * math.sqrt(NK))
```

```python
import functools
import math

import jax
import jax.numpy as jnp
from jax import lax
from jax.experimental import pallas as pl
from jax.experimental.pallas import tpu as pltpu
from jax.sharding import PartitionSpec as P

MESH = pl.DeviceIdType.MESH
F32 = jnp.float32
BF16 = jnp.bfloat16
HIGHEST = lax.Precision.HIGHEST

SEQ = 32
KVH = 8
PLANES = 4
RING = 8
HEADS = 8
HEAD = 128
RANK = 64
BLOCK = 128
QUERIES = 512
WIDE = QUERIES - BLOCK
KEYS = 1024
POWER = 2
CHUNK = 128

MASKED = -1e30
LOWEST = -1e29
SCALE = math.log2(math.e) / math.sqrt(HEAD)

LANES = (((1,), (1,)), ((), ()))
PLAIN = (((1,), (0,)), ((), ()))


def dot(left, right, dims=PLAIN, precision=None):
    return lax.dot_general(left, right, dims, precision=precision, preferred_element_type=F32)


def each(count, step, start=0):
    def run(index, carry):
        step(index)
        return carry

    lax.fori_loop(start, count, run, 0)


def inverse_factor(gram):
    lanes = lax.broadcasted_iota(jnp.int32, (RANK, RANK), 1)
    rows = lax.broadcasted_iota(jnp.int32, (RANK, RANK), 0)
    start = jnp.concatenate([gram, jnp.where(lanes == rows, 1.0, 0.0)], axis=1)
    sub = lax.broadcasted_iota(jnp.int32, (8, 2 * RANK), 0)

    def spread(tile, lane):
        return jnp.broadcast_to(tile[:, lane : lane + 1], tile.shape)

    def lift(tile, row):
        return jnp.broadcast_to(tile[row : row + 1, :], tile.shape)

    def block(step, tiles):
        pivot = tiles[0]
        columns = [spread(pivot, j) for j in range(8)]
        inverses, upper, roots = [], [], jnp.zeros_like(pivot)
        for j in range(8):
            diagonal = lift(columns[j], j)
            inverse = 1.0 / diagonal
            inverses.append(inverse)
            roots = jnp.where(sub == j, lax.rsqrt(diagonal), roots)
            factor = jnp.where(sub > j, columns[j] * inverse, 0.0)
            pivot = pivot - factor * lift(pivot, j)
            across = {}
            for other in range(j + 1, 8):
                across[other] = lift(columns[other], j)
                columns[other] = columns[other] - factor * across[other]
            upper.append(across)
        pivot_rows = [lift(pivot, j) for j in range(8)]
        later = []
        for index in range(1, 8):
            tile = tiles[index]
            live = jnp.where(step + index < 8, 1.0, 0.0)
            columns = [spread(tile, j) * live for j in range(8)]
            for j in range(8):
                factor = columns[j] * inverses[j]
                tile = tile - factor * pivot_rows[j]
                for other in range(j + 1, 8):
                    columns[other] = columns[other] - factor * upper[j][other]
            later.append(tile)
        later.append(pivot * roots)
        return tuple(pltpu.roll(tile, 2 * RANK - 8, 1) for tile in later)

    tiles = lax.fori_loop(0, 8, block, tuple(start[8 * i : 8 * i + 8] for i in range(8)))
    return jnp.concatenate(tiles, axis=0)[:, :RANK]


def orthonormal_rows(panel):
    gram = dot(panel, panel, LANES, HIGHEST)
    return dot(inverse_factor(gram), panel, PLAIN, HIGHEST)


def kernel(
    offsets,
    q_ref,
    k_hbm,
    omega_hbm,
    basis_ref,
    proj_hbm,
    q_wide,
    q_tiles,
    q_got,
    q_flat,
    q_turned,
    q_own,
    q_all,
    k_all,
    omega_rows,
    omega_turned,
    scores,
    scores_first,
    probs,
    probs_first,
    stat_out,
    stat_in,
    stat_all,
    part_wide,
    part_wide_in,
    part,
    part_in,
    basis,
    staged,
    local_sem,
    store_sem,
    qk_send,
    qk_recv,
    kk_send,
    kk_recv,
    qs_send,
    qs_recv,
    st_send,
    st_recv,
    pw_send,
    pw_recv,
    sa_send,
    sa_recv,
    pt_send,
    pt_recv,
    bs_send,
    bs_recv,
):
    s = lax.axis_index("seq")
    k = lax.axis_index("kvh")
    y = lax.div(s, RING)
    z = lax.rem(s, RING)
    core = lax.rem(k, 2)

    def owner_of(head):
        return lax.rem(head + core, 2) * RING + head

    owns = owner_of(z) == s

    def to_kvh(src, dst, send, recv, target):
        return pltpu.make_async_remote_copy(
            src_ref=src, dst_ref=dst, send_sem=send, recv_sem=recv,
            device_id={"kvh": target}, device_id_type=MESH,
        )

    def to_seq(src, dst, send, recv, target):
        return pltpu.make_async_remote_copy(
            src_ref=src, dst_ref=dst, send_sem=send, recv_sem=recv,
            device_id={"seq": target}, device_id_type=MESH,
        )

    barrier = pltpu.get_barrier_semaphore()

    def greet_seq(d):
        @pl.when(d != s)
        def _():
            pl.semaphore_signal(barrier, inc=1, device_id={"seq": d}, device_id_type=MESH)

    def greet_kvh(d):
        @pl.when(d != k)
        def _():
            pl.semaphore_signal(barrier, inc=1, device_id={"kvh": d}, device_id_type=MESH)

    each(KVH, greet_kvh)
    each(SEQ, greet_seq)

    omega_copy = pltpu.make_async_copy(omega_hbm, omega_rows, local_sem.at[0])
    omega_copy.start()
    keys_copy = pltpu.make_async_copy(
        k_hbm.at[:, pl.ds(pl.multiple_of(k * HEAD, HEAD), HEAD)], k_all.at[k], local_sem.at[1]
    )
    keys_copy.start()

    q_now = q_ref[...].astype(F32)
    for tile in range(KVH * HEADS):
        q_wide[2 * tile : 2 * tile + 2, :] = q_now[:, tile * HEAD : (tile + 1) * HEAD]
    q_tiles[...] = q_wide[...].astype(BF16).reshape(KVH, 16, HEAD)
    q_got[k] = q_tiles[k]

    def clear_queries(d):
        q_all[:, d] = jnp.zeros((HEADS, 16, HEAD), BF16)

    each(RING * y, clear_queries)
    basis[...] = jnp.zeros(basis.shape, BF16)

    pl.semaphore_wait(barrier, SEQ - 1 + KVH - 1)

    def q_copy(d, slot):
        return to_kvh(q_tiles.at[d], q_got.at[slot], qk_send.at[d], qk_recv.at[slot], d)

    def k_copy(d, slot):
        columns = pl.ds(pl.multiple_of(d * HEAD, HEAD), HEAD)
        return to_kvh(k_hbm.at[:, columns], k_all.at[slot], kk_send.at[d], kk_recv.at[slot], d)

    def others_kvh(step):
        def run(d):
            @pl.when(d != k)
            def _():
                step(d)

        each(KVH, run)

    others_kvh(lambda d: q_copy(d, k).start())
    others_kvh(lambda d: k_copy(d, k).start())
    others_kvh(lambda d: q_copy(d, d).wait_recv())

    q_flat[...] = q_got[...].astype(F32).reshape(KVH * 16, HEAD)
    for pair in range(16):
        q_turned[8 * pair : 8 * pair + 8, :] = q_flat[pl.ds(pair, 8, stride=16), :]
    q_own[...] = q_turned[...].astype(BF16).reshape(HEADS, 16, HEAD)
    q_all[:, s] = q_own[...]

    def q_spread(d, slot):
        return to_seq(q_own, q_all.at[:, slot], qs_send.at[d], qs_recv.at[slot], d)

    def others_seq(step, start=0, stop=SEQ):
        def run(d):
            @pl.when(d != s)
            def _():
                step(d)

        each(stop, run, start)

    others_seq(lambda d: q_spread(d, s).start(), 0, RING * (y + 1))

    omega_copy.wait()
    for tile in range(4):
        turned = omega_rows[:, tile * 128 : (tile + 1) * 128].astype(F32).T.astype(BF16)
        omega_turned[2 * tile] = turned[:RANK]
        omega_turned[2 * tile + 1] = turned[RANK:]

    keys_copy.wait()
    others_kvh(lambda d: k_copy(d, d).wait_recv())
    others_seq(lambda d: q_spread(d, d).wait_recv(), RING * y, SEQ)

    def positions(block, count):
        lane = lax.broadcasted_iota(jnp.int32, (1, count), 1)
        inside = lax.rem(lane, BLOCK)
        place = lax.rem(inside, 16)
        row = inside - place + 2 * lax.rem(place, 8) + lax.div(place, 8)
        which = lax.div(lane, BLOCK) + block
        first = jnp.zeros((1, count), jnp.int32)
        for index in range(4):
            first = jnp.where(which == index, offsets[index], first)
        return first * BLOCK + row - s * KEYS

    limit = positions(1, WIDE)
    limit_first = positions(0, BLOCK)
    key_row = lax.broadcasted_iota(jnp.int32, (CHUNK, 1), 0)

    def fold(tile, join):
        pieces = tile.reshape(CHUNK // 8, 8, tile.shape[1])
        return join(pieces, axis=0)

    def send_part(source, landing, send, recv, head, start):
        target = owner_of(head)
        for plane in range(PLANES):
            @pl.when((y == plane) & (target != s))
            def _():
                blocks = pl.ds(plane, PLANES - plane)
                copy = to_seq(
                    source.at[head, blocks], landing.at[s, blocks], send.at[head], recv.at[s], target
                )
                if start:
                    copy.start()
                else:
                    copy.wait_send()

    def stat_copy(head):
        target = owner_of(head)
        return to_seq(stat_out.at[head], stat_in.at[s], st_send.at[head], st_recv.at[s], target)

    def first_head(index):
        head = lax.rem(index + z, HEADS)
        q_head = q_all[head, 8:32].reshape(WIDE, HEAD)
        largest = jnp.full((8, WIDE), LOWEST, F32)
        for chunk in range(KEYS // CHUNK):
            piece = dot(k_all[chunk], q_head, LANES)
            piece = jnp.where(key_row + chunk * CHUNK <= limit, piece, MASKED)
            scores[head, chunk * CHUNK : (chunk + 1) * CHUNK, :] = piece
            largest = jnp.maximum(largest, fold(piece, jnp.max))
        top = jnp.max(largest, axis=0, keepdims=True)
        total = jnp.zeros((8, WIDE), F32)
        for chunk in range(KEYS // CHUNK):
            at = slice(chunk * CHUNK, (chunk + 1) * CHUNK)
            weight = jnp.exp2((scores[head, at, :] - top) * SCALE)
            total = total + fold(weight, jnp.sum)
            probs[head, at, :] = weight.astype(BF16)
        q_first = q_all[head, 0:8].reshape(BLOCK, HEAD)
        piece = jnp.where(key_row <= limit_first, dot(k_all[0], q_first, LANES), MASKED)
        scores_first[head] = piece
        top_first = jnp.maximum(jnp.max(piece, axis=0, keepdims=True), LOWEST)
        weight = jnp.exp2((piece - top_first) * SCALE)
        probs_first[head] = weight.astype(BF16)
        stat_out[head, 0:1, :] = jnp.concatenate([top_first, top], axis=1)
        stat_out[head, 1:2, :] = jnp.concatenate(
            [jnp.sum(weight, axis=0, keepdims=True), jnp.sum(total, axis=0, keepdims=True)], axis=1
        )
        forward(head, omega_turned[head], part_wide, part_wide_in)

        @pl.when(owner_of(head) == s)
        def _():
            stat_in[s] = stat_out[head]

        @pl.when(owner_of(head) != s)
        def _():
            stat_copy(head).start()

        send_part(part_wide, part_wide_in, pw_send, pw_recv, head, True)

    def forward(head, panel, out, landing):
        product = dot(panel, probs[head])
        first = dot(panel[:, :BLOCK], probs_first[head])
        pieces = [first] + [product[:, b * BLOCK : (b + 1) * BLOCK] for b in range(3)]
        for index, piece in enumerate(pieces):
            out[head, index] = piece.astype(out.dtype)

        @pl.when(owner_of(head) == s)
        def _():
            for index, piece in enumerate(pieces):
                landing[s, index] = piece.astype(out.dtype)

    def backward(head):
        low = jnp.concatenate([basis[head, 1], basis[head, 2], basis[head, 3]], axis=1)
        product = dot(low, probs[head], LANES)
        first = dot(basis[head, 0], probs_first[head], LANES)
        return jnp.concatenate([product[:, :BLOCK] + first, product[:, BLOCK:]], axis=1)

    each(HEADS, first_head)

    def wait_parts(source, landing, send, recv):
        for plane in range(PLANES):
            blocks = pl.ds(plane, PLANES - plane)

            def run(d, blocks=blocks):
                to_seq(
                    source.at[0, blocks], landing.at[d, blocks], send.at[0], recv.at[d], d
                ).wait_recv()

            others_seq(run, plane * RING, plane * RING + RING)

    def stat_share(d):
        return to_seq(stat_all.at[z], stat_all.at[z], sa_send.at[d], sa_recv.at[z], d)

    def basis_share(plane, d, head):
        blocks = pl.ds(plane, PLANES - plane)
        return to_seq(basis.at[head, blocks], basis.at[head, blocks], bs_send.at[d], bs_recv.at[head], d)

    def share_basis(start):
        for plane in range(PLANES):
            def run(d, plane=plane):
                copy = basis_share(plane, d, z)
                if start:
                    copy.start()
                else:
                    copy.wait_send()

            others_seq(run, plane * RING, plane * RING + RING)

    def store_basis(rows):
        for block in range(PLANES):
            basis[z, block] = rows[:, block * BLOCK : (block + 1) * BLOCK].astype(BF16)

    def add_parts(landing, weigh):
        totals = tuple(jnp.zeros((RANK, BLOCK), F32) for _ in range(PLANES))
        for plane in range(PLANES):
            def run(index, totals, plane=plane):
                d = plane * RING + index
                weight = weigh(d)
                return totals[:plane] + tuple(
                    totals[b] + (
                        landing[d, b].astype(F32)
                        if weight is None
                        else landing[d, b] * weight[:, b * BLOCK : (b + 1) * BLOCK]
                    )
                    for b in range(plane, PLANES)
                )

            totals = lax.fori_loop(0, RING, run, totals)
        return jnp.concatenate(totals, axis=1)

    @pl.when(owns)
    def _():
        others_seq(lambda d: to_seq(stat_out.at[0], stat_in.at[d], st_send.at[0], st_recv.at[d], d).wait_recv())
        top = lax.fori_loop(
            0, SEQ, lambda d, so_far: jnp.maximum(so_far, stat_in[d, 0:1, :]),
            jnp.full((1, QUERIES), MASKED, F32),
        )
        total = lax.fori_loop(
            0, SEQ,
            lambda d, so_far: so_far
            + stat_in[d, 1:2, :] * jnp.exp2((stat_in[d, 0:1, :] - top) * SCALE),
            jnp.zeros((1, QUERIES), F32),
        )
        inverse = 1.0 / total
        stat_all[z, 0:1, :] = top
        stat_all[z, 1:2, :] = inverse
        others_seq(lambda d: stat_share(d).start())
        wait_parts(part_wide, part_wide_in, pw_send, pw_recv)
        panel = add_parts(
            part_wide_in, lambda d: jnp.exp2((stat_in[d, 0:1, :] - top) * SCALE)
        ) * inverse
        store_basis(orthonormal_rows(panel))
        share_basis(True)

    def normalise(index):
        head = lax.rem(index + z, HEADS)

        @pl.when(owner_of(head) != s)
        def _():
            to_seq(
                stat_all.at[head], stat_all.at[head], sa_send.at[0], sa_recv.at[head], owner_of(head)
            ).wait_recv()

        top = stat_all[head, 0:1, :]
        inverse = stat_all[head, 1:2, :]
        for chunk in range(KEYS // CHUNK):
            at = slice(chunk * CHUNK, (chunk + 1) * CHUNK)
            weight = jnp.exp2((scores[head, at, :] - top[:, BLOCK:]) * SCALE)
            probs[head, at, :] = (weight * inverse[:, BLOCK:]).astype(BF16)
        weight = jnp.exp2((scores_first[head] - top[:, :BLOCK]) * SCALE)
        probs_first[head] = (weight * inverse[:, :BLOCK]).astype(BF16)

    each(HEADS, normalise)

    def wait_basis(head):
        target = owner_of(head)
        for plane in range(PLANES):
            @pl.when((y == plane) & (target != s))
            def _():
                basis_share(plane, target, head).wait_recv()

    def power_step(step):
        def one_head(index):
            head = lax.rem(index + z, HEADS)
            wait_basis(head)
            forward(head, backward(head).astype(BF16), part, part_in)
            send_part(part, part_in, pt_send, pt_recv, head, True)

        each(HEADS, one_head)

        @pl.when(owns)
        def _():
            wait_parts(part, part_in, pt_send, pt_recv)
            rows = orthonormal_rows(add_parts(part_in, lambda d: None))
            share_basis(False)
            store_basis(rows)
            share_basis(True)

        each(HEADS, lambda head: send_part(part, part_in, pt_send, pt_recv, head, False))

    each(POWER, power_step)

    def store_copy(head):
        rows = pl.ds(pl.multiple_of(head * RANK, RANK), RANK)
        return pltpu.make_async_copy(staged.at[rows], proj_hbm.at[rows], store_sem.at[head])

    def last_head(index):
        head = lax.rem(index + z, HEADS)
        wait_basis(head)
        rows = pl.ds(pl.multiple_of(head * RANK, RANK), RANK)
        staged[rows, :] = backward(head) * math.sqrt(SEQ * KEYS)
        store_copy(head).start()

    each(HEADS, last_head)

    row = lax.broadcasted_iota(jnp.int32, (16, QUERIES), 0)
    lane = lax.broadcasted_iota(jnp.int32, (16, QUERIES), 1)
    chosen = lane == s * 16 + 8 * lax.rem(row, 2) + lax.div(row, 2)
    chosen = jnp.where(chosen, 1.0, 0.0).astype(BF16)
    total = jnp.zeros((16, HEADS * RANK), F32)
    for block in range(PLANES):
        total = total + dot(
            chosen[:, block * BLOCK : (block + 1) * BLOCK],
            basis[:, block].reshape(HEADS * RANK, BLOCK),
            LANES,
        )
    basis_ref[...] = total * math.sqrt(QUERIES)

    each(HEADS, lambda head: store_copy(head).wait())
    others_kvh(lambda d: q_copy(d, k).wait_send())
    others_kvh(lambda d: k_copy(d, k).wait_send())
    others_seq(lambda d: q_spread(d, s).wait_send(), 0, RING * (y + 1))

    def sent(head):
        @pl.when(owner_of(head) != s)
        def _():
            stat_copy(head).wait_send()

        send_part(part_wide, part_wide_in, pw_send, pw_recv, head, False)

    each(HEADS, sent)

    @pl.when(owns)
    def _():
        others_seq(lambda d: stat_share(d).wait_send())
        share_basis(False)


def body(queries, keys, omega, block_offsets):
    vmem = lambda shape, kind: pltpu.VMEM(shape, kind)
    dma = lambda *shape: pltpu.SemaphoreType.DMA(shape)
    return pl.pallas_call(
        kernel,
        out_shape=(
            jax.ShapeDtypeStruct((16, HEADS * RANK), F32),
            jax.ShapeDtypeStruct((HEADS * RANK, KEYS), F32),
        ),
        in_specs=[
            pl.BlockSpec(memory_space=pltpu.SMEM),
            pl.BlockSpec(memory_space=pltpu.VMEM),
            pl.BlockSpec(memory_space=pl.ANY),
            pl.BlockSpec(memory_space=pl.ANY),
        ],
        out_specs=(
            pl.BlockSpec(memory_space=pltpu.VMEM),
            pl.BlockSpec(memory_space=pl.ANY),
        ),
        scratch_shapes=[
            vmem((128, HEAD), F32),
            vmem((KVH, 16, HEAD), BF16),
            vmem((KVH, 16, HEAD), BF16),
            vmem((128, HEAD), F32),
            vmem((128, HEAD), F32),
            vmem((HEADS, 16, HEAD), BF16),
            vmem((HEADS, SEQ, 16, HEAD), BF16),
            vmem((KVH, 128, HEAD), BF16),
            vmem((KEYS, HEADS * RANK), BF16),
            vmem((HEADS, RANK, KEYS), BF16),
            vmem((HEADS, KEYS, WIDE), F32),
            vmem((HEADS, BLOCK, BLOCK), F32),
            vmem((HEADS, KEYS, WIDE), BF16),
            vmem((HEADS, BLOCK, BLOCK), BF16),
            vmem((HEADS, 2, QUERIES), F32),
            vmem((SEQ, 2, QUERIES), F32),
            vmem((HEADS, 2, QUERIES), F32),
            vmem((HEADS, PLANES, RANK, BLOCK), F32),
            vmem((SEQ, PLANES, RANK, BLOCK), F32),
            vmem((HEADS, PLANES, RANK, BLOCK), BF16),
            vmem((SEQ, PLANES, RANK, BLOCK), BF16),
            vmem((HEADS, PLANES, RANK, BLOCK), BF16),
            vmem((HEADS * RANK, KEYS), F32),
            dma(2),
            dma(HEADS),
            dma(KVH), dma(KVH),
            dma(KVH), dma(KVH),
            dma(SEQ), dma(SEQ),
            dma(HEADS), dma(SEQ),
            dma(HEADS), dma(SEQ),
            dma(SEQ), dma(HEADS),
            dma(HEADS), dma(SEQ),
            dma(SEQ), dma(HEADS),
        ],
        compiler_params=pltpu.CompilerParams(
            collective_id=0, has_side_effects=True, vmem_limit_bytes=56 * 2**20
        ),
        cost_estimate=pl.CostEstimate(
            flops=6 * 10**9, bytes_accessed=8 * 2**20, transcendentals=8 * 10**6
        ),
        name="range_finder",
    )(block_offsets, queries, keys, omega)


def solution(mesh):
    placed = (P(("seq", "kvh"), None), P(("seq", "kvh"), None), P("seq", "kvh"), P())
    return jax.shard_map(
        body,
        mesh=mesh,
        in_specs=placed,
        out_specs=(P("seq", "kvh"), P("kvh", "seq")),
        check_vma=False,
    )
```

```python
import functools
import math

import jax
import jax.numpy as jnp
from jax import lax
from jax.experimental import pallas as pl
from jax.experimental.pallas import tpu as pltpu
from jax.sharding import PartitionSpec as P

MESH = pl.DeviceIdType.MESH
F32 = jnp.float32
BF16 = jnp.bfloat16
HIGHEST = lax.Precision.HIGHEST

SEQ = 32
KVH = 8
PLANES = 4
RING = 8
HEADS = 8
HEAD = 128
RANK = 64
BLOCK = 128
QUERIES = 512
WIDE = QUERIES - BLOCK
KEYS = 1024
POWER = 2
CHUNK = 128

MASKED = -1e30
LOWEST = -1e29
SCALE = math.log2(math.e) / math.sqrt(HEAD)

LANES = (((1,), (1,)), ((), ()))
PLAIN = (((1,), (0,)), ((), ()))


def dot(left, right, dims=PLAIN, precision=None):
    return lax.dot_general(left, right, dims, precision=precision, preferred_element_type=F32)


def each(count, step, start=0):
    def run(index, carry):
        step(index)
        return carry

    lax.fori_loop(start, count, run, 0)


def inverse_factor(gram):
    lanes = lax.broadcasted_iota(jnp.int32, (RANK, RANK), 1)
    rows = lax.broadcasted_iota(jnp.int32, (RANK, RANK), 0)
    start = jnp.concatenate([gram, jnp.where(lanes == rows, 1.0, 0.0)], axis=1)
    sub = lax.broadcasted_iota(jnp.int32, (8, 2 * RANK), 0)

    def spread(tile, lane):
        return jnp.broadcast_to(tile[:, lane : lane + 1], tile.shape)

    def lift(tile, row):
        return jnp.broadcast_to(tile[row : row + 1, :], tile.shape)

    def block(step, tiles):
        pivot = tiles[0]
        columns = [spread(pivot, j) for j in range(8)]
        inverses, upper, roots = [], [], jnp.zeros_like(pivot)
        for j in range(8):
            diagonal = lift(columns[j], j)
            inverse = 1.0 / diagonal
            inverses.append(inverse)
            roots = jnp.where(sub == j, lax.rsqrt(diagonal), roots)
            factor = jnp.where(sub > j, columns[j] * inverse, 0.0)
            pivot = pivot - factor * lift(pivot, j)
            across = {}
            for other in range(j + 1, 8):
                across[other] = lift(columns[other], j)
                columns[other] = columns[other] - factor * across[other]
            upper.append(across)
        pivot_rows = [lift(pivot, j) for j in range(8)]
        later = []
        for index in range(1, 8):
            tile = tiles[index]
            live = jnp.where(step + index < 8, 1.0, 0.0)
            columns = [spread(tile, j) * live for j in range(8)]
            for j in range(8):
                factor = columns[j] * inverses[j]
                tile = tile - factor * pivot_rows[j]
                for other in range(j + 1, 8):
                    columns[other] = columns[other] - factor * upper[j][other]
            later.append(tile)
        later.append(pivot * roots)
        return tuple(pltpu.roll(tile, 2 * RANK - 8, 1) for tile in later)

    tiles = lax.fori_loop(0, 8, block, tuple(start[8 * i : 8 * i + 8] for i in range(8)))
    return jnp.concatenate(tiles, axis=0)[:, :RANK]


def orthonormal_rows(panel):
    gram = dot(panel, panel, LANES, HIGHEST)
    return dot(inverse_factor(gram), panel, PLAIN, HIGHEST)


def kernel(
    offsets,
    q_ref,
    k_hbm,
    omega_hbm,
    basis_ref,
    proj_hbm,
    q_wide,
    q_tiles,
    q_got,
    q_flat,
    q_turned,
    q_own,
    q_all,
    k_all,
    omega_rows,
    omega_turned,
    scores,
    scores_first,
    probs,
    probs_first,
    stat_out,
    stat_y,
    stat_sum,
    stat_z,
    stat_all,
    wide_out,
    wide_y,
    wide_sum,
    wide_z,
    part_out,
    part_y,
    part_sum,
    part_z,
    basis,
    staged,
    local_sem,
    store_sem,
    qk_send,
    qk_recv,
    kk_send,
    kk_recv,
    qz_send,
    qf_send,
    q_recv,
    sty_send,
    sty_recv,
    stz_send,
    stz_recv,
    sta_send,
    stb_send,
    st_recv,
    wy_send,
    wy_recv,
    wz_send,
    wz_recv,
    py_send,
    py_recv,
    pz_send,
    pz_recv,
    bz_send,
    by_send,
    b_recv,
):
    s = lax.axis_index("seq")
    k = lax.axis_index("kvh")
    y = lax.div(s, RING)
    z = lax.rem(s, RING)
    core = lax.rem(k, 2)

    def owner_z(j):
        return 2 * (2 * j + core)

    own_j = lax.div(z, 4)
    own_head = 2 * y + own_j
    owns = owner_z(own_j) == z

    def at_seq(plane, place):
        return plane * RING + place

    def remote(src, dst, send, recv, **target):
        return pltpu.make_async_remote_copy(
            src_ref=src, dst_ref=dst, send_sem=send, recv_sem=recv,
            device_id=target, device_id_type=MESH,
        )

    def others(count, me, step):
        def run(d):
            @pl.when(d != me)
            def _():
                step(d)

        each(count, run)

    barrier = pltpu.get_barrier_semaphore()

    def greet(**target):
        pl.semaphore_signal(barrier, inc=1, device_id=target, device_id_type=MESH)

    others(KVH, k, lambda d: greet(kvh=d))
    others(RING, z, lambda d: greet(seq=at_seq(y, d)))
    others(PLANES, y, lambda d: greet(seq=at_seq(d, z)))

    omega_copy = pltpu.make_async_copy(omega_hbm, omega_rows, local_sem.at[0])
    omega_copy.start()
    keys_copy = pltpu.make_async_copy(
        k_hbm.at[:, pl.ds(pl.multiple_of(k * HEAD, HEAD), HEAD)], k_all.at[k], local_sem.at[1]
    )
    keys_copy.start()

    q_now = q_ref[...].astype(F32)
    for tile in range(KVH * HEADS):
        q_wide[2 * tile : 2 * tile + 2, :] = q_now[:, tile * HEAD : (tile + 1) * HEAD]
    q_tiles[...] = q_wide[...].astype(BF16).reshape(KVH, 16, HEAD)
    q_got[k] = q_tiles[k]

    basis[...] = jnp.zeros(basis.shape, BF16)
    probs_first[...] = jnp.zeros(probs_first.shape, BF16)
    stat_out[:, 0:1, :] = jnp.full((HEADS, 1, QUERIES), LOWEST, F32)
    stat_out[:, 1:2, :] = jnp.zeros((HEADS, 1, QUERIES), F32)

    @pl.when(y >= 2)
    def _():
        def clear(head):
            probs[head] = jnp.zeros((KEYS, WIDE), BF16)

        each(HEADS, clear)

    pl.semaphore_wait(barrier, KVH - 1 + RING - 1 + PLANES - 1)

    def q_copy(d, slot):
        return remote(q_tiles.at[d], q_got.at[slot], qk_send.at[d], qk_recv.at[slot], kvh=d)

    def k_copy(d, slot):
        columns = pl.ds(pl.multiple_of(d * HEAD, HEAD), HEAD)
        return remote(k_hbm.at[:, columns], k_all.at[slot], kk_send.at[d], kk_recv.at[slot], kvh=d)

    others(KVH, k, lambda d: q_copy(d, k).start())
    others(KVH, k, lambda d: k_copy(d, k).start())
    others(KVH, k, lambda d: q_copy(d, d).wait_recv())

    q_flat[...] = q_got[...].astype(F32).reshape(KVH * 16, HEAD)
    for pair in range(16):
        q_turned[8 * pair : 8 * pair + 8, :] = q_flat[pl.ds(pair, 8, stride=16), :]
    q_own[...] = q_turned[...].astype(BF16).reshape(HEADS, 16, HEAD)
    q_all[:, s] = q_own[...]

    def q_round(d):
        return remote(q_own, q_all.at[:, s], qz_send.at[d], q_recv.at[s], seq=at_seq(y, d))

    def q_pass(piece, way, plane):
        return remote(
            q_all.at[:, piece], q_all.at[:, piece], qf_send.at[way, piece], q_recv.at[piece],
            seq=at_seq(plane, z),
        )

    def q_arrived(piece):
        remote(q_own, q_all.at[:, piece], qz_send.at[0], q_recv.at[piece], seq=piece).wait_recv()

    def q_rounds(step):
        def run(index):
            d = lax.rem(z + index, RING)

            @pl.when((y > 0) | (d == 0))
            def _():
                step(d)

        each(RING, run, 1)

    q_rounds(lambda d: q_round(d).start())

    def pass_block(block, own, targets, start):
        def run(index):
            piece = at_seq(block, lax.rem(z + index, RING))
            if start:
                if own:
                    @pl.when(index > 0)
                    def _():
                        q_arrived(piece)
                else:
                    q_arrived(piece)
            for way, plane in enumerate(targets):
                copy = q_pass(piece, way, plane)
                if start:
                    copy.start()
                else:
                    copy.wait_send()

        each(RING, run)

    def pass_all(start):
        @pl.when(y == 3)
        def _():
            pass_block(3, True, (0, 2), start)

        @pl.when(y == 2)
        def _():
            pass_block(2, True, (1,), start)

        @pl.when(y == 1)
        def _():
            pass_block(1, True, (0,), start)
            pass_block(2, False, (0,), start)

        @pl.when(y == 0)
        def _():
            pass_block(3, False, (1,), start)

    omega_copy.wait()
    for tile in range(4):
        turned = omega_rows[:, tile * 128 : (tile + 1) * 128].astype(F32).T.astype(BF16)
        omega_turned[2 * tile] = turned[:RANK]
        omega_turned[2 * tile + 1] = turned[RANK:]

    pass_all(True)
    keys_copy.wait()
    others(KVH, k, lambda d: k_copy(d, d).wait_recv())

    lane = lax.broadcasted_iota(jnp.int32, (1, BLOCK), 1)
    place = lax.rem(lane, 16)
    row_in_block = lane - place + 2 * lax.rem(place, 8) + lax.div(place, 8)
    key_row = lax.broadcasted_iota(jnp.int32, (CHUNK, 1), 0)

    def limits(block):
        return offsets[block] * BLOCK + row_in_block - s * KEYS

    def fold(tile, join):
        return join(tile.reshape(CHUNK // 8, 8, tile.shape[1]), axis=0)

    def head_at(index):
        turn = lax.div(index, 2)
        turn = jnp.where(turn < 2, turn, 5 - turn)
        plane = lax.rem(y + turn, PLANES)
        return plane, lax.rem(index, 2), 2 * plane + lax.rem(index, 2)

    def spans(plane, act, everything=False):
        if isinstance(plane, int):
            if plane:
                act(plane)
            elif everything:
                act(0)
            else:
                pl.when(z == 0)(lambda: act(0))
                pl.when(z != 0)(lambda: act(1))
        else:
            if everything:
                pl.when(plane == 0)(lambda: act(0))
                pl.when(plane == 1)(lambda: act(1))
            else:
                pl.when((plane == 0) & (z == 0))(lambda: act(0))
                pl.when((plane == 1) | ((plane == 0) & (z != 0)))(lambda: act(1))
            pl.when(plane == 2)(lambda: act(2))
            pl.when(plane == 3)(lambda: act(3))

    def cut(ref, *place, first):
        return ref.at[(*place, pl.ds(first, PLANES - first))]

    def y_send(out, landing, send, recv, head, plane, j, start):
        @pl.when(plane != y)
        def _():
            def act(first):
                copy = remote(
                    cut(out, head, first=first), cut(landing, y, j, first=first),
                    send.at[head], recv.at[y, j], seq=at_seq(plane, z),
                )
                if start:
                    copy.start()
                else:
                    copy.wait_send()

            spans(y, act)

    def y_wait(out, landing, send, recv, j):
        for plane in range(PLANES):
            @pl.when(plane != y)
            def _():
                def act(first):
                    remote(
                        cut(out, 0, first=first), cut(landing, plane, j, first=first),
                        send.at[0], recv.at[plane, j], seq=at_seq(plane, z),
                    ).wait_recv()

                spans(plane, act)

    def z_send(through, landing, send, recv, j, start):
        target = owner_z(j)

        @pl.when(target != z)
        def _():
            def act(first):
                copy = remote(
                    cut(through, j, first=first), cut(landing, z, first=first),
                    send.at[j], recv.at[z], seq=at_seq(y, target),
                )
                if start:
                    copy.start()
                else:
                    copy.wait_send()

            spans(0, act)

    def z_wait(through, landing, send, recv):
        def run(d):
            for first in (0, 1):
                @pl.when((d == 0) if first == 0 else (d != 0))
                def _():
                    remote(
                        cut(through, 0, first=first), cut(landing, d, first=first),
                        send.at[0], recv.at[d], seq=at_seq(y, d),
                    ).wait_recv()

        others(RING, z, run)

    def stat_y_copy(head, plane, j, source):
        return remote(
            stat_out.at[head], stat_y.at[source, j], sty_send.at[head], sty_recv.at[source, j],
            seq=at_seq(plane, z),
        )

    def first_block(block, columns, head):
        q_head = q_all[head, pl.ds(pl.multiple_of(8 * block, 8), 8)].reshape(BLOCK, HEAD)
        limit = limits(block)
        largest = jnp.full((8, BLOCK), LOWEST, F32)
        for chunk in range(KEYS // CHUNK):
            piece = dot(k_all[chunk], q_head, LANES)
            piece = jnp.where(key_row + chunk * CHUNK <= limit, piece, MASKED)
            scores[head, chunk * CHUNK : (chunk + 1) * CHUNK, columns] = piece
            largest = jnp.maximum(largest, fold(piece, jnp.max))
        top = jnp.max(largest, axis=0, keepdims=True)
        total = jnp.zeros((8, BLOCK), F32)
        for chunk in range(KEYS // CHUNK):
            at = slice(chunk * CHUNK, (chunk + 1) * CHUNK)
            weight = jnp.exp2((scores[head, at, columns] - top) * SCALE)
            total = total + fold(weight, jnp.sum)
            probs[head, at, columns] = weight.astype(BF16)
        place = pl.ds(pl.multiple_of(block * BLOCK, BLOCK), BLOCK)
        stat_out[head, 0:1, place] = top
        stat_out[head, 1:2, place] = jnp.sum(total, axis=0, keepdims=True)
        wide_out[head, block] = dot(omega_turned[head], probs[head, :, columns])

    def block_zero(head):
        q_head = q_all[head, 0:8].reshape(BLOCK, HEAD)
        piece = jnp.where(key_row <= limits(0), dot(k_all[0], q_head, LANES), MASKED)
        scores_first[head] = piece
        top = jnp.max(piece, axis=0, keepdims=True)
        weight = jnp.exp2((piece - top) * SCALE)
        probs_first[head] = weight.astype(BF16)
        stat_out[head, 0:1, :BLOCK] = top
        stat_out[head, 1:2, :BLOCK] = jnp.sum(weight, axis=0, keepdims=True)
        wide_out[head, 0] = dot(omega_turned[head, :, :BLOCK], probs_first[head])

    @pl.when(s == 0)
    def _():
        others(RING, z, q_arrived)
        each(HEADS, block_zero)

    steps = jnp.where(y == 0, 3, PLANES - y)

    def one_block(step):
        block = jnp.where(y == 0, jnp.where(step == 0, 3, step), y + step)
        columns = pl.ds(pl.multiple_of((block - 1) * BLOCK, BLOCK), BLOCK)

        @pl.when(jnp.where(y == 0, block != 3, (block == 3) & (y < 3)))
        def _():
            each(RING, lambda d: q_arrived(at_seq(block, d)))

        def run(index):
            plane, j, head = head_at(index)
            first_block(block, columns, head)

            @pl.when(step == steps - 1)
            def _():
                @pl.when(plane != y)
                def _():
                    stat_y_copy(head, plane, j, y).start()

                y_send(wide_out, wide_y, wy_send, wy_recv, head, plane, j, True)

                @pl.when(plane == y)
                def _():
                    wide_y[y, j] = wide_out[head]
                    stat_y[y, j] = stat_out[head]

        each(HEADS, run)

    each(steps, one_block)

    def merge_scale(value, top):
        return jnp.exp2((value - top) * SCALE)

    def block_of(row, block):
        return row[:, block * BLOCK : (block + 1) * BLOCK]

    def join_wide(j):
        for plane in range(PLANES):
            @pl.when(plane != y)
            def _():
                stat_y_copy(0, plane, j, plane).wait_recv()

        tops = [stat_y[p, j, 0:1, :] for p in range(PLANES)]
        top = functools.reduce(jnp.maximum, tops)
        scales = [merge_scale(value, top) for value in tops]
        stat_sum[j, 0:1, :] = top
        stat_sum[j, 1:2, :] = sum(stat_y[p, j, 1:2, :] * scales[p] for p in range(PLANES))

        @pl.when(owner_z(j) == z)
        def _():
            stat_z[z] = stat_sum[j]

        @pl.when(owner_z(j) != z)
        def _():
            stat_z_copy(j, z).start()

        y_wait(wide_out, wide_y, wy_send, wy_recv, j)
        for block in range(1, PLANES):
            wide_sum[j, block] = sum(
                wide_y[p, j, block] * block_of(scales[p], block) for p in range(block + 1)
            )

        @pl.when(z == 0)
        def _():
            wide_sum[j, 0] = wide_y[0, j, 0] * block_of(scales[0], 0)

        @pl.when(owner_z(j) == z)
        def _():
            wide_z[z] = wide_sum[j]

        z_send(wide_sum, wide_z, wz_send, wz_recv, j, True)

    def stat_z_copy(j, source):
        return remote(
            stat_sum.at[j], stat_z.at[source], stz_send.at[j], stz_recv.at[source],
            seq=at_seq(y, owner_z(j)),
        )

    join_wide(0)
    join_wide(1)

    def stat_share(d):
        return remote(
            stat_all.at[own_head], stat_all.at[own_head], sta_send.at[d], st_recv.at[own_head],
            seq=at_seq(y, d),
        )

    def basis_share(d):
        return remote(
            basis.at[own_head], basis.at[own_head], bz_send.at[d], b_recv.at[own_head],
            seq=at_seq(y, d),
        )

    def store_basis(rows):
        for block in range(PLANES):
            basis[own_head, block] = block_of(rows, block).astype(BF16)

    @pl.when(owns)
    def _():
        others(RING, z, lambda d: stat_z_copy(0, d).wait_recv())
        top = functools.reduce(jnp.maximum, [stat_z[d, 0:1, :] for d in range(RING)])
        scales = [merge_scale(stat_z[d, 0:1, :], top) for d in range(RING)]
        inverse = 1.0 / sum(stat_z[d, 1:2, :] * scales[d] for d in range(RING))
        stat_all[own_head, 0:1, :] = top
        stat_all[own_head, 1:2, :] = inverse
        others(RING, z, lambda d: stat_share(d).start())
        z_wait(wide_sum, wide_z, wz_send, wz_recv)
        pieces = [wide_z[0, 0] * block_of(scales[0], 0)]
        for block in range(1, PLANES):
            pieces.append(sum(wide_z[d, block] * block_of(scales[d], block) for d in range(RING)))
        store_basis(orthonormal_rows(jnp.concatenate(pieces, axis=1) * inverse))
        others(RING, z, lambda d: basis_share(d).start())

    def stat_pass(j, plane):
        head = 2 * y + j
        return remote(
            stat_all.at[head], stat_all.at[head], stb_send.at[j, plane], st_recv.at[head],
            seq=at_seq(plane, z),
        )

    def stat_wait(head):
        remote(stat_all.at[head], stat_all.at[head], sta_send.at[0], st_recv.at[head], seq=s).wait_recv()

    def relay_stats(j):
        @pl.when(owner_z(j) != z)
        def _():
            stat_wait(2 * y + j)

        others(PLANES, y, lambda plane: stat_pass(j, plane).start())

    def relay_basis(j, last, start):
        head = 2 * y + j
        if start:
            @pl.when(owner_z(j) != z)
            def _():
                remote(
                    basis.at[head], basis.at[head], bz_send.at[0], b_recv.at[head], seq=s
                ).wait_recv()

        for plane in range(PLANES):
            @pl.when(plane != y)
            def _():
                def act(first):
                    copy = remote(
                        cut(basis, head, first=first), cut(basis, head, first=first),
                        by_send.at[j, plane], b_recv.at[head], seq=at_seq(plane, z),
                    )
                    if start:
                        copy.start()
                    else:
                        copy.wait_send()

                spans(plane, act, last)

    def wait_basis(plane, head, last):
        @pl.when(plane != y)
        def _():
            def act(first):
                remote(
                    cut(basis, head, first=first), cut(basis, head, first=first),
                    by_send.at[0, 0], b_recv.at[head], seq=at_seq(plane, z),
                ).wait_recv()

            spans(y, act, last)

    relay_stats(0)
    relay_stats(1)

    def normalise(index):
        plane, j, head = head_at(index)

        @pl.when(plane != y)
        def _():
            stat_wait(head)

        def run(block):
            columns = pl.ds(pl.multiple_of((block - 1) * BLOCK, BLOCK), BLOCK)
            place = pl.ds(pl.multiple_of(block * BLOCK, BLOCK), BLOCK)
            top = stat_all[head, 0:1, place]
            inverse = stat_all[head, 1:2, place]
            for chunk in range(KEYS // CHUNK):
                at = slice(chunk * CHUNK, (chunk + 1) * CHUNK)
                weight = merge_scale(scores[head, at, columns], top)
                probs[head, at, columns] = (weight * inverse).astype(BF16)

        each(PLANES, run, jnp.maximum(y, 1))

        @pl.when(s == 0)
        def _():
            weight = merge_scale(scores_first[head], stat_all[head, 0:1, :BLOCK])
            probs_first[head] = (weight * stat_all[head, 1:2, :BLOCK]).astype(BF16)

    @pl.when(owns)
    def _():
        relay_basis(own_j, False, True)

    each(HEADS, normalise)

    def forward(head, plane, j, panel):
        product = dot(panel, probs[head]).astype(BF16)
        for b in range(3):
            part_out[head, b + 1] = product[:, b * BLOCK : (b + 1) * BLOCK]

        @pl.when(s == 0)
        def _():
            part_out[head, 0] = dot(panel[:, :BLOCK], probs_first[head]).astype(BF16)

        @pl.when(plane == y)
        def _():
            part_y[y, j] = part_out[head]

    def backward(head):
        low = jnp.concatenate([basis[head, 1], basis[head, 2], basis[head, 3]], axis=1)
        product = dot(low, probs[head], LANES)
        first = dot(basis[head, 0], probs_first[head], LANES)
        return jnp.concatenate([product[:, :BLOCK] + first, product[:, BLOCK:]], axis=1)

    def join_parts(j):
        y_wait(part_out, part_y, py_send, py_recv, j)
        relay_basis(j, False, False)
        for block in range(1, PLANES):
            part_sum[j, block] = sum(
                part_y[p, j, block].astype(F32) for p in range(block + 1)
            ).astype(BF16)

        @pl.when(z == 0)
        def _():
            part_sum[j, 0] = part_y[0, j, 0]

        @pl.when(owner_z(j) == z)
        def _():
            part_z[z] = part_sum[j]

        z_send(part_sum, part_z, pz_send, pz_recv, j, True)

    def start_relays(last, first_round):
        for j in range(2):
            if first_round is None:
                relay_basis(j, last, True)
            else:
                @pl.when(jnp.logical_not(first_round & (owner_z(j) == z)))
                def _():
                    relay_basis(j, last, True)

    def power_step(step):
        start_relays(False, step == 0)

        def one_head(index):
            plane, j, head = head_at(index)
            wait_basis(plane, head, False)
            forward(head, plane, j, backward(head).astype(BF16))
            y_send(part_out, part_y, py_send, py_recv, head, plane, j, True)

        each(HEADS, one_head)
        join_parts(0)
        join_parts(1)

        @pl.when(owns)
        def _():
            z_wait(part_sum, part_z, pz_send, pz_recv)
            pieces = [part_z[0, 0].astype(F32)]
            for block in range(1, PLANES):
                pieces.append(sum(part_z[d, block].astype(F32) for d in range(RING)))
            rows = orthonormal_rows(jnp.concatenate(pieces, axis=1))
            others(RING, z, lambda d: basis_share(d).wait_send())
            store_basis(rows)
            others(RING, z, lambda d: basis_share(d).start())

        def sent(index):
            plane, j, head = head_at(index)
            y_send(part_out, part_y, py_send, py_recv, head, plane, j, False)

        each(HEADS, sent)
        z_send(part_sum, part_z, pz_send, pz_recv, 0, False)
        z_send(part_sum, part_z, pz_send, pz_recv, 1, False)

    each(POWER, power_step)

    def store_copy(head):
        rows = pl.ds(pl.multiple_of(head * RANK, RANK), RANK)
        return pltpu.make_async_copy(staged.at[rows], proj_hbm.at[rows], store_sem.at[head])

    start_relays(True, None)

    def last_head(index):
        plane, j, head = head_at(index)
        wait_basis(plane, head, True)
        rows = pl.ds(pl.multiple_of(head * RANK, RANK), RANK)
        staged[rows, :] = backward(head) * math.sqrt(SEQ * KEYS)
        store_copy(head).start()

    each(HEADS, last_head)

    row = lax.broadcasted_iota(jnp.int32, (16, QUERIES), 0)
    lane = lax.broadcasted_iota(jnp.int32, (16, QUERIES), 1)
    chosen = lane == s * 16 + 8 * lax.rem(row, 2) + lax.div(row, 2)
    chosen = jnp.where(chosen, 1.0, 0.0).astype(BF16)
    total = jnp.zeros((16, HEADS * RANK), F32)
    for block in range(PLANES):
        total = total + dot(
            chosen[:, block * BLOCK : (block + 1) * BLOCK],
            basis[:, block].reshape(HEADS * RANK, BLOCK),
            LANES,
        )
    basis_ref[...] = total * math.sqrt(QUERIES)

    each(HEADS, lambda head: store_copy(head).wait())
    others(KVH, k, lambda d: q_copy(d, k).wait_send())
    others(KVH, k, lambda d: k_copy(d, k).wait_send())
    q_rounds(lambda d: q_round(d).wait_send())
    pass_all(False)

    def sent_wide(index):
        plane, j, head = head_at(index)

        @pl.when(plane != y)
        def _():
            stat_y_copy(head, plane, j, y).wait_send()

        y_send(wide_out, wide_y, wy_send, wy_recv, head, plane, j, False)

    each(HEADS, sent_wide)
    for j in range(2):
        z_send(wide_sum, wide_z, wz_send, wz_recv, j, False)

        @pl.when(owner_z(j) != z)
        def _():
            stat_z_copy(j, z).wait_send()

        others(PLANES, y, lambda plane: stat_pass(j, plane).wait_send())
        relay_basis(j, True, False)

    @pl.when(owns)
    def _():
        others(RING, z, lambda d: stat_share(d).wait_send())
        others(RING, z, lambda d: basis_share(d).wait_send())


def body(queries, keys, omega, block_offsets):
    vmem = lambda shape, kind: pltpu.VMEM(shape, kind)
    dma = lambda *shape: pltpu.SemaphoreType.DMA(shape)
    panel = (PLANES, RANK, BLOCK)
    return pl.pallas_call(
        kernel,
        out_shape=(
            jax.ShapeDtypeStruct((16, HEADS * RANK), F32),
            jax.ShapeDtypeStruct((HEADS * RANK, KEYS), F32),
        ),
        in_specs=[
            pl.BlockSpec(memory_space=pltpu.SMEM),
            pl.BlockSpec(memory_space=pltpu.VMEM),
            pl.BlockSpec(memory_space=pl.ANY),
            pl.BlockSpec(memory_space=pl.ANY),
        ],
        out_specs=(
            pl.BlockSpec(memory_space=pltpu.VMEM),
            pl.BlockSpec(memory_space=pl.ANY),
        ),
        scratch_shapes=[
            vmem((128, HEAD), F32),
            vmem((KVH, 16, HEAD), BF16),
            vmem((KVH, 16, HEAD), BF16),
            vmem((128, HEAD), F32),
            vmem((128, HEAD), F32),
            vmem((HEADS, 16, HEAD), BF16),
            vmem((HEADS, SEQ, 16, HEAD), BF16),
            vmem((KVH, 128, HEAD), BF16),
            vmem((KEYS, HEADS * RANK), BF16),
            vmem((HEADS, RANK, KEYS), BF16),
            vmem((HEADS, KEYS, WIDE), F32),
            vmem((HEADS, BLOCK, BLOCK), F32),
            vmem((HEADS, KEYS, WIDE), BF16),
            vmem((HEADS, BLOCK, BLOCK), BF16),
            vmem((HEADS, 2, QUERIES), F32),
            vmem((PLANES, 2, 2, QUERIES), F32),
            vmem((2, 2, QUERIES), F32),
            vmem((RING, 2, QUERIES), F32),
            vmem((HEADS, 2, QUERIES), F32),
            vmem((HEADS, *panel), F32),
            vmem((PLANES, 2, *panel), F32),
            vmem((2, *panel), F32),
            vmem((RING, *panel), F32),
            vmem((HEADS, *panel), BF16),
            vmem((PLANES, 2, *panel), BF16),
            vmem((2, *panel), BF16),
            vmem((RING, *panel), BF16),
            vmem((HEADS, *panel), BF16),
            vmem((HEADS * RANK, KEYS), F32),
            dma(2),
            dma(HEADS),
            dma(KVH), dma(KVH),
            dma(KVH), dma(KVH),
            dma(RING), dma(2, SEQ), dma(SEQ),
            dma(HEADS), dma(PLANES, 2),
            dma(2), dma(RING),
            dma(RING), dma(2, PLANES), dma(HEADS),
            dma(HEADS), dma(PLANES, 2),
            dma(2), dma(RING),
            dma(HEADS), dma(PLANES, 2),
            dma(2), dma(RING),
            dma(RING), dma(2, PLANES), dma(HEADS),
        ],
        compiler_params=pltpu.CompilerParams(
            collective_id=0, has_side_effects=True, vmem_limit_bytes=56 * 2**20
        ),
        cost_estimate=pl.CostEstimate(
            flops=6 * 10**9, bytes_accessed=8 * 2**20, transcendentals=8 * 10**6
        ),
        name="range_finder",
    )(block_offsets, queries, keys, omega)


def solution(mesh):
    placed = (P(("seq", "kvh"), None), P(("seq", "kvh"), None), P("seq", "kvh"), P())
    return jax.shard_map(
        body,
        mesh=mesh,
        in_specs=placed,
        out_specs=(P("seq", "kvh"), P("kvh", "seq")),
        check_vma=False,
    )
```

```python
import functools
import math

import jax
import jax.numpy as jnp
from jax import lax
from jax.experimental import pallas as pl
from jax.experimental.pallas import tpu as pltpu
from jax.sharding import PartitionSpec as P

MESH = pl.DeviceIdType.MESH
F32 = jnp.float32
BF16 = jnp.bfloat16
HIGHEST = lax.Precision.HIGHEST

SEQ = 32
KVH = 8
PLANES = 4
RING = 8
HEADS = 8
HEAD = 128
RANK = 64
BLOCK = 128
QUERIES = 512
WIDE = QUERIES - BLOCK
KEYS = 1024
POWER = 2
CHUNK = 128

MASKED = -1e30
LOWEST = -1e29
SCALE = math.log2(math.e) / math.sqrt(HEAD)

LANES = (((1,), (1,)), ((), ()))
PLAIN = (((1,), (0,)), ((), ()))


def dot(left, right, dims=PLAIN, precision=None):
    return lax.dot_general(left, right, dims, precision=precision, preferred_element_type=F32)


def each(count, step, start=0):
    def run(index, carry):
        step(index)
        return carry

    lax.fori_loop(start, count, run, 0)


def inverse_factor(gram):
    lanes = lax.broadcasted_iota(jnp.int32, (RANK, RANK), 1)
    rows = lax.broadcasted_iota(jnp.int32, (RANK, RANK), 0)
    start = jnp.concatenate([gram, jnp.where(lanes == rows, 1.0, 0.0)], axis=1)
    sub = lax.broadcasted_iota(jnp.int32, (8, 2 * RANK), 0)

    def spread(tile, lane):
        return jnp.broadcast_to(tile[:, lane : lane + 1], tile.shape)

    def lift(tile, row):
        return jnp.broadcast_to(tile[row : row + 1, :], tile.shape)

    def block(step, tiles):
        pivot = tiles[0]
        columns = [spread(pivot, j) for j in range(8)]
        inverses, upper, roots = [], [], jnp.zeros_like(pivot)
        for j in range(8):
            diagonal = lift(columns[j], j)
            inverse = 1.0 / diagonal
            inverses.append(inverse)
            roots = jnp.where(sub == j, lax.rsqrt(diagonal), roots)
            factor = jnp.where(sub > j, columns[j] * inverse, 0.0)
            pivot = pivot - factor * lift(pivot, j)
            across = {}
            for other in range(j + 1, 8):
                across[other] = lift(columns[other], j)
                columns[other] = columns[other] - factor * across[other]
            upper.append(across)
        pivot_rows = [lift(pivot, j) for j in range(8)]
        later = []
        for index in range(1, 8):
            tile = tiles[index]
            live = jnp.where(step + index < 8, 1.0, 0.0)
            columns = [spread(tile, j) * live for j in range(8)]
            for j in range(8):
                factor = columns[j] * inverses[j]
                tile = tile - factor * pivot_rows[j]
                for other in range(j + 1, 8):
                    columns[other] = columns[other] - factor * upper[j][other]
            later.append(tile)
        later.append(pivot * roots)
        return tuple(pltpu.roll(tile, 2 * RANK - 8, 1) for tile in later)

    tiles = lax.fori_loop(0, 8, block, tuple(start[8 * i : 8 * i + 8] for i in range(8)))
    return jnp.concatenate(tiles, axis=0)[:, :RANK]


def orthonormal_rows(panel):
    gram = dot(panel, panel, LANES, HIGHEST)
    return dot(inverse_factor(gram), panel, PLAIN, HIGHEST)


def kernel(
    offsets,
    q_ref,
    k_hbm,
    omega_hbm,
    basis_ref,
    proj_hbm,
    q_wide,
    q_tiles,
    q_got,
    q_flat,
    q_turned,
    q_own,
    q_all,
    k_all,
    omega_rows,
    omega_turned,
    scores,
    scores_first,
    probs,
    probs_first,
    stat_out,
    stat_y,
    stat_sum,
    stat_z,
    stat_all,
    wide_out,
    wide_y,
    wide_sum,
    wide_z,
    part_out,
    part_y,
    part_sum,
    part_z,
    basis,
    staged,
    local_sem,
    store_sem,
    qk_send,
    qk_recv,
    kk_send,
    kk_recv,
    qz_send,
    qf_send,
    q_recv,
    sty_send,
    sty_recv,
    stz_send,
    stz_recv,
    sta_send,
    stb_send,
    st_recv,
    wy_send,
    wy_recv,
    wz_send,
    wz_recv,
    py_send,
    py_recv,
    pz_send,
    pz_recv,
    bz_send,
    by_send,
    b_recv,
):
    s = lax.axis_index("seq")
    k = lax.axis_index("kvh")
    y = lax.div(s, RING)
    z = lax.rem(s, RING)
    core = lax.rem(k, 2)

    def owner_z(j):
        return 2 * (2 * j + core)

    own_j = lax.div(z, 4)
    own_head = 2 * y + own_j
    owns = owner_z(own_j) == z

    def at_seq(plane, place):
        return plane * RING + place

    def remote(src, dst, send, recv, **target):
        return pltpu.make_async_remote_copy(
            src_ref=src, dst_ref=dst, send_sem=send, recv_sem=recv,
            device_id=target, device_id_type=MESH,
        )

    def others(count, me, step):
        def run(d):
            @pl.when(d != me)
            def _():
                step(d)

        each(count, run)

    barrier = pltpu.get_barrier_semaphore()

    def greet(**target):
        pl.semaphore_signal(barrier, inc=1, device_id=target, device_id_type=MESH)

    others(KVH, k, lambda d: greet(kvh=d))
    others(RING, z, lambda d: greet(seq=at_seq(y, d)))
    others(PLANES, y, lambda d: greet(seq=at_seq(d, z)))

    omega_copy = pltpu.make_async_copy(omega_hbm, omega_rows, local_sem.at[0])
    omega_copy.start()
    keys_copy = pltpu.make_async_copy(
        k_hbm.at[:, pl.ds(pl.multiple_of(k * HEAD, HEAD), HEAD)], k_all.at[k], local_sem.at[1]
    )
    keys_copy.start()

    q_now = q_ref[...].astype(F32)
    for tile in range(KVH * HEADS):
        q_wide[2 * tile : 2 * tile + 2, :] = q_now[:, tile * HEAD : (tile + 1) * HEAD]
    q_tiles[...] = q_wide[...].astype(BF16).reshape(KVH, 16, HEAD)
    q_got[k] = q_tiles[k]

    basis[...] = jnp.zeros(basis.shape, BF16)
    probs_first[...] = jnp.zeros(probs_first.shape, BF16)
    stat_out[:, 0:1, :] = jnp.full((HEADS, 1, QUERIES), LOWEST, F32)
    stat_out[:, 1:2, :] = jnp.zeros((HEADS, 1, QUERIES), F32)

    @pl.when(y >= 2)
    def _():
        def clear(head):
            probs[head] = jnp.zeros((KEYS, WIDE), BF16)

        each(HEADS, clear)

    pl.semaphore_wait(barrier, KVH - 1 + RING - 1 + PLANES - 1)

    def q_copy(d, slot):
        return remote(q_tiles.at[d], q_got.at[slot], qk_send.at[d], qk_recv.at[slot], kvh=d)

    def k_copy(d, slot):
        columns = pl.ds(pl.multiple_of(d * HEAD, HEAD), HEAD)
        return remote(k_hbm.at[:, columns], k_all.at[slot], kk_send.at[d], kk_recv.at[slot], kvh=d)

    others(KVH, k, lambda d: q_copy(d, k).start())
    others(KVH, k, lambda d: k_copy(d, k).start())
    others(KVH, k, lambda d: q_copy(d, d).wait_recv())

    q_flat[...] = q_got[...].astype(F32).reshape(KVH * 16, HEAD)
    for pair in range(16):
        q_turned[8 * pair : 8 * pair + 8, :] = q_flat[pl.ds(pair, 8, stride=16), :]
    q_own[...] = q_turned[...].astype(BF16).reshape(HEADS, 16, HEAD)
    q_all[:, s] = q_own[...]

    def q_round(d):
        return remote(q_own, q_all.at[:, s], qz_send.at[d], q_recv.at[s], seq=at_seq(y, d))

    def q_pass(piece, way, plane):
        return remote(
            q_all.at[:, piece], q_all.at[:, piece], qf_send.at[way, piece], q_recv.at[piece],
            seq=at_seq(plane, z),
        )

    def q_arrived(piece):
        remote(q_own, q_all.at[:, piece], qz_send.at[0], q_recv.at[piece], seq=piece).wait_recv()

    def q_rounds(step):
        def run(index):
            d = lax.rem(z + index, RING)

            @pl.when((y > 0) | (d == 0))
            def _():
                step(d)

        each(RING, run, 1)

    q_rounds(lambda d: q_round(d).start())

    def pass_block(block, own, step, start):
        def run(index):
            place = lax.rem(z + index, RING)
            piece = at_seq(block, place)
            if start:
                if own:
                    pl.when(index > 0)(lambda: q_arrived(piece))
                else:
                    q_arrived(piece)
            step(piece, lax.rem(place, 2) == 1)

        each(RING, run)

    def pass_all(start):
        def go(piece, way, plane):
            copy = q_pass(piece, way, plane)
            if start:
                copy.start()
            else:
                copy.wait_send()

        @pl.when(y == 3)
        def _():
            def both(piece, odd):
                go(piece, 0, 0)
                go(piece, 1, 2)

            pass_block(3, True, both, start)

            def other(index):
                piece = at_seq(2, 2 * index + 1)
                if start:
                    q_arrived(piece)
                go(piece, 0, 0)

            each(RING // 2, other)

        @pl.when(y == 2)
        def _():
            def both(piece, odd):
                pl.when(odd)(lambda: go(piece, 1, 3))
                go(piece, 0, 1)

            pass_block(2, True, both, start)

        @pl.when(y == 1)
        def _():
            pass_block(1, True, lambda piece, odd: go(piece, 0, 0), start)
            pass_block(
                2, False, lambda piece, odd: pl.when(~odd)(lambda: go(piece, 0, 0)), start
            )

        @pl.when(y == 0)
        def _():
            pass_block(3, False, lambda piece, odd: go(piece, 0, 1), start)

    omega_copy.wait()
    for tile in range(4):
        turned = omega_rows[:, tile * 128 : (tile + 1) * 128].astype(F32).T.astype(BF16)
        omega_turned[2 * tile] = turned[:RANK]
        omega_turned[2 * tile + 1] = turned[RANK:]

    pass_all(True)
    keys_copy.wait()
    others(KVH, k, lambda d: k_copy(d, d).wait_recv())

    lane = lax.broadcasted_iota(jnp.int32, (1, BLOCK), 1)
    place = lax.rem(lane, 16)
    row_in_block = lane - place + 2 * lax.rem(place, 8) + lax.div(place, 8)
    key_row = lax.broadcasted_iota(jnp.int32, (CHUNK, 1), 0)

    def block_of(row, block):
        return row[:, block * BLOCK : (block + 1) * BLOCK]

    def limits(block):
        return offsets[block] * BLOCK + row_in_block - s * KEYS

    def fold(tile, join):
        return join(tile.reshape(CHUNK // 8, 8, tile.shape[1]), axis=0)

    def head_at(index):
        turn = lax.rem(index, 4)
        turn = jnp.where(turn < 2, turn, 5 - turn)
        plane = lax.rem(y + turn, PLANES)
        j = lax.div(index, 4)
        return plane, j, 2 * plane + j

    def spans(plane, act, everything=False):
        if isinstance(plane, int):
            if plane:
                act(plane)
            elif everything:
                act(0)
            else:
                pl.when(z == 0)(lambda: act(0))
                pl.when(z != 0)(lambda: act(1))
        else:
            if everything:
                pl.when(plane == 0)(lambda: act(0))
                pl.when(plane == 1)(lambda: act(1))
            else:
                pl.when((plane == 0) & (z == 0))(lambda: act(0))
                pl.when((plane == 1) | ((plane == 0) & (z != 0)))(lambda: act(1))
            pl.when(plane == 2)(lambda: act(2))
            pl.when(plane == 3)(lambda: act(3))

    def cut(ref, *place, first):
        return ref.at[(*place, pl.ds(first, PLANES - first))]

    def y_send(out, landing, send, recv, head, plane, j, start):
        @pl.when(plane != y)
        def _():
            def act(first):
                copy = remote(
                    cut(out, head, first=first), cut(landing, y, j, first=first),
                    send.at[head], recv.at[y, j], seq=at_seq(plane, z),
                )
                if start:
                    copy.start()
                else:
                    copy.wait_send()

            spans(y, act)

    def y_wait(out, landing, send, recv, j):
        for plane in range(PLANES):
            @pl.when(plane != y)
            def _():
                def act(first):
                    remote(
                        cut(out, 0, first=first), cut(landing, plane, j, first=first),
                        send.at[0], recv.at[plane, j], seq=at_seq(plane, z),
                    ).wait_recv()

                spans(plane, act)

    def z_send(through, landing, send, recv, j, start):
        target = owner_z(j)

        @pl.when(target != z)
        def _():
            def act(first):
                copy = remote(
                    cut(through, j, first=first), cut(landing, z, first=first),
                    send.at[j], recv.at[z], seq=at_seq(y, target),
                )
                if start:
                    copy.start()
                else:
                    copy.wait_send()

            spans(0, act)

    def z_wait(through, landing, send, recv):
        def run(d):
            for first in (0, 1):
                @pl.when((d == 0) if first == 0 else (d != 0))
                def _():
                    remote(
                        cut(through, 0, first=first), cut(landing, d, first=first),
                        send.at[0], recv.at[d], seq=at_seq(y, d),
                    ).wait_recv()

        others(RING, z, run)

    def stat_y_copy(head, plane, j, source):
        return remote(
            stat_out.at[head], stat_y.at[source, j], sty_send.at[head], sty_recv.at[source, j],
            seq=at_seq(plane, z),
        )

    def first_block(block, columns, heads):
        rows = pl.ds(pl.multiple_of(8 * block, 8), 8)
        q_heads = jnp.concatenate([q_all[h, rows].reshape(BLOCK, HEAD) for h in heads], axis=0)
        limit = limits(block)
        limit = jnp.concatenate([limit, limit], axis=1)
        largest = jnp.full((8, 2 * BLOCK), LOWEST, F32)
        for chunk in range(KEYS // CHUNK):
            at = slice(chunk * CHUNK, (chunk + 1) * CHUNK)
            piece = dot(k_all[chunk], q_heads, LANES)
            piece = jnp.where(key_row + chunk * CHUNK <= limit, piece, MASKED)
            for n, head in enumerate(heads):
                scores[head, at, columns] = block_of(piece, n)
            largest = jnp.maximum(largest, fold(piece, jnp.max))
        top = jnp.max(largest, axis=0, keepdims=True)
        totals = [jnp.zeros((8, BLOCK), F32) for _ in heads]
        for chunk in range(KEYS // CHUNK):
            at = slice(chunk * CHUNK, (chunk + 1) * CHUNK)
            for n, head in enumerate(heads):
                weight = jnp.exp2((scores[head, at, columns] - block_of(top, n)) * SCALE)
                totals[n] = totals[n] + fold(weight, jnp.sum)
                probs[head, at, columns] = weight.astype(BF16)
        place = pl.ds(pl.multiple_of(block * BLOCK, BLOCK), BLOCK)
        for n, head in enumerate(heads):
            stat_out[head, 0:1, place] = block_of(top, n)
            stat_out[head, 1:2, place] = jnp.sum(totals[n], axis=0, keepdims=True)
            wide_out[head, block] = dot(omega_turned[head], probs[head, :, columns])

    def block_zero(head):
        q_head = q_all[head, 0:8].reshape(BLOCK, HEAD)
        piece = jnp.where(key_row <= limits(0), dot(k_all[0], q_head, LANES), MASKED)
        scores_first[head] = piece
        top = jnp.max(piece, axis=0, keepdims=True)
        weight = jnp.exp2((piece - top) * SCALE)
        probs_first[head] = weight.astype(BF16)
        stat_out[head, 0:1, :BLOCK] = top
        stat_out[head, 1:2, :BLOCK] = jnp.sum(weight, axis=0, keepdims=True)
        wide_out[head, 0] = dot(omega_turned[head, :, :BLOCK], probs_first[head])

    @pl.when(s == 0)
    def _():
        others(RING, z, q_arrived)
        each(HEADS, block_zero)

    steps = jnp.where(y == 0, 3, PLANES - y)

    def one_block(step):
        block = jnp.where(y == 0, jnp.where(step == 0, 3, step), y + step)
        columns = pl.ds(pl.multiple_of((block - 1) * BLOCK, BLOCK), BLOCK)

        @pl.when(jnp.where(y == 0, block != 3, (block == 3) & (y < 3)))
        def _():
            each(RING, lambda d: q_arrived(at_seq(block, d)))

        def run(pair):
            two = [head_at(2 * pair), head_at(2 * pair + 1)]
            first_block(block, columns, [head for _, _, head in two])

            @pl.when(step == steps - 1)
            def _():
                for plane, j, head in two:
                    send_first(plane, j, head)

        def send_first(plane, j, head):
            @pl.when(plane != y)
            def _():
                stat_y_copy(head, plane, j, y).start()

            y_send(wide_out, wide_y, wy_send, wy_recv, head, plane, j, True)

            @pl.when(plane == y)
            def _():
                wide_y[y, j] = wide_out[head]
                stat_y[y, j] = stat_out[head]

        each(HEADS // 2, run)

    each(steps, one_block)

    def merge_scale(value, top):
        return jnp.exp2((value - top) * SCALE)

    def join_wide(j):
        for plane in range(PLANES):
            @pl.when(plane != y)
            def _():
                stat_y_copy(0, plane, j, plane).wait_recv()

        tops = [stat_y[p, j, 0:1, :] for p in range(PLANES)]
        top = functools.reduce(jnp.maximum, tops)
        scales = [merge_scale(value, top) for value in tops]
        stat_sum[j, 0:1, :] = top
        stat_sum[j, 1:2, :] = sum(stat_y[p, j, 1:2, :] * scales[p] for p in range(PLANES))

        @pl.when(owner_z(j) == z)
        def _():
            stat_z[z] = stat_sum[j]

        @pl.when(owner_z(j) != z)
        def _():
            stat_z_copy(j, z).start()

        y_wait(wide_out, wide_y, wy_send, wy_recv, j)
        for block in range(1, PLANES):
            wide_sum[j, block] = sum(
                wide_y[p, j, block] * block_of(scales[p], block) for p in range(block + 1)
            )

        @pl.when(z == 0)
        def _():
            wide_sum[j, 0] = wide_y[0, j, 0] * block_of(scales[0], 0)

        @pl.when(owner_z(j) == z)
        def _():
            wide_z[z] = wide_sum[j]

        z_send(wide_sum, wide_z, wz_send, wz_recv, j, True)

    def stat_z_copy(j, source):
        return remote(
            stat_sum.at[j], stat_z.at[source], stz_send.at[j], stz_recv.at[source],
            seq=at_seq(y, owner_z(j)),
        )

    def stat_share(d):
        return remote(
            stat_all.at[own_head], stat_all.at[own_head], sta_send.at[d], st_recv.at[own_head],
            seq=at_seq(y, d),
        )

    def around(d, everything, act):
        whole = (d == 0) | everything
        pl.when(whole)(lambda: act(0))
        pl.when(~whole)(lambda: act(1))

    def share_basis(everything, start):
        def run(d):
            def act(first):
                copy = remote(
                    cut(basis, own_head, first=first), cut(basis, own_head, first=first),
                    bz_send.at[d], b_recv.at[own_head], seq=at_seq(y, d),
                )
                if start:
                    copy.start()
                else:
                    copy.wait_send()

            around(d, everything, act)

        others(RING, z, run)

    def store_basis(rows):
        for block in range(PLANES):
            basis[own_head, block] = block_of(rows, block).astype(BF16)

    def own_wide():
        others(RING, z, lambda d: stat_z_copy(0, d).wait_recv())
        top = functools.reduce(jnp.maximum, [stat_z[d, 0:1, :] for d in range(RING)])
        scales = [merge_scale(stat_z[d, 0:1, :], top) for d in range(RING)]
        inverse = 1.0 / sum(stat_z[d, 1:2, :] * scales[d] for d in range(RING))
        stat_all[own_head, 0:1, :] = top
        stat_all[own_head, 1:2, :] = inverse
        others(RING, z, lambda d: stat_share(d).start())
        z_wait(wide_sum, wide_z, wz_send, wz_recv)
        pieces = [wide_z[0, 0] * block_of(scales[0], 0)]
        for block in range(1, PLANES):
            pieces.append(sum(wide_z[d, block] * block_of(scales[d], block) for d in range(RING)))
        store_basis(orthonormal_rows(jnp.concatenate(pieces, axis=1) * inverse))
        share_basis(False, True)

    def finish_wide(j):
        join_wide(j)
        pl.when(owns & (own_j == j))(own_wide)

    each(2, finish_wide)

    def stat_pass(j, plane):
        head = 2 * y + j
        return remote(
            stat_all.at[head], stat_all.at[head], stb_send.at[j, plane], st_recv.at[head],
            seq=at_seq(plane, z),
        )

    def stat_wait(head):
        remote(stat_all.at[head], stat_all.at[head], sta_send.at[0], st_recv.at[head], seq=s).wait_recv()

    def relay_stats(j):
        @pl.when(owner_z(j) != z)
        def _():
            stat_wait(2 * y + j)

        others(PLANES, y, lambda plane: stat_pass(j, plane).start())

    def relay_basis(j, last, start):
        head = 2 * y + j
        if start:
            @pl.when(owner_z(j) != z)
            def _():
                def arrived(first):
                    remote(
                        cut(basis, head, first=first), cut(basis, head, first=first),
                        bz_send.at[0], b_recv.at[head], seq=s,
                    ).wait_recv()

                around(z, last, arrived)

        for plane in range(PLANES):
            @pl.when(plane != y)
            def _():
                def act(first):
                    copy = remote(
                        cut(basis, head, first=first), cut(basis, head, first=first),
                        by_send.at[j, plane], b_recv.at[head], seq=at_seq(plane, z),
                    )
                    if start:
                        copy.start()
                    else:
                        copy.wait_send()

                spans(plane, act, last)

    def wait_basis(plane, head, last):
        @pl.when(plane != y)
        def _():
            def act(first):
                remote(
                    cut(basis, head, first=first), cut(basis, head, first=first),
                    by_send.at[0, 0], b_recv.at[head], seq=at_seq(plane, z),
                ).wait_recv()

            spans(y, act, last)

    relay_stats(0)
    relay_stats(1)

    def normalise(index):
        plane, j, head = head_at(index)

        @pl.when(plane != y)
        def _():
            stat_wait(head)

        def run(block):
            columns = pl.ds(pl.multiple_of((block - 1) * BLOCK, BLOCK), BLOCK)
            place = pl.ds(pl.multiple_of(block * BLOCK, BLOCK), BLOCK)
            top = stat_all[head, 0:1, place]
            inverse = stat_all[head, 1:2, place]
            for chunk in range(KEYS // CHUNK):
                at = slice(chunk * CHUNK, (chunk + 1) * CHUNK)
                weight = merge_scale(scores[head, at, columns], top)
                probs[head, at, columns] = (weight * inverse).astype(BF16)

        each(PLANES, run, jnp.maximum(y, 1))

        @pl.when(s == 0)
        def _():
            weight = merge_scale(scores_first[head], stat_all[head, 0:1, :BLOCK])
            probs_first[head] = (weight * stat_all[head, 1:2, :BLOCK]).astype(BF16)

    @pl.when(owns)
    def _():
        relay_basis(own_j, False, True)

    each(HEADS, normalise)

    def forward(head, plane, j, panel):
        product = dot(panel, probs[head]).astype(BF16)
        for b in range(3):
            part_out[head, b + 1] = product[:, b * BLOCK : (b + 1) * BLOCK]

        @pl.when(s == 0)
        def _():
            part_out[head, 0] = dot(panel[:, :BLOCK], probs_first[head]).astype(BF16)

        @pl.when(plane == y)
        def _():
            part_y[y, j] = part_out[head]

    def backward(head):
        low = jnp.concatenate([basis[head, 1], basis[head, 2], basis[head, 3]], axis=1)
        product = dot(low, probs[head], LANES)
        first = dot(basis[head, 0], probs_first[head], LANES)
        return jnp.concatenate([product[:, :BLOCK] + first, product[:, BLOCK:]], axis=1)

    def join_parts(j):
        y_wait(part_out, part_y, py_send, py_recv, j)
        relay_basis(j, False, False)
        for block in range(1, PLANES):
            part_sum[j, block] = sum(
                part_y[p, j, block].astype(F32) for p in range(block + 1)
            ).astype(BF16)

        @pl.when(z == 0)
        def _():
            part_sum[j, 0] = part_y[0, j, 0]

        @pl.when(owner_z(j) == z)
        def _():
            part_z[z] = part_sum[j]

        z_send(part_sum, part_z, pz_send, pz_recv, j, True)

    def own_parts(step):
        z_wait(part_sum, part_z, pz_send, pz_recv)
        pieces = [part_z[0, 0].astype(F32)]
        for block in range(1, PLANES):
            pieces.append(sum(part_z[d, block].astype(F32) for d in range(RING)))
        rows = orthonormal_rows(jnp.concatenate(pieces, axis=1))
        share_basis(False, False)
        store_basis(rows)
        share_basis(step == POWER - 1, True)

    def power_step(step):
        def group(j):
            @pl.when(~((step == 0) & (owner_z(j) == z)))
            def _():
                relay_basis(j, False, True)

            def one_head(turn):
                plane, _, head = head_at(4 * j + turn)
                wait_basis(plane, head, False)
                forward(head, plane, j, backward(head).astype(BF16))
                y_send(part_out, part_y, py_send, py_recv, head, plane, j, True)

            each(PLANES, one_head)

        def finish(j):
            join_parts(j)
            pl.when(owns & (own_j == j))(lambda: own_parts(step))

        each(2, group)
        each(2, finish)

        def sent(index):
            plane, j, head = head_at(index)
            y_send(part_out, part_y, py_send, py_recv, head, plane, j, False)

        each(HEADS, sent)
        z_send(part_sum, part_z, pz_send, pz_recv, 0, False)
        z_send(part_sum, part_z, pz_send, pz_recv, 1, False)

    each(POWER, power_step)

    def store_copy(head):
        rows = pl.ds(pl.multiple_of(head * RANK, RANK), RANK)
        return pltpu.make_async_copy(staged.at[rows], proj_hbm.at[rows], store_sem.at[head])

    def last_group(j):
        relay_basis(j, True, True)

        def last_head(turn):
            plane, _, head = head_at(4 * j + turn)
            wait_basis(plane, head, True)
            rows = pl.ds(pl.multiple_of(head * RANK, RANK), RANK)
            staged[rows, :] = backward(head)
            store_copy(head).start()

        each(PLANES, last_head)

    each(2, last_group)

    row = lax.broadcasted_iota(jnp.int32, (16, QUERIES), 0)
    lane = lax.broadcasted_iota(jnp.int32, (16, QUERIES), 1)
    chosen = lane == s * 16 + 8 * lax.rem(row, 2) + lax.div(row, 2)
    chosen = jnp.where(chosen, 1.0, 0.0).astype(BF16)
    total = jnp.zeros((16, HEADS * RANK), F32)
    for block in range(PLANES):
        total = total + dot(
            chosen[:, block * BLOCK : (block + 1) * BLOCK],
            basis[:, block].reshape(HEADS * RANK, BLOCK),
            LANES,
        )
    basis_ref[...] = total

    each(HEADS, lambda head: store_copy(head).wait())
    others(KVH, k, lambda d: q_copy(d, k).wait_send())
    others(KVH, k, lambda d: k_copy(d, k).wait_send())
    q_rounds(lambda d: q_round(d).wait_send())
    pass_all(False)

    def sent_wide(index):
        plane, j, head = head_at(index)

        @pl.when(plane != y)
        def _():
            stat_y_copy(head, plane, j, y).wait_send()

        y_send(wide_out, wide_y, wy_send, wy_recv, head, plane, j, False)

    each(HEADS, sent_wide)
    for j in range(2):
        z_send(wide_sum, wide_z, wz_send, wz_recv, j, False)

        @pl.when(owner_z(j) != z)
        def _():
            stat_z_copy(j, z).wait_send()

        others(PLANES, y, lambda plane: stat_pass(j, plane).wait_send())
        relay_basis(j, True, False)

    @pl.when(owns)
    def _():
        others(RING, z, lambda d: stat_share(d).wait_send())
        share_basis(True, False)


def body(queries, keys, omega, block_offsets):
    vmem = lambda shape, kind: pltpu.VMEM(shape, kind)
    dma = lambda *shape: pltpu.SemaphoreType.DMA(shape)
    panel = (PLANES, RANK, BLOCK)
    basis, projection = pl.pallas_call(
        kernel,
        out_shape=(
            jax.ShapeDtypeStruct((16, HEADS * RANK), F32),
            jax.ShapeDtypeStruct((HEADS * RANK, KEYS), F32),
        ),
        in_specs=[
            pl.BlockSpec(memory_space=pltpu.SMEM),
            pl.BlockSpec(memory_space=pltpu.VMEM),
            pl.BlockSpec(memory_space=pl.ANY),
            pl.BlockSpec(memory_space=pl.ANY),
        ],
        out_specs=(
            pl.BlockSpec(memory_space=pltpu.VMEM),
            pl.BlockSpec(memory_space=pl.ANY),
        ),
        scratch_shapes=[
            vmem((128, HEAD), F32),
            vmem((KVH, 16, HEAD), BF16),
            vmem((KVH, 16, HEAD), BF16),
            vmem((128, HEAD), F32),
            vmem((128, HEAD), F32),
            vmem((HEADS, 16, HEAD), BF16),
            vmem((HEADS, SEQ, 16, HEAD), BF16),
            vmem((KVH, 128, HEAD), BF16),
            vmem((KEYS, HEADS * RANK), BF16),
            vmem((HEADS, RANK, KEYS), BF16),
            vmem((HEADS, KEYS, WIDE), F32),
            vmem((HEADS, BLOCK, BLOCK), F32),
            vmem((HEADS, KEYS, WIDE), BF16),
            vmem((HEADS, BLOCK, BLOCK), BF16),
            vmem((HEADS, 2, QUERIES), F32),
            vmem((PLANES, 2, 2, QUERIES), F32),
            vmem((2, 2, QUERIES), F32),
            vmem((RING, 2, QUERIES), F32),
            vmem((HEADS, 2, QUERIES), F32),
            vmem((HEADS, *panel), F32),
            vmem((PLANES, 2, *panel), F32),
            vmem((2, *panel), F32),
            vmem((RING, *panel), F32),
            vmem((HEADS, *panel), BF16),
            vmem((PLANES, 2, *panel), BF16),
            vmem((2, *panel), BF16),
            vmem((RING, *panel), BF16),
            vmem((HEADS, *panel), BF16),
            vmem((HEADS * RANK, KEYS), F32),
            dma(2),
            dma(HEADS),
            dma(KVH), dma(KVH),
            dma(KVH), dma(KVH),
            dma(RING), dma(2, SEQ), dma(SEQ),
            dma(HEADS), dma(PLANES, 2),
            dma(2), dma(RING),
            dma(RING), dma(2, PLANES), dma(HEADS),
            dma(HEADS), dma(PLANES, 2),
            dma(2), dma(RING),
            dma(HEADS), dma(PLANES, 2),
            dma(2), dma(RING),
            dma(RING), dma(2, PLANES), dma(HEADS),
        ],
        compiler_params=pltpu.CompilerParams(
            collective_id=0, has_side_effects=True, vmem_limit_bytes=56 * 2**20
        ),
        cost_estimate=pl.CostEstimate(
            flops=6 * 10**9, bytes_accessed=8 * 2**20, transcendentals=8 * 10**6
        ),
        name="range_finder",
    )(block_offsets, queries, keys, omega)
    return basis * math.sqrt(QUERIES), projection * math.sqrt(SEQ * KEYS)


def solution(mesh):
    placed = (P(("seq", "kvh"), None), P(("seq", "kvh"), None), P("seq", "kvh"), P())
    return jax.shard_map(
        body,
        mesh=mesh,
        in_specs=placed,
        out_specs=(P("seq", "kvh"), P("kvh", "seq")),
        check_vma=False,
    )
```

```python
import functools
import math

import jax
import jax.numpy as jnp
from jax import lax
from jax.experimental import pallas as pl
from jax.experimental.pallas import tpu as pltpu
from jax.sharding import PartitionSpec as P

MESH = pl.DeviceIdType.MESH
F32 = jnp.float32
BF16 = jnp.bfloat16
HIGHEST = lax.Precision.HIGHEST

SEQ = 32
KVH = 8
PLANES = 4
RING = 8
HEADS = 8
HEAD = 128
RANK = 64
BLOCK = 128
QUERIES = 512
WIDE = QUERIES - BLOCK
KEYS = 1024
POWER = 2
CHUNK = 128

MASKED = -1e30
LOWEST = -1e29
SCALE = math.log2(math.e) / math.sqrt(HEAD)

LANES = (((1,), (1,)), ((), ()))
PLAIN = (((1,), (0,)), ((), ()))


def dot(left, right, dims=PLAIN, precision=None):
    return lax.dot_general(left, right, dims, precision=precision, preferred_element_type=F32)


def each(count, step, start=0):
    def run(index, carry):
        step(index)
        return carry

    lax.fori_loop(start, count, run, 0)


def inverse_factor(gram):
    lanes = lax.broadcasted_iota(jnp.int32, (RANK, RANK), 1)
    rows = lax.broadcasted_iota(jnp.int32, (RANK, RANK), 0)
    start = jnp.concatenate([gram, jnp.where(lanes == rows, 1.0, 0.0)], axis=1)
    sub = lax.broadcasted_iota(jnp.int32, (8, 2 * RANK), 0)

    def spread(tile, lane):
        return jnp.broadcast_to(tile[:, lane : lane + 1], tile.shape)

    def lift(tile, row):
        return jnp.broadcast_to(tile[row : row + 1, :], tile.shape)

    tiles = [start[8 * i : 8 * i + 8] for i in range(8)]
    for step in range(8):
        pivot = tiles[step]
        columns = [spread(pivot, 8 * step + j) for j in range(8)]
        inverses, upper, roots = [], [], jnp.zeros_like(pivot)
        for j in range(8):
            diagonal = lift(columns[j], j)
            inverse = 1.0 / diagonal
            inverses.append(inverse)
            roots = jnp.where(sub == j, lax.rsqrt(diagonal), roots)
            factor = jnp.where(sub > j, columns[j] * inverse, 0.0)
            pivot = pivot - factor * lift(pivot, j)
            across = {}
            for other in range(j + 1, 8):
                across[other] = lift(columns[other], j)
                columns[other] = columns[other] - factor * across[other]
            upper.append(across)
        pivot_rows = [lift(pivot, j) for j in range(8)]
        for index in range(step + 1, 8):
            tile = tiles[index]
            columns = [spread(tile, 8 * step + j) for j in range(8)]
            for j in range(8):
                factor = columns[j] * inverses[j]
                tile = tile - factor * pivot_rows[j]
                for other in range(j + 1, 8):
                    columns[other] = columns[other] - factor * upper[j][other]
            tiles[index] = tile
        tiles[step] = pivot * roots
    return jnp.concatenate(tiles, axis=0)[:, RANK:]


def orthonormal_rows(panel):
    gram = dot(panel, panel, LANES, HIGHEST)
    return dot(inverse_factor(gram), panel, PLAIN, HIGHEST)


def kernel(
    offsets,
    q_ref,
    k_hbm,
    omega_hbm,
    basis_ref,
    proj_hbm,
    q_wide,
    q_tiles,
    q_got,
    q_flat,
    q_turned,
    q_own,
    q_all,
    k_all,
    omega_rows,
    omega_turned,
    scores,
    scores_first,
    probs,
    probs_first,
    stat_out,
    stat_y,
    stat_sum,
    stat_z,
    stat_all,
    wide_out,
    wide_y,
    wide_sum,
    wide_z,
    part_out,
    part_y,
    part_sum,
    part_z,
    basis,
    staged,
    local_sem,
    store_sem,
    qk_send,
    qk_recv,
    kk_send,
    kk_recv,
    qz_send,
    qf_send,
    q_recv,
    sty_send,
    sty_recv,
    stz_send,
    stz_recv,
    sta_send,
    stb_send,
    st_recv,
    wy_send,
    wy_recv,
    wz_send,
    wz_recv,
    py_send,
    py_recv,
    pz_send,
    pz_recv,
    bz_send,
    by_send,
    b_recv,
):
    s = lax.axis_index("seq")
    k = lax.axis_index("kvh")
    y = lax.div(s, RING)
    z = lax.rem(s, RING)
    core = lax.rem(k, 2)

    def owner_z(j):
        return 2 * (2 * j + core)

    own_j = lax.div(z, 4)
    own_head = 2 * y + own_j
    owns = owner_z(own_j) == z

    def at_seq(plane, place):
        return plane * RING + place

    def remote(src, dst, send, recv, **target):
        return pltpu.make_async_remote_copy(
            src_ref=src, dst_ref=dst, send_sem=send, recv_sem=recv,
            device_id=target, device_id_type=MESH,
        )

    def others(count, me, step):
        def run(d):
            @pl.when(d != me)
            def _():
                step(d)

        each(count, run)

    barrier = pltpu.get_barrier_semaphore()

    def greet(**target):
        pl.semaphore_signal(barrier, inc=1, device_id=target, device_id_type=MESH)

    others(KVH, k, lambda d: greet(kvh=d))
    others(RING, z, lambda d: greet(seq=at_seq(y, d)))
    others(PLANES, y, lambda d: greet(seq=at_seq(d, z)))

    omega_copy = pltpu.make_async_copy(omega_hbm, omega_rows, local_sem.at[0])
    omega_copy.start()
    keys_copy = pltpu.make_async_copy(
        k_hbm.at[:, pl.ds(pl.multiple_of(k * HEAD, HEAD), HEAD)], k_all.at[k], local_sem.at[1]
    )
    keys_copy.start()

    q_now = q_ref[...].astype(F32)
    for tile in range(KVH * HEADS):
        q_wide[2 * tile : 2 * tile + 2, :] = q_now[:, tile * HEAD : (tile + 1) * HEAD]
    q_tiles[...] = q_wide[...].astype(BF16).reshape(KVH, 16, HEAD)
    q_got[k] = q_tiles[k]

    basis[...] = jnp.zeros(basis.shape, BF16)
    probs_first[...] = jnp.zeros(probs_first.shape, BF16)
    stat_out[:, 0:1, :] = jnp.full((HEADS, 1, QUERIES), LOWEST, F32)
    stat_out[:, 1:2, :] = jnp.zeros((HEADS, 1, QUERIES), F32)

    @pl.when(y >= 2)
    def _():
        def clear(head):
            probs[head] = jnp.zeros((KEYS, WIDE), BF16)

        each(HEADS, clear)

    pl.semaphore_wait(barrier, KVH - 1 + RING - 1 + PLANES - 1)

    def q_copy(d, slot):
        return remote(q_tiles.at[d], q_got.at[slot], qk_send.at[d], qk_recv.at[slot], kvh=d)

    def k_copy(d, slot):
        columns = pl.ds(pl.multiple_of(d * HEAD, HEAD), HEAD)
        return remote(k_hbm.at[:, columns], k_all.at[slot], kk_send.at[d], kk_recv.at[slot], kvh=d)

    others(KVH, k, lambda d: q_copy(d, k).start())
    others(KVH, k, lambda d: k_copy(d, k).start())
    others(KVH, k, lambda d: q_copy(d, d).wait_recv())

    q_flat[...] = q_got[...].astype(F32).reshape(KVH * 16, HEAD)
    for pair in range(16):
        q_turned[8 * pair : 8 * pair + 8, :] = q_flat[pl.ds(pair, 8, stride=16), :]
    q_own[...] = q_turned[...].astype(BF16).reshape(HEADS, 16, HEAD)
    q_all[:, s] = q_own[...]

    def q_round(d):
        return remote(q_own, q_all.at[:, s], qz_send.at[d], q_recv.at[s], seq=at_seq(y, d))

    def q_pass(piece, way, plane):
        return remote(
            q_all.at[:, piece], q_all.at[:, piece], qf_send.at[way, piece], q_recv.at[piece],
            seq=at_seq(plane, z),
        )

    def q_arrived(piece):
        remote(q_own, q_all.at[:, piece], qz_send.at[0], q_recv.at[piece], seq=piece).wait_recv()

    def q_rounds(step):
        def run(index):
            d = lax.rem(z + index, RING)

            @pl.when((y > 0) | (d == 0))
            def _():
                step(d)

        each(RING, run, 1)

    q_rounds(lambda d: q_round(d).start())

    def pass_block(block, own, step, start):
        def run(index):
            place = lax.rem(z + index, RING)
            piece = at_seq(block, place)
            if start:
                if own:
                    pl.when(index > 0)(lambda: q_arrived(piece))
                else:
                    q_arrived(piece)
            step(piece, lax.rem(place, 2) == 1)

        each(RING, run)

    def pass_all(start):
        def go(piece, way, plane):
            copy = q_pass(piece, way, plane)
            if start:
                copy.start()
            else:
                copy.wait_send()

        @pl.when(y == 3)
        def _():
            def both(piece, odd):
                go(piece, 0, 0)
                go(piece, 1, 2)

            pass_block(3, True, both, start)

            def other(index):
                piece = at_seq(2, 2 * index + 1)
                if start:
                    q_arrived(piece)
                go(piece, 0, 0)

            each(RING // 2, other)

        @pl.when(y == 2)
        def _():
            def both(piece, odd):
                pl.when(odd)(lambda: go(piece, 1, 3))
                go(piece, 0, 1)

            pass_block(2, True, both, start)

        @pl.when(y == 1)
        def _():
            pass_block(1, True, lambda piece, odd: go(piece, 0, 0), start)
            pass_block(
                2, False, lambda piece, odd: pl.when(~odd)(lambda: go(piece, 0, 0)), start
            )

        @pl.when(y == 0)
        def _():
            pass_block(3, False, lambda piece, odd: go(piece, 0, 1), start)

    omega_copy.wait()
    for tile in range(4):
        turned = omega_rows[:, tile * 128 : (tile + 1) * 128].astype(F32).T.astype(BF16)
        omega_turned[2 * tile] = turned[:RANK]
        omega_turned[2 * tile + 1] = turned[RANK:]

    pass_all(True)
    keys_copy.wait()
    others(KVH, k, lambda d: k_copy(d, d).wait_recv())

    lane = lax.broadcasted_iota(jnp.int32, (1, BLOCK), 1)
    place = lax.rem(lane, 16)
    row_in_block = lane - place + 2 * lax.rem(place, 8) + lax.div(place, 8)
    key_row = lax.broadcasted_iota(jnp.int32, (CHUNK, 1), 0)

    def block_of(row, block):
        return row[:, block * BLOCK : (block + 1) * BLOCK]

    def limits(block):
        return offsets[block] * BLOCK + row_in_block - s * KEYS

    def fold(tile, join):
        return join(tile.reshape(CHUNK // 8, 8, tile.shape[1]), axis=0)

    def head_at(index):
        plane = lax.rem(y + lax.div(index, 2), PLANES)
        j = lax.rem(index, 2)
        return plane, j, 2 * plane + j

    def spans(plane, act, everything=False):
        if isinstance(plane, int):
            if plane:
                act(plane)
            elif everything:
                act(0)
            else:
                pl.when(z == 0)(lambda: act(0))
                pl.when(z != 0)(lambda: act(1))
        else:
            if everything:
                pl.when(plane == 0)(lambda: act(0))
                pl.when(plane == 1)(lambda: act(1))
            else:
                pl.when((plane == 0) & (z == 0))(lambda: act(0))
                pl.when((plane == 1) | ((plane == 0) & (z != 0)))(lambda: act(1))
            pl.when(plane == 2)(lambda: act(2))
            pl.when(plane == 3)(lambda: act(3))

    def cut(ref, *place, first):
        return ref.at[(*place, pl.ds(first, PLANES - first))]

    def y_send(out, landing, send, recv, head, plane, j, start):
        @pl.when(plane != y)
        def _():
            def act(first):
                copy = remote(
                    cut(out, head, first=first), cut(landing, y, j, first=first),
                    send.at[head], recv.at[y, j], seq=at_seq(plane, z),
                )
                if start:
                    copy.start()
                else:
                    copy.wait_send()

            spans(y, act)

    def y_wait(out, landing, send, recv, j):
        for plane in range(PLANES):
            @pl.when(plane != y)
            def _():
                def act(first):
                    remote(
                        cut(out, 0, first=first), cut(landing, plane, j, first=first),
                        send.at[0], recv.at[plane, j], seq=at_seq(plane, z),
                    ).wait_recv()

                spans(plane, act)

    def z_send(through, landing, send, recv, j, start):
        target = owner_z(j)

        @pl.when(target != z)
        def _():
            def act(first):
                copy = remote(
                    cut(through, j, first=first), cut(landing, z, first=first),
                    send.at[j], recv.at[z], seq=at_seq(y, target),
                )
                if start:
                    copy.start()
                else:
                    copy.wait_send()

            spans(0, act)

    def z_wait(through, landing, send, recv):
        def run(d):
            for first in (0, 1):
                @pl.when((d == 0) if first == 0 else (d != 0))
                def _():
                    remote(
                        cut(through, 0, first=first), cut(landing, d, first=first),
                        send.at[0], recv.at[d], seq=at_seq(y, d),
                    ).wait_recv()

        others(RING, z, run)

    def stat_y_copy(head, plane, j, source):
        return remote(
            stat_out.at[head], stat_y.at[source, j], sty_send.at[head], sty_recv.at[source, j],
            seq=at_seq(plane, z),
        )

    def first_block(block, columns, heads):
        rows = pl.ds(pl.multiple_of(8 * block, 8), 8)
        q_heads = jnp.concatenate([q_all[h, rows].reshape(BLOCK, HEAD) for h in heads], axis=0)
        limit = limits(block)
        limit = jnp.concatenate([limit] * len(heads), axis=1)
        largest = jnp.full((8, len(heads) * BLOCK), LOWEST, F32)
        for chunk in range(KEYS // CHUNK):
            at = slice(chunk * CHUNK, (chunk + 1) * CHUNK)
            piece = dot(k_all[chunk], q_heads, LANES)
            piece = jnp.where(key_row + chunk * CHUNK <= limit, piece, MASKED)
            for n, head in enumerate(heads):
                scores[head, at, columns] = block_of(piece, n)
            largest = jnp.maximum(largest, fold(piece, jnp.max))
        top = jnp.max(largest, axis=0, keepdims=True)
        totals = [jnp.zeros((8, BLOCK), F32) for _ in heads]
        for chunk in range(KEYS // CHUNK):
            at = slice(chunk * CHUNK, (chunk + 1) * CHUNK)
            for n, head in enumerate(heads):
                weight = jnp.exp2((scores[head, at, columns] - block_of(top, n)) * SCALE)
                totals[n] = totals[n] + fold(weight, jnp.sum)
                probs[head, at, columns] = weight.astype(BF16)
        place = pl.ds(pl.multiple_of(block * BLOCK, BLOCK), BLOCK)
        for n, head in enumerate(heads):
            stat_out[head, 0:1, place] = block_of(top, n)
            stat_out[head, 1:2, place] = jnp.sum(totals[n], axis=0, keepdims=True)
            wide_out[head, block] = dot(omega_turned[head], probs[head, :, columns])

    def block_zero(head):
        q_head = q_all[head, 0:8].reshape(BLOCK, HEAD)
        piece = jnp.where(key_row <= limits(0), dot(k_all[0], q_head, LANES), MASKED)
        scores_first[head] = piece
        top = jnp.max(piece, axis=0, keepdims=True)
        weight = jnp.exp2((piece - top) * SCALE)
        probs_first[head] = weight.astype(BF16)
        stat_out[head, 0:1, :BLOCK] = top
        stat_out[head, 1:2, :BLOCK] = jnp.sum(weight, axis=0, keepdims=True)
        wide_out[head, 0] = dot(omega_turned[head, :, :BLOCK], probs_first[head])

    @pl.when(s == 0)
    def _():
        others(RING, z, q_arrived)
        each(HEADS, block_zero)

    steps = jnp.where(y == 0, 3, PLANES - y)

    def one_block(step):
        block = jnp.where(y == 0, jnp.where(step == 0, 3, step), y + step)
        columns = pl.ds(pl.multiple_of((block - 1) * BLOCK, BLOCK), BLOCK)

        @pl.when(jnp.where(y == 0, block != 3, (block == 3) & (y < 3)))
        def _():
            each(RING, lambda d: q_arrived(at_seq(block, d)))

        def run(pair):
            two = [head_at(4 * pair + n) for n in range(4)]
            first_block(block, columns, [head for _, _, head in two])

            @pl.when(step == steps - 1)
            def _():
                for plane, j, head in two:
                    send_first(plane, j, head)

        def send_first(plane, j, head):
            @pl.when(plane != y)
            def _():
                stat_y_copy(head, plane, j, y).start()

            y_send(wide_out, wide_y, wy_send, wy_recv, head, plane, j, True)

            @pl.when(plane == y)
            def _():
                wide_y[y, j] = wide_out[head]
                stat_y[y, j] = stat_out[head]

        each(HEADS // 4, run)

    each(steps, one_block)

    def merge_scale(value, top):
        return jnp.exp2((value - top) * SCALE)

    def join_wide(j):
        for plane in range(PLANES):
            @pl.when(plane != y)
            def _():
                stat_y_copy(0, plane, j, plane).wait_recv()

        tops = [stat_y[p, j, 0:1, :] for p in range(PLANES)]
        top = functools.reduce(jnp.maximum, tops)
        scales = [merge_scale(value, top) for value in tops]
        stat_sum[j, 0:1, :] = top
        stat_sum[j, 1:2, :] = sum(stat_y[p, j, 1:2, :] * scales[p] for p in range(PLANES))

        @pl.when(owner_z(j) == z)
        def _():
            stat_z[z] = stat_sum[j]

        @pl.when(owner_z(j) != z)
        def _():
            stat_z_copy(j, z).start()

        y_wait(wide_out, wide_y, wy_send, wy_recv, j)
        for block in range(1, PLANES):
            wide_sum[j, block] = sum(
                wide_y[p, j, block] * block_of(scales[p], block) for p in range(block + 1)
            )

        @pl.when(z == 0)
        def _():
            wide_sum[j, 0] = wide_y[0, j, 0] * block_of(scales[0], 0)

        @pl.when(owner_z(j) == z)
        def _():
            wide_z[z] = wide_sum[j]

        z_send(wide_sum, wide_z, wz_send, wz_recv, j, True)

    def stat_z_copy(j, source):
        return remote(
            stat_sum.at[j], stat_z.at[source], stz_send.at[j], stz_recv.at[source],
            seq=at_seq(y, owner_z(j)),
        )

    def stat_share(d):
        return remote(
            stat_all.at[own_head], stat_all.at[own_head], sta_send.at[d], st_recv.at[own_head],
            seq=at_seq(y, d),
        )

    def around(d, everything, act):
        whole = (d == 0) | everything
        pl.when(whole)(lambda: act(0))
        pl.when(~whole)(lambda: act(1))

    def share_basis(everything, start):
        def run(d):
            def act(first):
                copy = remote(
                    cut(basis, own_head, first=first), cut(basis, own_head, first=first),
                    bz_send.at[d], b_recv.at[own_head], seq=at_seq(y, d),
                )
                if start:
                    copy.start()
                else:
                    copy.wait_send()

            around(d, everything, act)

        others(RING, z, run)

    def store_basis(rows):
        for block in range(PLANES):
            basis[own_head, block] = block_of(rows, block).astype(BF16)

    def own_wide():
        others(RING, z, lambda d: stat_z_copy(0, d).wait_recv())
        top = functools.reduce(jnp.maximum, [stat_z[d, 0:1, :] for d in range(RING)])
        scales = [merge_scale(stat_z[d, 0:1, :], top) for d in range(RING)]
        inverse = 1.0 / sum(stat_z[d, 1:2, :] * scales[d] for d in range(RING))
        stat_all[own_head, 0:1, :] = top
        stat_all[own_head, 1:2, :] = inverse
        others(RING, z, lambda d: stat_share(d).start())
        z_wait(wide_sum, wide_z, wz_send, wz_recv)
        pieces = [wide_z[0, 0] * block_of(scales[0], 0)]
        for block in range(1, PLANES):
            pieces.append(sum(wide_z[d, block] * block_of(scales[d], block) for d in range(RING)))
        store_basis(orthonormal_rows(jnp.concatenate(pieces, axis=1) * inverse))
        share_basis(False, True)

    each(2, join_wide)
    pl.when(owns)(own_wide)

    def stat_pass(j, plane):
        head = 2 * y + j
        return remote(
            stat_all.at[head], stat_all.at[head], stb_send.at[j, plane], st_recv.at[head],
            seq=at_seq(plane, z),
        )

    def stat_wait(head):
        remote(stat_all.at[head], stat_all.at[head], sta_send.at[0], st_recv.at[head], seq=s).wait_recv()

    def relay_stats(j):
        @pl.when(owner_z(j) != z)
        def _():
            stat_wait(2 * y + j)

        others(PLANES, y, lambda plane: stat_pass(j, plane).start())

    def relay_basis(j, last, start):
        head = 2 * y + j
        if start:
            @pl.when(owner_z(j) != z)
            def _():
                def arrived(first):
                    remote(
                        cut(basis, head, first=first), cut(basis, head, first=first),
                        bz_send.at[0], b_recv.at[head], seq=s,
                    ).wait_recv()

                around(z, last, arrived)

        for plane in range(PLANES):
            @pl.when(plane != y)
            def _():
                def act(first):
                    copy = remote(
                        cut(basis, head, first=first), cut(basis, head, first=first),
                        by_send.at[j, plane], b_recv.at[head], seq=at_seq(plane, z),
                    )
                    if start:
                        copy.start()
                    else:
                        copy.wait_send()

                spans(plane, act, last)

    def wait_basis(plane, head, last):
        @pl.when(plane != y)
        def _():
            def act(first):
                remote(
                    cut(basis, head, first=first), cut(basis, head, first=first),
                    by_send.at[0, 0], b_recv.at[head], seq=at_seq(plane, z),
                ).wait_recv()

            spans(y, act, last)

    relay_stats(0)
    relay_stats(1)

    def normalise(index):
        plane, j, head = head_at(index)

        @pl.when(plane != y)
        def _():
            stat_wait(head)

        def run(block):
            columns = pl.ds(pl.multiple_of((block - 1) * BLOCK, BLOCK), BLOCK)
            place = pl.ds(pl.multiple_of(block * BLOCK, BLOCK), BLOCK)
            top = stat_all[head, 0:1, place]
            inverse = stat_all[head, 1:2, place]
            for chunk in range(KEYS // CHUNK):
                at = slice(chunk * CHUNK, (chunk + 1) * CHUNK)
                weight = merge_scale(scores[head, at, columns], top)
                probs[head, at, columns] = (weight * inverse).astype(BF16)

        each(PLANES, run, jnp.maximum(y, 1))

        @pl.when(s == 0)
        def _():
            weight = merge_scale(scores_first[head], stat_all[head, 0:1, :BLOCK])
            probs_first[head] = (weight * stat_all[head, 1:2, :BLOCK]).astype(BF16)

    @pl.when(owns)
    def _():
        relay_basis(own_j, False, True)

    each(HEADS, normalise)

    def forward(head, plane, j, panel):
        product = dot(panel, probs[head]).astype(BF16)
        for b in range(3):
            part_out[head, b + 1] = product[:, b * BLOCK : (b + 1) * BLOCK]

        @pl.when(s == 0)
        def _():
            part_out[head, 0] = dot(panel[:, :BLOCK], probs_first[head]).astype(BF16)

        @pl.when(plane == y)
        def _():
            part_y[y, j] = part_out[head]

    def backward(head):
        low = jnp.concatenate([basis[head, 1], basis[head, 2], basis[head, 3]], axis=1)
        product = dot(low, probs[head], LANES)
        first = dot(basis[head, 0], probs_first[head], LANES)
        return jnp.concatenate([product[:, :BLOCK] + first, product[:, BLOCK:]], axis=1)

    def join_parts(j):
        y_wait(part_out, part_y, py_send, py_recv, j)
        relay_basis(j, False, False)
        for block in range(1, PLANES):
            part_sum[j, block] = sum(
                part_y[p, j, block].astype(F32) for p in range(block + 1)
            ).astype(BF16)

        @pl.when(z == 0)
        def _():
            part_sum[j, 0] = part_y[0, j, 0]

        @pl.when(owner_z(j) == z)
        def _():
            part_z[z] = part_sum[j]

        z_send(part_sum, part_z, pz_send, pz_recv, j, True)

    def own_parts(step):
        z_wait(part_sum, part_z, pz_send, pz_recv)
        pieces = [part_z[0, 0].astype(F32)]
        for block in range(1, PLANES):
            pieces.append(sum(part_z[d, block].astype(F32) for d in range(RING)))
        rows = orthonormal_rows(jnp.concatenate(pieces, axis=1))
        share_basis(False, False)
        store_basis(rows)
        share_basis(step == POWER - 1, True)

    def power_step(step):
        def relay(j):
            @pl.when(~((step == 0) & (owner_z(j) == z)))
            def _():
                relay_basis(j, False, True)

        def one_head(index):
            plane, j, head = head_at(index)
            wait_basis(plane, head, False)
            forward(head, plane, j, backward(head).astype(BF16))
            y_send(part_out, part_y, py_send, py_recv, head, plane, j, True)

        each(2, relay)
        each(HEADS, one_head)
        each(2, join_parts)
        pl.when(owns)(lambda: own_parts(step))

        def sent(index):
            plane, j, head = head_at(index)
            y_send(part_out, part_y, py_send, py_recv, head, plane, j, False)

        each(HEADS, sent)
        z_send(part_sum, part_z, pz_send, pz_recv, 0, False)
        z_send(part_sum, part_z, pz_send, pz_recv, 1, False)

    each(POWER, power_step)

    def store_copy(head):
        rows = pl.ds(pl.multiple_of(head * RANK, RANK), RANK)
        return pltpu.make_async_copy(staged.at[rows], proj_hbm.at[rows], store_sem.at[head])

    each(2, lambda j: relay_basis(j, True, True))

    def last_head(index):
        plane, j, head = head_at(index)
        wait_basis(plane, head, True)
        rows = pl.ds(pl.multiple_of(head * RANK, RANK), RANK)
        staged[rows, :] = backward(head)
        store_copy(head).start()

    each(HEADS, last_head)

    row = lax.broadcasted_iota(jnp.int32, (16, QUERIES), 0)
    lane = lax.broadcasted_iota(jnp.int32, (16, QUERIES), 1)
    chosen = lane == s * 16 + 8 * lax.rem(row, 2) + lax.div(row, 2)
    chosen = jnp.where(chosen, 1.0, 0.0).astype(BF16)
    total = jnp.zeros((16, HEADS * RANK), F32)
    for block in range(PLANES):
        total = total + dot(
            chosen[:, block * BLOCK : (block + 1) * BLOCK],
            basis[:, block].reshape(HEADS * RANK, BLOCK),
            LANES,
        )
    basis_ref[...] = total

    each(HEADS, lambda head: store_copy(head).wait())
    others(KVH, k, lambda d: q_copy(d, k).wait_send())
    others(KVH, k, lambda d: k_copy(d, k).wait_send())
    q_rounds(lambda d: q_round(d).wait_send())
    pass_all(False)

    def sent_wide(index):
        plane, j, head = head_at(index)

        @pl.when(plane != y)
        def _():
            stat_y_copy(head, plane, j, y).wait_send()

        y_send(wide_out, wide_y, wy_send, wy_recv, head, plane, j, False)

    each(HEADS, sent_wide)
    for j in range(2):
        z_send(wide_sum, wide_z, wz_send, wz_recv, j, False)

        @pl.when(owner_z(j) != z)
        def _():
            stat_z_copy(j, z).wait_send()

        others(PLANES, y, lambda plane: stat_pass(j, plane).wait_send())
        relay_basis(j, True, False)

    @pl.when(owns)
    def _():
        others(RING, z, lambda d: stat_share(d).wait_send())
        share_basis(True, False)


def body(queries, keys, omega, block_offsets):
    vmem = lambda shape, kind: pltpu.VMEM(shape, kind)
    dma = lambda *shape: pltpu.SemaphoreType.DMA(shape)
    panel = (PLANES, RANK, BLOCK)
    basis, projection = pl.pallas_call(
        kernel,
        out_shape=(
            jax.ShapeDtypeStruct((16, HEADS * RANK), F32),
            jax.ShapeDtypeStruct((HEADS * RANK, KEYS), F32),
        ),
        in_specs=[
            pl.BlockSpec(memory_space=pltpu.SMEM),
            pl.BlockSpec(memory_space=pltpu.VMEM),
            pl.BlockSpec(memory_space=pl.ANY),
            pl.BlockSpec(memory_space=pl.ANY),
        ],
        out_specs=(
            pl.BlockSpec(memory_space=pltpu.VMEM),
            pl.BlockSpec(memory_space=pl.ANY),
        ),
        scratch_shapes=[
            vmem((128, HEAD), F32),
            vmem((KVH, 16, HEAD), BF16),
            vmem((KVH, 16, HEAD), BF16),
            vmem((128, HEAD), F32),
            vmem((128, HEAD), F32),
            vmem((HEADS, 16, HEAD), BF16),
            vmem((HEADS, SEQ, 16, HEAD), BF16),
            vmem((KVH, 128, HEAD), BF16),
            vmem((KEYS, HEADS * RANK), BF16),
            vmem((HEADS, RANK, KEYS), BF16),
            vmem((HEADS, KEYS, WIDE), F32),
            vmem((HEADS, BLOCK, BLOCK), F32),
            vmem((HEADS, KEYS, WIDE), BF16),
            vmem((HEADS, BLOCK, BLOCK), BF16),
            vmem((HEADS, 2, QUERIES), F32),
            vmem((PLANES, 2, 2, QUERIES), F32),
            vmem((2, 2, QUERIES), F32),
            vmem((RING, 2, QUERIES), F32),
            vmem((HEADS, 2, QUERIES), F32),
            vmem((HEADS, *panel), F32),
            vmem((PLANES, 2, *panel), F32),
            vmem((2, *panel), F32),
            vmem((RING, *panel), F32),
            vmem((HEADS, *panel), BF16),
            vmem((PLANES, 2, *panel), BF16),
            vmem((2, *panel), BF16),
            vmem((RING, *panel), BF16),
            vmem((HEADS, *panel), BF16),
            vmem((HEADS * RANK, KEYS), F32),
            dma(2),
            dma(HEADS),
            dma(KVH), dma(KVH),
            dma(KVH), dma(KVH),
            dma(RING), dma(2, SEQ), dma(SEQ),
            dma(HEADS), dma(PLANES, 2),
            dma(2), dma(RING),
            dma(RING), dma(2, PLANES), dma(HEADS),
            dma(HEADS), dma(PLANES, 2),
            dma(2), dma(RING),
            dma(HEADS), dma(PLANES, 2),
            dma(2), dma(RING),
            dma(RING), dma(2, PLANES), dma(HEADS),
        ],
        compiler_params=pltpu.CompilerParams(
            collective_id=0, has_side_effects=True, vmem_limit_bytes=56 * 2**20
        ),
        cost_estimate=pl.CostEstimate(
            flops=6 * 10**9, bytes_accessed=8 * 2**20, transcendentals=8 * 10**6
        ),
        name="range_finder",
    )(block_offsets, queries, keys, omega)
    return basis * math.sqrt(QUERIES), projection * math.sqrt(SEQ * KEYS)


def solution(mesh):
    placed = (P(("seq", "kvh"), None), P(("seq", "kvh"), None), P("seq", "kvh"), P())
    return jax.shard_map(
        body,
        mesh=mesh,
        in_specs=placed,
        out_specs=(P("seq", "kvh"), P("kvh", "seq")),
        check_vma=False,
    )
```

```python
import functools
import math

import jax
import jax.numpy as jnp
from jax import lax
from jax.experimental import pallas as pl
from jax.experimental.pallas import tpu as pltpu
from jax.sharding import PartitionSpec as P

MESH = pl.DeviceIdType.MESH
F32 = jnp.float32
BF16 = jnp.bfloat16
HIGHEST = lax.Precision.HIGHEST

SEQ = 32
KVH = 8
PLANES = 4
RING = 8
HEADS = 8
HEAD = 128
RANK = 64
BLOCK = 128
QUERIES = 512
WIDE = QUERIES - BLOCK
KEYS = 1024
POWER = 2
CHUNK = 128

MASKED = -1e30
LOWEST = -1e29
SCALE = math.log2(math.e) / math.sqrt(HEAD)

LANES = (((1,), (1,)), ((), ()))
PLAIN = (((1,), (0,)), ((), ()))


def dot(left, right, dims=PLAIN, precision=None):
    return lax.dot_general(left, right, dims, precision=precision, preferred_element_type=F32)


def each(count, step, start=0):
    def run(index, carry):
        step(index)
        return carry

    lax.fori_loop(start, count, run, 0)


def inverse_factor(gram):
    lanes = lax.broadcasted_iota(jnp.int32, (RANK, RANK), 1)
    rows = lax.broadcasted_iota(jnp.int32, (RANK, RANK), 0)
    start = jnp.concatenate([gram, jnp.where(lanes == rows, 1.0, 0.0)], axis=1)
    sub = lax.broadcasted_iota(jnp.int32, (8, 2 * RANK), 0)

    def spread(tile, lane):
        return jnp.broadcast_to(tile[:, lane : lane + 1], tile.shape)

    def lift(tile, row):
        return jnp.broadcast_to(tile[row : row + 1, :], tile.shape)

    tiles = [start[8 * i : 8 * i + 8] for i in range(8)]
    for step in range(8):
        pivot = tiles[step]
        columns = [spread(pivot, 8 * step + j) for j in range(8)]
        inverses, upper, roots = [], [], jnp.zeros_like(pivot)
        for j in range(8):
            diagonal = lift(columns[j], j)
            inverse = 1.0 / diagonal
            inverses.append(inverse)
            roots = jnp.where(sub == j, lax.rsqrt(diagonal), roots)
            factor = jnp.where(sub > j, columns[j] * inverse, 0.0)
            pivot = pivot - factor * lift(pivot, j)
            across = {}
            for other in range(j + 1, 8):
                across[other] = lift(columns[other], j)
                columns[other] = columns[other] - factor * across[other]
            upper.append(across)
        pivot_rows = [lift(pivot, j) for j in range(8)]
        for index in range(step + 1, 8):
            tile = tiles[index]
            columns = [spread(tile, 8 * step + j) for j in range(8)]
            for j in range(8):
                factor = columns[j] * inverses[j]
                tile = tile - factor * pivot_rows[j]
                for other in range(j + 1, 8):
                    columns[other] = columns[other] - factor * upper[j][other]
            tiles[index] = tile
        tiles[step] = pivot * roots
    return jnp.concatenate(tiles, axis=0)[:, RANK:]


def orthonormal_rows(panel):
    gram = dot(panel, panel, LANES, HIGHEST)
    return dot(inverse_factor(gram), panel, PLAIN, HIGHEST)


def kernel(
    offsets_hbm,
    q_hbm,
    k_hbm,
    omega_hbm,
    basis_hbm,
    proj_hbm,
    q_wide,
    q_tiles,
    q_got,
    q_flat,
    q_turned,
    q_own,
    q_all,
    k_all,
    omega_rows,
    omega_turned,
    scores,
    scores_first,
    probs,
    probs_first,
    stat_out,
    stat_y,
    stat_sum,
    stat_z,
    stat_all,
    wide_out,
    wide_y,
    wide_sum,
    wide_z,
    part_out,
    part_y,
    part_sum,
    part_z,
    basis,
    staged,
    chosen_rows,
    offsets,
    q_ref,
    local_sem,
    store_sem,
    qk_send,
    qk_recv,
    kk_send,
    kk_recv,
    qz_send,
    qf_send,
    q_recv,
    sty_send,
    sty_recv,
    stz_send,
    stz_recv,
    sta_send,
    stb_send,
    st_recv,
    wy_send,
    wy_recv,
    wz_send,
    wz_recv,
    py_send,
    py_recv,
    pz_send,
    pz_recv,
    bz_send,
    by_send,
    b_recv,
):
    s = lax.axis_index("seq")
    k = lax.axis_index("kvh")
    y = lax.div(s, RING)
    z = lax.rem(s, RING)
    core = lax.rem(k, 2)

    def owner_z(j):
        return 2 * (2 * j + core)

    own_j = lax.div(z, 4)
    own_head = 2 * y + own_j
    owns = owner_z(own_j) == z

    def at_seq(plane, place):
        return plane * RING + place

    def remote(src, dst, send, recv, **target):
        return pltpu.make_async_remote_copy(
            src_ref=src, dst_ref=dst, send_sem=send, recv_sem=recv,
            device_id=target, device_id_type=MESH,
        )

    def others(count, me, step):
        def run(d):
            @pl.when(d != me)
            def _():
                step(d)

        each(count, run)

    offsets_copy = pltpu.make_async_copy(offsets_hbm, offsets, local_sem.at[2])
    q_copy_in = pltpu.make_async_copy(q_hbm, q_ref, local_sem.at[3])
    q_copy_in.start()
    offsets_copy.start()
    barrier = pltpu.get_barrier_semaphore()

    def greet(**target):
        pl.semaphore_signal(barrier, inc=1, device_id=target, device_id_type=MESH)

    for hop in (4, 3, 5, 2, 6, 1, 7):
        greet(seq=at_seq(y, lax.rem(z + hop, RING)))
    for hop in (2, 1, 3):
        greet(seq=at_seq(lax.rem(y + hop, PLANES), z))
    others(KVH, k, lambda d: greet(kvh=d))

    omega_copy = pltpu.make_async_copy(omega_hbm, omega_rows, local_sem.at[0])
    omega_copy.start()
    keys_copy = pltpu.make_async_copy(
        k_hbm.at[:, pl.ds(pl.multiple_of(k * HEAD, HEAD), HEAD)], k_all.at[k], local_sem.at[1]
    )
    keys_copy.start()

    q_copy_in.wait()
    offsets_copy.wait()
    q_now = q_ref[...].astype(F32)
    for tile in range(KVH * HEADS):
        q_wide[2 * tile : 2 * tile + 2, :] = q_now[:, tile * HEAD : (tile + 1) * HEAD]
    q_tiles[...] = q_wide[...].astype(BF16).reshape(KVH, 16, HEAD)
    q_got[k] = q_tiles[k]

    basis[...] = jnp.zeros(basis.shape, BF16)
    probs_first[...] = jnp.zeros(probs_first.shape, BF16)
    stat_out[:, 0:1, :] = jnp.full((HEADS, 1, QUERIES), LOWEST, F32)
    stat_out[:, 1:2, :] = jnp.zeros((HEADS, 1, QUERIES), F32)

    @pl.when(y >= 2)
    def _():
        def clear(head):
            probs[head] = jnp.zeros((KEYS, WIDE), BF16)

        each(HEADS, clear)

    pl.semaphore_wait(barrier, KVH - 1 + RING - 1 + PLANES - 1)

    def q_copy(d, slot):
        return remote(q_tiles.at[d], q_got.at[slot], qk_send.at[d], qk_recv.at[slot], kvh=d)

    def k_copy(d, slot):
        columns = pl.ds(pl.multiple_of(d * HEAD, HEAD), HEAD)
        return remote(k_hbm.at[:, columns], k_all.at[slot], kk_send.at[d], kk_recv.at[slot], kvh=d)

    others(KVH, k, lambda d: q_copy(d, k).start())
    others(KVH, k, lambda d: k_copy(d, k).start())
    others(KVH, k, lambda d: q_copy(d, d).wait_recv())

    q_flat[...] = q_got[...].astype(F32).reshape(KVH * 16, HEAD)
    for pair in range(16):
        q_turned[8 * pair : 8 * pair + 8, :] = q_flat[pl.ds(pair, 8, stride=16), :]
    q_own[...] = q_turned[...].astype(BF16).reshape(HEADS, 16, HEAD)
    q_all[:, s] = q_own[...]

    def q_round(d):
        return remote(q_own, q_all.at[:, s], qz_send.at[d], q_recv.at[s], seq=at_seq(y, d))

    def q_pass(piece, way, plane):
        return remote(
            q_all.at[:, piece], q_all.at[:, piece], qf_send.at[way, piece], q_recv.at[piece],
            seq=at_seq(plane, z),
        )

    def q_arrived(piece):
        remote(q_own, q_all.at[:, piece], qz_send.at[0], q_recv.at[piece], seq=piece).wait_recv()

    def q_rounds(step):
        def run(index):
            d = lax.rem(z + index, RING)

            @pl.when((y > 0) | (d == 0))
            def _():
                step(d)

        each(RING, run, 1)

    q_rounds(lambda d: q_round(d).start())

    def pass_block(block, own, step, start):
        def run(index):
            place = lax.rem(z + index, RING)
            piece = at_seq(block, place)
            if start:
                if own:
                    pl.when(index > 0)(lambda: q_arrived(piece))
                else:
                    q_arrived(piece)
            step(piece, lax.rem(place, 2) == 1)

        each(RING, run)

    def pass_all(start):
        def go(piece, way, plane):
            copy = q_pass(piece, way, plane)
            if start:
                copy.start()
            else:
                copy.wait_send()

        @pl.when(y == 3)
        def _():
            def both(piece, odd):
                go(piece, 0, 0)
                go(piece, 1, 2)

            pass_block(3, True, both, start)

            def other(index):
                piece = at_seq(2, 2 * index + 1)
                if start:
                    q_arrived(piece)
                go(piece, 0, 0)

            each(RING // 2, other)

        @pl.when(y == 2)
        def _():
            def both(piece, odd):
                pl.when(odd)(lambda: go(piece, 1, 3))
                go(piece, 0, 1)

            pass_block(2, True, both, start)

        @pl.when(y == 1)
        def _():
            pass_block(1, True, lambda piece, odd: go(piece, 0, 0), start)
            pass_block(
                2, False, lambda piece, odd: pl.when(~odd)(lambda: go(piece, 0, 0)), start
            )

        @pl.when(y == 0)
        def _():
            pass_block(3, False, lambda piece, odd: go(piece, 0, 1), start)

    omega_copy.wait()
    for tile in range(4):
        turned = omega_rows[:, tile * 128 : (tile + 1) * 128].astype(F32).T.astype(BF16)
        omega_turned[2 * tile] = turned[:RANK]
        omega_turned[2 * tile + 1] = turned[RANK:]

    pass_all(True)
    keys_copy.wait()
    others(KVH, k, lambda d: k_copy(d, d).wait_recv())

    lane = lax.broadcasted_iota(jnp.int32, (1, BLOCK), 1)
    place = lax.rem(lane, 16)
    row_in_block = lane - place + 2 * lax.rem(place, 8) + lax.div(place, 8)
    key_row = lax.broadcasted_iota(jnp.int32, (CHUNK, 1), 0)

    def block_of(row, block):
        return row[:, block * BLOCK : (block + 1) * BLOCK]

    def limits(block):
        return offsets[block] * BLOCK + row_in_block - s * KEYS

    def fold(tile, join):
        return join(tile.reshape(CHUNK // 8, 8, tile.shape[1]), axis=0)

    def head_at(index):
        plane = lax.rem(y + lax.div(index, 2), PLANES)
        j = lax.rem(index, 2)
        return plane, j, 2 * plane + j

    def spans(plane, act, everything=False):
        whole = (z == 0) | everything
        if isinstance(plane, int):
            if plane:
                act(plane)
            else:
                pl.when(whole)(lambda: act(0))
                pl.when(~whole)(lambda: act(1))
        else:
            pl.when((plane == 0) & whole)(lambda: act(0))
            pl.when((plane == 1) | ((plane == 0) & ~whole))(lambda: act(1))
            pl.when(plane == 2)(lambda: act(2))
            pl.when(plane == 3)(lambda: act(3))

    def cut(ref, *place, first):
        return ref.at[(*place, pl.ds(first, PLANES - first))]

    def y_send(out, landing, send, recv, head, plane, j, start):
        @pl.when(plane != y)
        def _():
            def act(first):
                copy = remote(
                    cut(out, head, first=first), cut(landing, y, j, first=first),
                    send.at[head], recv.at[y, j], seq=at_seq(plane, z),
                )
                if start:
                    copy.start()
                else:
                    copy.wait_send()

            spans(y, act)

    def y_wait(out, landing, send, recv, j):
        for plane in range(PLANES):
            @pl.when(plane != y)
            def _():
                def act(first):
                    remote(
                        cut(out, 0, first=first), cut(landing, plane, j, first=first),
                        send.at[0], recv.at[plane, j], seq=at_seq(plane, z),
                    ).wait_recv()

                spans(plane, act)

    def z_send(through, landing, send, recv, j, start):
        target = owner_z(j)

        @pl.when(target != z)
        def _():
            def act(first):
                copy = remote(
                    cut(through, j, first=first), cut(landing, z, first=first),
                    send.at[j], recv.at[z], seq=at_seq(y, target),
                )
                if start:
                    copy.start()
                else:
                    copy.wait_send()

            spans(0, act)

    def z_wait(through, landing, send, recv):
        def run(d):
            for first in (0, 1):
                @pl.when((d == 0) if first == 0 else (d != 0))
                def _():
                    remote(
                        cut(through, 0, first=first), cut(landing, d, first=first),
                        send.at[0], recv.at[d], seq=at_seq(y, d),
                    ).wait_recv()

        others(RING, z, run)

    def stat_y_copy(head, plane, j, source):
        return remote(
            stat_out.at[head], stat_y.at[source, j], sty_send.at[head], sty_recv.at[source, j],
            seq=at_seq(plane, z),
        )

    def first_block(block, columns, heads, masked):
        rows = pl.ds(pl.multiple_of(8 * block, 8), 8)
        q_heads = jnp.concatenate([q_all[h, rows].reshape(BLOCK, HEAD) for h in heads], axis=0)
        limit = limits(block)
        limit = jnp.concatenate([limit] * len(heads), axis=1)
        largest = jnp.full((8, len(heads) * BLOCK), LOWEST, F32)
        for chunk in range(KEYS // CHUNK):
            at = slice(chunk * CHUNK, (chunk + 1) * CHUNK)
            piece = dot(k_all[chunk], q_heads, LANES)
            if masked:
                piece = jnp.where(key_row + chunk * CHUNK <= limit, piece, MASKED)
            for n, head in enumerate(heads):
                scores[head, at, columns] = block_of(piece, n)
            largest = jnp.maximum(largest, fold(piece, jnp.max))
        top = jnp.max(largest, axis=0, keepdims=True)
        totals = [jnp.zeros((8, BLOCK), F32) for _ in heads]
        for chunk in range(KEYS // CHUNK):
            at = slice(chunk * CHUNK, (chunk + 1) * CHUNK)
            for n, head in enumerate(heads):
                weight = jnp.exp2((scores[head, at, columns] - block_of(top, n)) * SCALE)
                totals[n] = totals[n] + fold(weight, jnp.sum)
                probs[head, at, columns] = weight.astype(BF16)
        place = pl.ds(pl.multiple_of(block * BLOCK, BLOCK), BLOCK)
        for n, head in enumerate(heads):
            stat_out[head, 0:1, place] = block_of(top, n)
            stat_out[head, 1:2, place] = jnp.sum(totals[n], axis=0, keepdims=True)
            wide_out[head, block] = dot(omega_turned[head], probs[head, :, columns])

    def block_zero(head):
        q_head = q_all[head, 0:8].reshape(BLOCK, HEAD)
        piece = jnp.where(key_row <= limits(0), dot(k_all[0], q_head, LANES), MASKED)
        scores_first[head] = piece
        top = jnp.max(piece, axis=0, keepdims=True)
        weight = jnp.exp2((piece - top) * SCALE)
        probs_first[head] = weight.astype(BF16)
        stat_out[head, 0:1, :BLOCK] = top
        stat_out[head, 1:2, :BLOCK] = jnp.sum(weight, axis=0, keepdims=True)
        wide_out[head, 0] = dot(omega_turned[head, :, :BLOCK], probs_first[head])

    @pl.when(s == 0)
    def _():
        others(RING, z, q_arrived)
        each(HEADS, block_zero)

    steps = jnp.where(y == 0, 3, PLANES - y)

    def one_block(step):
        block = jnp.where(y == 0, jnp.where(step == 0, 3, step), y + step)
        columns = pl.ds(pl.multiple_of((block - 1) * BLOCK, BLOCK), BLOCK)

        @pl.when(jnp.where(y == 0, block != 3, (block == 3) & (y < 3)))
        def _():
            each(RING, lambda d: q_arrived(at_seq(block, d)))

        def run(pair):
            two = [head_at(4 * pair + n) for n in range(4)]
            heads = [head for _, _, head in two]
            pl.when(block == y)(lambda: first_block(block, columns, heads, True))
            pl.when(block != y)(lambda: first_block(block, columns, heads, False))

            @pl.when(step == steps - 1)
            def _():
                for plane, j, head in two:
                    send_first(plane, j, head)

        def send_first(plane, j, head):
            @pl.when(plane != y)
            def _():
                stat_y_copy(head, plane, j, y).start()

            y_send(wide_out, wide_y, wy_send, wy_recv, head, plane, j, True)

            @pl.when(plane == y)
            def _():
                wide_y[y, j] = wide_out[head]
                stat_y[y, j] = stat_out[head]

        each(HEADS // 4, run)

    each(steps, one_block)

    def merge_scale(value, top):
        return jnp.exp2((value - top) * SCALE)

    def join_wide(j):
        for plane in range(PLANES):
            @pl.when(plane != y)
            def _():
                stat_y_copy(0, plane, j, plane).wait_recv()

        tops = [stat_y[p, j, 0:1, :] for p in range(PLANES)]
        top = functools.reduce(jnp.maximum, tops)
        scales = [merge_scale(value, top) for value in tops]
        stat_sum[j, 0:1, :] = top
        stat_sum[j, 1:2, :] = sum(stat_y[p, j, 1:2, :] * scales[p] for p in range(PLANES))

        @pl.when(owner_z(j) == z)
        def _():
            stat_z[z] = stat_sum[j]

        @pl.when(owner_z(j) != z)
        def _():
            stat_z_copy(j, z).start()

        y_wait(wide_out, wide_y, wy_send, wy_recv, j)
        for block in range(1, PLANES):
            wide_sum[j, block] = sum(
                wide_y[p, j, block] * block_of(scales[p], block) for p in range(block + 1)
            )

        @pl.when(z == 0)
        def _():
            wide_sum[j, 0] = wide_y[0, j, 0] * block_of(scales[0], 0)

        @pl.when(owner_z(j) == z)
        def _():
            wide_z[z] = wide_sum[j]

        z_send(wide_sum, wide_z, wz_send, wz_recv, j, True)

    def stat_z_copy(j, source):
        return remote(
            stat_sum.at[j], stat_z.at[source], stz_send.at[j], stz_recv.at[source],
            seq=at_seq(y, owner_z(j)),
        )

    def stat_share(d):
        return remote(
            stat_all.at[own_head], stat_all.at[own_head], sta_send.at[d], st_recv.at[own_head],
            seq=at_seq(y, d),
        )

    def around(d, everything, act):
        whole = (d == 0) | everything
        pl.when(whole)(lambda: act(0))
        pl.when(~whole)(lambda: act(1))

    def share_basis(everything, start):
        def run(d):
            def act(first):
                copy = remote(
                    cut(basis, own_head, first=first), cut(basis, own_head, first=first),
                    bz_send.at[d], b_recv.at[own_head], seq=at_seq(y, d),
                )
                if start:
                    copy.start()
                else:
                    copy.wait_send()

            around(d, everything, act)

        others(RING, z, run)

    def store_basis(rows):
        for block in range(PLANES):
            basis[own_head, block] = block_of(rows, block).astype(BF16)

    def own_wide():
        others(RING, z, lambda d: stat_z_copy(0, d).wait_recv())
        top = functools.reduce(jnp.maximum, [stat_z[d, 0:1, :] for d in range(RING)])
        scales = [merge_scale(stat_z[d, 0:1, :], top) for d in range(RING)]
        inverse = 1.0 / sum(stat_z[d, 1:2, :] * scales[d] for d in range(RING))
        stat_all[own_head, 0:1, :] = top
        stat_all[own_head, 1:2, :] = inverse
        others(RING, z, lambda d: stat_share(d).start())
        z_wait(wide_sum, wide_z, wz_send, wz_recv)
        pieces = [wide_z[0, 0] * block_of(scales[0], 0)]
        for block in range(1, PLANES):
            pieces.append(sum(wide_z[d, block] * block_of(scales[d], block) for d in range(RING)))
        store_basis(orthonormal_rows(jnp.concatenate(pieces, axis=1) * inverse))
        share_basis(False, True)

    each(2, join_wide)
    pl.when(owns)(own_wide)

    def stat_pass(j, plane):
        head = 2 * y + j
        return remote(
            stat_all.at[head], stat_all.at[head], stb_send.at[j, plane], st_recv.at[head],
            seq=at_seq(plane, z),
        )

    def stat_wait(head):
        remote(stat_all.at[head], stat_all.at[head], sta_send.at[0], st_recv.at[head], seq=s).wait_recv()

    def relay_stats(j):
        @pl.when(owner_z(j) != z)
        def _():
            stat_wait(2 * y + j)

        others(PLANES, y, lambda plane: stat_pass(j, plane).start())

    def relay_basis(j, last, start):
        head = 2 * y + j
        if start:
            @pl.when(owner_z(j) != z)
            def _():
                def arrived(first):
                    remote(
                        cut(basis, head, first=first), cut(basis, head, first=first),
                        bz_send.at[0], b_recv.at[head], seq=s,
                    ).wait_recv()

                around(z, last, arrived)

        for plane in range(PLANES):
            @pl.when(plane != y)
            def _():
                def act(first):
                    copy = remote(
                        cut(basis, head, first=first), cut(basis, head, first=first),
                        by_send.at[j, plane], b_recv.at[head], seq=at_seq(plane, z),
                    )
                    if start:
                        copy.start()
                    else:
                        copy.wait_send()

                spans(plane, act, last)

    def wait_basis(plane, head, last):
        @pl.when(plane != y)
        def _():
            def act(first):
                remote(
                    cut(basis, head, first=first), cut(basis, head, first=first),
                    by_send.at[0, 0], b_recv.at[head], seq=at_seq(plane, z),
                ).wait_recv()

            spans(y, act, last)

    relay_stats(0)
    relay_stats(1)

    def normalise(index):
        plane, j, head = head_at(index)

        @pl.when(plane != y)
        def _():
            stat_wait(head)

        def run(block):
            columns = pl.ds(pl.multiple_of((block - 1) * BLOCK, BLOCK), BLOCK)
            place = pl.ds(pl.multiple_of(block * BLOCK, BLOCK), BLOCK)
            top = stat_all[head, 0:1, place]
            inverse = stat_all[head, 1:2, place]
            for chunk in range(KEYS // CHUNK):
                at = slice(chunk * CHUNK, (chunk + 1) * CHUNK)
                weight = merge_scale(scores[head, at, columns], top)
                probs[head, at, columns] = (weight * inverse).astype(BF16)

        each(PLANES, run, jnp.maximum(y, 1))

        @pl.when(s == 0)
        def _():
            weight = merge_scale(scores_first[head], stat_all[head, 0:1, :BLOCK])
            probs_first[head] = (weight * stat_all[head, 1:2, :BLOCK]).astype(BF16)

    @pl.when(owns)
    def _():
        relay_basis(own_j, False, True)

    each(HEADS, normalise)

    def forward(head, plane, j, panel):
        product = dot(panel, probs[head]).astype(BF16)
        for b in range(3):
            part_out[head, b + 1] = product[:, b * BLOCK : (b + 1) * BLOCK]

        @pl.when(s == 0)
        def _():
            part_out[head, 0] = dot(panel[:, :BLOCK], probs_first[head]).astype(BF16)

        @pl.when(plane == y)
        def _():
            part_y[y, j] = part_out[head]

    def backward(head):
        low = jnp.concatenate([basis[head, 1], basis[head, 2], basis[head, 3]], axis=1)
        product = dot(low, probs[head], LANES)
        first = dot(basis[head, 0], probs_first[head], LANES)
        return jnp.concatenate([product[:, :BLOCK] + first, product[:, BLOCK:]], axis=1)

    def join_parts(j):
        y_wait(part_out, part_y, py_send, py_recv, j)
        relay_basis(j, False, False)
        for block in range(1, PLANES):
            part_sum[j, block] = sum(
                part_y[p, j, block].astype(F32) for p in range(block + 1)
            ).astype(BF16)

        @pl.when(z == 0)
        def _():
            part_sum[j, 0] = part_y[0, j, 0]

        @pl.when(owner_z(j) == z)
        def _():
            part_z[z] = part_sum[j]

        z_send(part_sum, part_z, pz_send, pz_recv, j, True)

    def own_parts(step):
        z_wait(part_sum, part_z, pz_send, pz_recv)
        pieces = [part_z[0, 0].astype(F32)]
        for block in range(1, PLANES):
            pieces.append(sum(part_z[d, block].astype(F32) for d in range(RING)))
        rows = orthonormal_rows(jnp.concatenate(pieces, axis=1))
        share_basis(False, False)
        store_basis(rows)
        share_basis(step == POWER - 1, True)
        relay_basis(own_j, step == POWER - 1, True)

    def settle():
        others(KVH, k, lambda d: q_copy(d, k).wait_send())
        others(KVH, k, lambda d: k_copy(d, k).wait_send())
        q_rounds(lambda d: q_round(d).wait_send())
        pass_all(False)

        def sent_wide(index):
            plane, j, head = head_at(index)

            @pl.when(plane != y)
            def _():
                stat_y_copy(head, plane, j, y).wait_send()

            y_send(wide_out, wide_y, wy_send, wy_recv, head, plane, j, False)

        each(HEADS, sent_wide)
        for j in range(2):
            z_send(wide_sum, wide_z, wz_send, wz_recv, j, False)

            @pl.when(owner_z(j) != z)
            def _():
                stat_z_copy(j, z).wait_send()

            others(PLANES, y, lambda plane: stat_pass(j, plane).wait_send())

        @pl.when(owns)
        def _():
            others(RING, z, lambda d: stat_share(d).wait_send())

    def power_step(step):
        def relay(j):
            pl.when(owner_z(j) != z)(lambda: relay_basis(j, False, True))

        def one_head(index):
            plane, j, head = head_at(index)
            wait_basis(plane, head, False)
            forward(head, plane, j, backward(head).astype(BF16))
            y_send(part_out, part_y, py_send, py_recv, head, plane, j, True)

        each(2, relay)
        each(HEADS, one_head)
        each(2, join_parts)
        pl.when(owns)(lambda: own_parts(step))

        def sent(index):
            plane, j, head = head_at(index)
            y_send(part_out, part_y, py_send, py_recv, head, plane, j, False)

        each(HEADS, sent)
        z_send(part_sum, part_z, pz_send, pz_recv, 0, False)
        z_send(part_sum, part_z, pz_send, pz_recv, 1, False)
        pl.when(step == 0)(settle)

    each(POWER, power_step)

    def store_copy(head):
        rows = pl.ds(pl.multiple_of(head * RANK, RANK), RANK)
        return pltpu.make_async_copy(staged.at[rows], proj_hbm.at[rows], store_sem.at[head])

    def last_relay(j):
        pl.when(owner_z(j) != z)(lambda: relay_basis(j, True, True))

    each(2, last_relay)

    def last_head(index):
        plane, j, head = head_at(index)
        wait_basis(plane, head, True)
        rows = pl.ds(pl.multiple_of(head * RANK, RANK), RANK)
        staged[rows, :] = backward(head)
        store_copy(head).start()

    each(HEADS, last_head)

    row = lax.broadcasted_iota(jnp.int32, (16, QUERIES), 0)
    lane = lax.broadcasted_iota(jnp.int32, (16, QUERIES), 1)
    chosen = lane == s * 16 + 8 * lax.rem(row, 2) + lax.div(row, 2)
    chosen = jnp.where(chosen, 1.0, 0.0).astype(BF16)
    total = jnp.zeros((16, HEADS * RANK), F32)
    for block in range(PLANES):
        total = total + dot(
            chosen[:, block * BLOCK : (block + 1) * BLOCK],
            basis[:, block].reshape(HEADS * RANK, BLOCK),
            LANES,
        )
    chosen_rows[...] = total
    basis_copy = pltpu.make_async_copy(chosen_rows, basis_hbm, local_sem.at[0])
    basis_copy.start()

    each(HEADS, lambda head: store_copy(head).wait())
    basis_copy.wait()
    for j in range(2):
        relay_basis(j, True, False)
    pl.when(owns)(lambda: share_basis(True, False))


def body(queries, keys, omega, block_offsets):
    vmem = lambda shape, kind: pltpu.VMEM(shape, kind)
    dma = lambda *shape: pltpu.SemaphoreType.DMA(shape)
    panel = (PLANES, RANK, BLOCK)
    basis, projection = pl.pallas_call(
        kernel,
        out_shape=(
            jax.ShapeDtypeStruct((16, HEADS * RANK), F32),
            jax.ShapeDtypeStruct((HEADS * RANK, KEYS), F32),
        ),
        in_specs=[
            pl.BlockSpec(memory_space=pl.ANY),
            pl.BlockSpec(memory_space=pl.ANY),
            pl.BlockSpec(memory_space=pl.ANY),
            pl.BlockSpec(memory_space=pl.ANY),
        ],
        out_specs=(
            pl.BlockSpec(memory_space=pl.ANY),
            pl.BlockSpec(memory_space=pl.ANY),
        ),
        scratch_shapes=[
            vmem((128, HEAD), F32),
            vmem((KVH, 16, HEAD), BF16),
            vmem((KVH, 16, HEAD), BF16),
            vmem((128, HEAD), F32),
            vmem((128, HEAD), F32),
            vmem((HEADS, 16, HEAD), BF16),
            vmem((HEADS, SEQ, 16, HEAD), BF16),
            vmem((KVH, 128, HEAD), BF16),
            vmem((KEYS, HEADS * RANK), BF16),
            vmem((HEADS, RANK, KEYS), BF16),
            vmem((HEADS, KEYS, WIDE), F32),
            vmem((HEADS, BLOCK, BLOCK), F32),
            vmem((HEADS, KEYS, WIDE), BF16),
            vmem((HEADS, BLOCK, BLOCK), BF16),
            vmem((HEADS, 2, QUERIES), F32),
            vmem((PLANES, 2, 2, QUERIES), F32),
            vmem((2, 2, QUERIES), F32),
            vmem((RING, 2, QUERIES), F32),
            vmem((HEADS, 2, QUERIES), F32),
            vmem((HEADS, *panel), F32),
            vmem((PLANES, 2, *panel), F32),
            vmem((2, *panel), F32),
            vmem((RING, *panel), F32),
            vmem((HEADS, *panel), BF16),
            vmem((PLANES, 2, *panel), BF16),
            vmem((2, *panel), BF16),
            vmem((RING, *panel), BF16),
            vmem((HEADS, *panel), BF16),
            vmem((HEADS * RANK, KEYS), F32),
            vmem((16, HEADS * RANK), F32),
            pltpu.SMEM((4,), jnp.int32),
            vmem((2, KVH * HEADS * HEAD), BF16),
            dma(4),
            dma(HEADS),
            dma(KVH), dma(KVH),
            dma(KVH), dma(KVH),
            dma(RING), dma(2, SEQ), dma(SEQ),
            dma(HEADS), dma(PLANES, 2),
            dma(2), dma(RING),
            dma(RING), dma(2, PLANES), dma(HEADS),
            dma(HEADS), dma(PLANES, 2),
            dma(2), dma(RING),
            dma(HEADS), dma(PLANES, 2),
            dma(2), dma(RING),
            dma(RING), dma(2, PLANES), dma(HEADS),
        ],
        compiler_params=pltpu.CompilerParams(
            collective_id=0, has_side_effects=True, vmem_limit_bytes=56 * 2**20
        ),
        cost_estimate=pl.CostEstimate(
            flops=6 * 10**9, bytes_accessed=8 * 2**20, transcendentals=8 * 10**6
        ),
        name="range_finder",
    )(block_offsets, queries, keys, omega)
    return basis * math.sqrt(QUERIES), projection * math.sqrt(SEQ * KEYS)


def solution(mesh):
    placed = (P(("seq", "kvh"), None), P(("seq", "kvh"), None), P("seq", "kvh"), P())
    return jax.shard_map(
        body,
        mesh=mesh,
        in_specs=placed,
        out_specs=(P("seq", "kvh"), P("kvh", "seq")),
        check_vma=False,
    )
```

```python
import functools
import math

import jax
import jax.numpy as jnp
from jax import lax
from jax.experimental import pallas as pl
from jax.experimental.pallas import tpu as pltpu
from jax.sharding import PartitionSpec as P

MESH = pl.DeviceIdType.MESH
F32 = jnp.float32
BF16 = jnp.bfloat16
HIGHEST = lax.Precision.HIGHEST

SEQ = 32
KVH = 8
PLANES = 4
RING = 8
HEADS = 8
HEAD = 128
RANK = 64
BLOCK = 128
QUERIES = 512
WIDE = QUERIES - BLOCK
KEYS = 1024
POWER = 2
CHUNK = 128

MASKED = -1e30
LOWEST = -1e29
SCALE = math.log2(math.e) / math.sqrt(HEAD)

LANES = (((1,), (1,)), ((), ()))
PLAIN = (((1,), (0,)), ((), ()))


def dot(left, right, dims=PLAIN, precision=None):
    return lax.dot_general(left, right, dims, precision=precision, preferred_element_type=F32)


def each(count, step, start=0):
    def run(index, carry):
        step(index)
        return carry

    lax.fori_loop(start, count, run, 0)


def inverse_factor(gram):
    lanes = lax.broadcasted_iota(jnp.int32, (RANK, RANK), 1)
    rows = lax.broadcasted_iota(jnp.int32, (RANK, RANK), 0)
    start = jnp.concatenate([gram, jnp.where(lanes == rows, 1.0, 0.0)], axis=1)
    sub = lax.broadcasted_iota(jnp.int32, (8, 2 * RANK), 0)

    def spread(tile, lane):
        return jnp.broadcast_to(tile[:, lane : lane + 1], tile.shape)

    def lift(tile, row):
        return jnp.broadcast_to(tile[row : row + 1, :], tile.shape)

    tiles = [start[8 * i : 8 * i + 8] for i in range(8)]
    for step in range(8):
        pivot = tiles[step]
        columns = [spread(pivot, 8 * step + j) for j in range(8)]
        inverses, upper, roots = [], [], jnp.zeros_like(pivot)
        for j in range(8):
            diagonal = lift(columns[j], j)
            inverse = 1.0 / diagonal
            inverses.append(inverse)
            roots = jnp.where(sub == j, lax.rsqrt(diagonal), roots)
            factor = jnp.where(sub > j, columns[j] * inverse, 0.0)
            pivot = pivot - factor * lift(pivot, j)
            across = {}
            for other in range(j + 1, 8):
                across[other] = lift(columns[other], j)
                columns[other] = columns[other] - factor * across[other]
            upper.append(across)
        pivot_rows = [lift(pivot, j) for j in range(8)]
        for index in range(step + 1, 8):
            tile = tiles[index]
            columns = [spread(tile, 8 * step + j) for j in range(8)]
            for j in range(8):
                factor = columns[j] * inverses[j]
                tile = tile - factor * pivot_rows[j]
                for other in range(j + 1, 8):
                    columns[other] = columns[other] - factor * upper[j][other]
            tiles[index] = tile
        tiles[step] = pivot * roots
    return jnp.concatenate(tiles, axis=0)[:, RANK:]


def orthonormal_rows(panel):
    gram = dot(panel, panel, LANES, HIGHEST)
    return dot(inverse_factor(gram), panel, PLAIN, HIGHEST)


def kernel(
    offsets_hbm,
    q_hbm,
    k_hbm,
    omega_hbm,
    basis_hbm,
    proj_hbm,
    q_wide,
    q_tiles,
    q_got,
    q_flat,
    q_turned,
    q_own,
    q_all,
    k_all,
    omega_rows,
    omega_turned,
    scores,
    scores_first,
    probs,
    probs_first,
    stat_out,
    stat_y,
    stat_sum,
    stat_z,
    stat_all,
    wide_out,
    wide_y,
    wide_sum,
    wide_z,
    part_out,
    part_y,
    part_sum,
    part_z,
    basis,
    staged,
    chosen_rows,
    offsets,
    q_ref,
    local_sem,
    store_sem,
    qk_send,
    qk_recv,
    kk_send,
    kk_recv,
    qz_send,
    qf_send,
    q_recv,
    sty_send,
    sty_recv,
    stz_send,
    stz_recv,
    sta_send,
    stb_send,
    st_recv,
    wy_send,
    wy_recv,
    wz_send,
    wz_recv,
    py_send,
    py_recv,
    pz_send,
    pz_recv,
    bz_send,
    by_send,
    b_recv,
):
    s = lax.axis_index("seq")
    k = lax.axis_index("kvh")
    y = lax.div(s, RING)
    z = lax.rem(s, RING)
    core = lax.rem(k, 2)

    def owner_z(j):
        return 2 * (2 * j + core)

    own_j = lax.div(z, 4)
    own_head = 2 * y + own_j
    owns = owner_z(own_j) == z

    def at_seq(plane, place):
        return plane * RING + place

    def remote(src, dst, send, recv, **target):
        return pltpu.make_async_remote_copy(
            src_ref=src, dst_ref=dst, send_sem=send, recv_sem=recv,
            device_id=target, device_id_type=MESH,
        )

    def others(count, me, step):
        def run(d):
            @pl.when(d != me)
            def _():
                step(d)

        each(count, run)

    offsets_copy = pltpu.make_async_copy(offsets_hbm, offsets, local_sem.at[2])
    q_copy_in = pltpu.make_async_copy(q_hbm, q_ref, local_sem.at[3])
    q_copy_in.start()
    offsets_copy.start()
    barrier = pltpu.get_barrier_semaphore()

    def greet(**target):
        pl.semaphore_signal(barrier, inc=1, device_id=target, device_id_type=MESH)

    for hop in (4, 3, 5, 2, 6, 1, 7):
        greet(seq=at_seq(y, lax.rem(z + hop, RING)))
    for hop in (2, 1, 3):
        greet(seq=at_seq(lax.rem(y + hop, PLANES), z))
    others(KVH, k, lambda d: greet(kvh=d))

    omega_copy = pltpu.make_async_copy(omega_hbm, omega_rows, local_sem.at[0])
    omega_copy.start()
    keys_copy = pltpu.make_async_copy(
        k_hbm.at[:, pl.ds(pl.multiple_of(k * HEAD, HEAD), HEAD)], k_all.at[k], local_sem.at[1]
    )
    keys_copy.start()

    q_copy_in.wait()
    offsets_copy.wait()
    q_now = q_ref[...].astype(F32)
    for tile in range(KVH * HEADS):
        q_wide[2 * tile : 2 * tile + 2, :] = q_now[:, tile * HEAD : (tile + 1) * HEAD]
    q_tiles[...] = q_wide[...].astype(BF16).reshape(KVH, 16, HEAD)
    q_got[k] = q_tiles[k]

    basis[...] = jnp.zeros(basis.shape, BF16)
    probs_first[...] = jnp.zeros(probs_first.shape, BF16)
    stat_out[:, 0:1, :] = jnp.full((HEADS, 1, QUERIES), LOWEST, F32)
    stat_out[:, 1:2, :] = jnp.zeros((HEADS, 1, QUERIES), F32)

    @pl.when(y >= 2)
    def _():
        def clear(head):
            probs[head] = jnp.zeros((KEYS, WIDE), BF16)

        each(HEADS, clear)

    pl.semaphore_wait(barrier, KVH - 1 + RING - 1 + PLANES - 1)

    def q_copy(d, slot):
        return remote(q_tiles.at[d], q_got.at[slot], qk_send.at[d], qk_recv.at[slot], kvh=d)

    def k_copy(d, slot):
        columns = pl.ds(pl.multiple_of(d * HEAD, HEAD), HEAD)
        return remote(k_hbm.at[:, columns], k_all.at[slot], kk_send.at[d], kk_recv.at[slot], kvh=d)

    others(KVH, k, lambda d: q_copy(d, k).start())
    others(KVH, k, lambda d: k_copy(d, k).start())
    others(KVH, k, lambda d: q_copy(d, d).wait_recv())

    q_flat[...] = q_got[...].astype(F32).reshape(KVH * 16, HEAD)
    for pair in range(16):
        q_turned[8 * pair : 8 * pair + 8, :] = q_flat[pl.ds(pair, 8, stride=16), :]
    q_own[...] = q_turned[...].astype(BF16).reshape(HEADS, 16, HEAD)
    q_all[:, s] = q_own[...]

    def q_round(d):
        return remote(q_own, q_all.at[:, s], qz_send.at[d], q_recv.at[s], seq=at_seq(y, d))

    def q_pass(piece, way, plane):
        return remote(
            q_all.at[:, piece], q_all.at[:, piece], qf_send.at[way, piece], q_recv.at[piece],
            seq=at_seq(plane, z),
        )

    def q_arrived(piece):
        remote(q_own, q_all.at[:, piece], qz_send.at[0], q_recv.at[piece], seq=piece).wait_recv()

    def q_rounds(step):
        def run(index):
            d = lax.rem(z + index, RING)

            @pl.when((y > 0) | (d == 0))
            def _():
                step(d)

        each(RING, run, 1)

    q_rounds(lambda d: q_round(d).start())

    def pass_block(block, own, step, start):
        def run(index):
            place = lax.rem(z + index, RING)
            piece = at_seq(block, place)
            if start:
                if own:
                    pl.when(index > 0)(lambda: q_arrived(piece))
                else:
                    q_arrived(piece)
            step(piece, lax.rem(place, 2) == 1)

        each(RING, run)

    def pass_all(start):
        def go(piece, way, plane):
            copy = q_pass(piece, way, plane)
            if start:
                copy.start()
            else:
                copy.wait_send()

        @pl.when(y == 3)
        def _():
            def both(piece, odd):
                go(piece, 0, 0)
                go(piece, 1, 2)

            pass_block(3, True, both, start)

            def other(index):
                piece = at_seq(2, 2 * index + 1)
                if start:
                    q_arrived(piece)
                go(piece, 0, 0)

            each(RING // 2, other)

        @pl.when(y == 2)
        def _():
            def both(piece, odd):
                pl.when(odd)(lambda: go(piece, 1, 3))
                go(piece, 0, 1)

            pass_block(2, True, both, start)

        @pl.when(y == 1)
        def _():
            pass_block(1, True, lambda piece, odd: go(piece, 0, 0), start)
            pass_block(
                2, False, lambda piece, odd: pl.when(~odd)(lambda: go(piece, 0, 0)), start
            )

        @pl.when(y == 0)
        def _():
            pass_block(3, False, lambda piece, odd: go(piece, 0, 1), start)

    omega_copy.wait()
    for tile in range(4):
        turned = omega_rows[:, tile * 128 : (tile + 1) * 128].astype(F32).T.astype(BF16)
        omega_turned[2 * tile] = turned[:RANK]
        omega_turned[2 * tile + 1] = turned[RANK:]

    pass_all(True)
    keys_copy.wait()
    others(KVH, k, lambda d: k_copy(d, d).wait_recv())

    lane = lax.broadcasted_iota(jnp.int32, (1, BLOCK), 1)
    place = lax.rem(lane, 16)
    row_in_block = lane - place + 2 * lax.rem(place, 8) + lax.div(place, 8)
    key_row = lax.broadcasted_iota(jnp.int32, (CHUNK, 1), 0)

    def block_of(row, block):
        return row[:, block * BLOCK : (block + 1) * BLOCK]

    def limits(block):
        return offsets[block] * BLOCK + row_in_block - s * KEYS

    def fold(tile, join):
        return join(tile.reshape(CHUNK // 8, 8, tile.shape[1]), axis=0)

    def head_at(index):
        plane = lax.rem(y + lax.div(index, 2), PLANES)
        j = lax.rem(index, 2)
        return plane, j, 2 * plane + j

    def spans(plane, act, everything=False):
        whole = (z == 0) | everything
        if isinstance(plane, int):
            if plane:
                act(plane)
            else:
                pl.when(whole)(lambda: act(0))
                pl.when(~whole)(lambda: act(1))
        else:
            pl.when((plane == 0) & whole)(lambda: act(0))
            pl.when((plane == 1) | ((plane == 0) & ~whole))(lambda: act(1))
            pl.when(plane == 2)(lambda: act(2))
            pl.when(plane == 3)(lambda: act(3))

    def cut(ref, *place, first):
        return ref.at[(*place, pl.ds(first, PLANES - first))]

    def y_send(out, landing, send, recv, head, plane, j, start):
        @pl.when(plane != y)
        def _():
            def act(first):
                copy = remote(
                    cut(out, head, first=first), cut(landing, y, j, first=first),
                    send.at[head], recv.at[y, j], seq=at_seq(plane, z),
                )
                if start:
                    copy.start()
                else:
                    copy.wait_send()

            spans(y, act)

    def y_wait(out, landing, send, recv, j):
        for plane in range(PLANES):
            @pl.when(plane != y)
            def _():
                def act(first):
                    remote(
                        cut(out, 0, first=first), cut(landing, plane, j, first=first),
                        send.at[0], recv.at[plane, j], seq=at_seq(plane, z),
                    ).wait_recv()

                spans(plane, act)

    def z_send(through, landing, send, recv, j, start):
        target = owner_z(j)

        @pl.when(target != z)
        def _():
            def act(first):
                copy = remote(
                    cut(through, j, first=first), cut(landing, z, first=first),
                    send.at[j], recv.at[z], seq=at_seq(y, target),
                )
                if start:
                    copy.start()
                else:
                    copy.wait_send()

            spans(0, act)

    def z_wait(through, landing, send, recv):
        def run(d):
            for first in (0, 1):
                @pl.when((d == 0) if first == 0 else (d != 0))
                def _():
                    remote(
                        cut(through, 0, first=first), cut(landing, d, first=first),
                        send.at[0], recv.at[d], seq=at_seq(y, d),
                    ).wait_recv()

        others(RING, z, run)

    def stat_y_copy(head, plane, j, source):
        return remote(
            stat_out.at[head], stat_y.at[source, j], sty_send.at[head], sty_recv.at[source, j],
            seq=at_seq(plane, z),
        )

    def first_block(block, columns, heads, masked):
        rows = pl.ds(pl.multiple_of(8 * block, 8), 8)
        q_heads = jnp.concatenate([q_all[h, rows].reshape(BLOCK, HEAD) for h in heads], axis=0)
        limit = limits(block)
        limit = jnp.concatenate([limit] * len(heads), axis=1)
        largest = jnp.full((8, len(heads) * BLOCK), LOWEST, F32)
        for chunk in range(KEYS // CHUNK):
            at = slice(chunk * CHUNK, (chunk + 1) * CHUNK)
            piece = dot(k_all[chunk], q_heads, LANES)
            if masked:
                piece = jnp.where(key_row + chunk * CHUNK <= limit, piece, MASKED)
            for n, head in enumerate(heads):
                scores[head, at, columns] = block_of(piece, n)
            largest = jnp.maximum(largest, fold(piece, jnp.max))
        top = jnp.max(largest, axis=0, keepdims=True)
        totals = [jnp.zeros((8, BLOCK), F32) for _ in heads]
        for chunk in range(KEYS // CHUNK):
            at = slice(chunk * CHUNK, (chunk + 1) * CHUNK)
            for n, head in enumerate(heads):
                weight = jnp.exp2((scores[head, at, columns] - block_of(top, n)) * SCALE)
                totals[n] = totals[n] + fold(weight, jnp.sum)
                probs[head, at, columns] = weight.astype(BF16)
        place = pl.ds(pl.multiple_of(block * BLOCK, BLOCK), BLOCK)
        for n, head in enumerate(heads):
            stat_out[head, 0:1, place] = block_of(top, n)
            stat_out[head, 1:2, place] = jnp.sum(totals[n], axis=0, keepdims=True)
            wide_out[head, block] = dot(omega_turned[head], probs[head, :, columns])

    def block_zero(head):
        q_head = q_all[head, 0:8].reshape(BLOCK, HEAD)
        piece = jnp.where(key_row <= limits(0), dot(k_all[0], q_head, LANES), MASKED)
        scores_first[head] = piece
        top = jnp.max(piece, axis=0, keepdims=True)
        weight = jnp.exp2((piece - top) * SCALE)
        probs_first[head] = weight.astype(BF16)
        stat_out[head, 0:1, :BLOCK] = top
        stat_out[head, 1:2, :BLOCK] = jnp.sum(weight, axis=0, keepdims=True)
        wide_out[head, 0] = dot(omega_turned[head, :, :BLOCK], probs_first[head])

    @pl.when(s == 0)
    def _():
        others(RING, z, q_arrived)
        each(HEADS, block_zero)

    steps = jnp.where(y == 0, 3, PLANES - y)

    def one_block(step):
        block = jnp.where(y == 0, jnp.where(step == 0, 3, step), y + step)
        columns = pl.ds(pl.multiple_of((block - 1) * BLOCK, BLOCK), BLOCK)

        @pl.when(jnp.where(y == 0, block != 3, (block == 3) & (y < 3)))
        def _():
            each(RING, lambda d: q_arrived(at_seq(block, d)))

        def run(pair):
            two = [head_at(4 * pair + n) for n in range(4)]
            heads = [head for _, _, head in two]
            pl.when(block == y)(lambda: first_block(block, columns, heads, True))
            pl.when(block != y)(lambda: first_block(block, columns, heads, False))

            @pl.when(step == steps - 1)
            def _():
                for plane, j, head in two:
                    send_first(plane, j, head)

        def send_first(plane, j, head):
            @pl.when(plane != y)
            def _():
                stat_y_copy(head, plane, j, y).start()

            y_send(wide_out, wide_y, wy_send, wy_recv, head, plane, j, True)

            @pl.when(plane == y)
            def _():
                wide_y[y, j] = wide_out[head]
                stat_y[y, j] = stat_out[head]

        each(HEADS // 4, run)

    each(steps, one_block)

    def merge_scale(value, top):
        return jnp.exp2((value - top) * SCALE)

    def join_wide(j):
        for plane in range(PLANES):
            @pl.when(plane != y)
            def _():
                stat_y_copy(0, plane, j, plane).wait_recv()

        tops = [stat_y[p, j, 0:1, :] for p in range(PLANES)]
        top = functools.reduce(jnp.maximum, tops)
        scales = [merge_scale(value, top) for value in tops]
        stat_sum[j, 0:1, :] = top
        stat_sum[j, 1:2, :] = sum(stat_y[p, j, 1:2, :] * scales[p] for p in range(PLANES))

        @pl.when(owner_z(j) == z)
        def _():
            stat_z[z] = stat_sum[j]

        @pl.when(owner_z(j) != z)
        def _():
            stat_z_copy(j, z).start()

        y_wait(wide_out, wide_y, wy_send, wy_recv, j)
        for block in range(1, PLANES):
            wide_sum[j, block] = sum(
                wide_y[p, j, block] * block_of(scales[p], block) for p in range(block + 1)
            )

        @pl.when(z == 0)
        def _():
            wide_sum[j, 0] = wide_y[0, j, 0] * block_of(scales[0], 0)

        @pl.when(owner_z(j) == z)
        def _():
            wide_z[z] = wide_sum[j]

        z_send(wide_sum, wide_z, wz_send, wz_recv, j, True)

    def stat_z_copy(j, source):
        return remote(
            stat_sum.at[j], stat_z.at[source], stz_send.at[j], stz_recv.at[source],
            seq=at_seq(y, owner_z(j)),
        )

    def stat_share(d):
        return remote(
            stat_all.at[own_head], stat_all.at[own_head], sta_send.at[d], st_recv.at[own_head],
            seq=at_seq(y, d),
        )

    def around(d, everything, act):
        whole = (d == 0) | everything
        pl.when(whole)(lambda: act(0))
        pl.when(~whole)(lambda: act(1))

    def share_basis(everything, start):
        def run(d):
            def act(first):
                copy = remote(
                    cut(basis, own_head, first=first), cut(basis, own_head, first=first),
                    bz_send.at[d], b_recv.at[own_head], seq=at_seq(y, d),
                )
                if start:
                    copy.start()
                else:
                    copy.wait_send()

            around(d, everything, act)

        others(RING, z, run)

    def store_basis(rows):
        for block in range(PLANES):
            basis[own_head, block] = block_of(rows, block).astype(BF16)

    def own_wide():
        others(RING, z, lambda d: stat_z_copy(0, d).wait_recv())
        top = functools.reduce(jnp.maximum, [stat_z[d, 0:1, :] for d in range(RING)])
        scales = [merge_scale(stat_z[d, 0:1, :], top) for d in range(RING)]
        inverse = 1.0 / sum(stat_z[d, 1:2, :] * scales[d] for d in range(RING))
        stat_all[own_head, 0:1, :] = top
        stat_all[own_head, 1:2, :] = inverse
        others(RING, z, lambda d: stat_share(d).start())
        z_wait(wide_sum, wide_z, wz_send, wz_recv)
        pieces = [wide_z[0, 0] * block_of(scales[0], 0)]
        for block in range(1, PLANES):
            pieces.append(sum(wide_z[d, block] * block_of(scales[d], block) for d in range(RING)))
        store_basis(orthonormal_rows(jnp.concatenate(pieces, axis=1) * inverse))
        share_basis(False, True)

    each(2, join_wide)
    pl.when(owns)(own_wide)

    def stat_pass(j, plane):
        head = 2 * y + j
        return remote(
            stat_all.at[head], stat_all.at[head], stb_send.at[j, plane], st_recv.at[head],
            seq=at_seq(plane, z),
        )

    def stat_wait(head):
        remote(stat_all.at[head], stat_all.at[head], sta_send.at[0], st_recv.at[head], seq=s).wait_recv()

    def relay_stats(j):
        @pl.when(owner_z(j) != z)
        def _():
            stat_wait(2 * y + j)

        others(PLANES, y, lambda plane: stat_pass(j, plane).start())

    def relay_basis(j, last, start):
        head = 2 * y + j
        if start:
            @pl.when(owner_z(j) != z)
            def _():
                def arrived(first):
                    remote(
                        cut(basis, head, first=first), cut(basis, head, first=first),
                        bz_send.at[0], b_recv.at[head], seq=s,
                    ).wait_recv()

                around(z, last, arrived)

        for plane in range(PLANES):
            @pl.when(plane != y)
            def _():
                def act(first):
                    copy = remote(
                        cut(basis, head, first=first), cut(basis, head, first=first),
                        by_send.at[j, plane], b_recv.at[head], seq=at_seq(plane, z),
                    )
                    if start:
                        copy.start()
                    else:
                        copy.wait_send()

                spans(plane, act, last)

    def wait_basis(plane, head, last):
        @pl.when(plane != y)
        def _():
            def act(first):
                remote(
                    cut(basis, head, first=first), cut(basis, head, first=first),
                    by_send.at[0, 0], b_recv.at[head], seq=at_seq(plane, z),
                ).wait_recv()

            spans(y, act, last)

    relay_stats(0)
    relay_stats(1)

    def normalise(index):
        plane, j, head = head_at(index)

        @pl.when(plane != y)
        def _():
            stat_wait(head)

        def run(block):
            columns = pl.ds(pl.multiple_of((block - 1) * BLOCK, BLOCK), BLOCK)
            place = pl.ds(pl.multiple_of(block * BLOCK, BLOCK), BLOCK)
            top = stat_all[head, 0:1, place]
            inverse = stat_all[head, 1:2, place]
            for chunk in range(KEYS // CHUNK):
                at = slice(chunk * CHUNK, (chunk + 1) * CHUNK)
                weight = merge_scale(scores[head, at, columns], top)
                probs[head, at, columns] = (weight * inverse).astype(BF16)

        each(PLANES, run, jnp.maximum(y, 1))

        @pl.when(s == 0)
        def _():
            weight = merge_scale(scores_first[head], stat_all[head, 0:1, :BLOCK])
            probs_first[head] = (weight * stat_all[head, 1:2, :BLOCK]).astype(BF16)

    @pl.when(owns)
    def _():
        relay_basis(own_j, False, True)

    each(HEADS, normalise)

    def forward(head, plane, j, panel):
        product = dot(panel, probs[head]).astype(BF16)
        for b in range(3):
            part_out[head, b + 1] = product[:, b * BLOCK : (b + 1) * BLOCK]

        @pl.when(s == 0)
        def _():
            part_out[head, 0] = dot(panel[:, :BLOCK], probs_first[head]).astype(BF16)

        @pl.when(plane == y)
        def _():
            part_y[y, j] = part_out[head]

    def backward(head):
        low = jnp.concatenate([basis[head, 1], basis[head, 2], basis[head, 3]], axis=1)
        product = dot(low, probs[head], LANES)
        first = dot(basis[head, 0], probs_first[head], LANES)
        return jnp.concatenate([product[:, :BLOCK] + first, product[:, BLOCK:]], axis=1)

    def join_parts(j):
        y_wait(part_out, part_y, py_send, py_recv, j)
        relay_basis(j, False, False)
        for block in range(1, PLANES):
            part_sum[j, block] = sum(
                part_y[p, j, block].astype(F32) for p in range(block + 1)
            ).astype(BF16)

        @pl.when(z == 0)
        def _():
            part_sum[j, 0] = part_y[0, j, 0]

        @pl.when(owner_z(j) == z)
        def _():
            part_z[z] = part_sum[j]

        z_send(part_sum, part_z, pz_send, pz_recv, j, True)

    def own_parts(step):
        z_wait(part_sum, part_z, pz_send, pz_recv)
        pieces = [part_z[0, 0].astype(F32)]
        for block in range(1, PLANES):
            pieces.append(sum(part_z[d, block].astype(F32) for d in range(RING)))
        rows = orthonormal_rows(jnp.concatenate(pieces, axis=1))
        share_basis(False, False)
        store_basis(rows)
        share_basis(step == POWER - 1, True)
        relay_basis(own_j, step == POWER - 1, True)

    def settle():
        others(KVH, k, lambda d: q_copy(d, k).wait_send())
        others(KVH, k, lambda d: k_copy(d, k).wait_send())
        q_rounds(lambda d: q_round(d).wait_send())
        pass_all(False)

        def sent_wide(index):
            plane, j, head = head_at(index)

            @pl.when(plane != y)
            def _():
                stat_y_copy(head, plane, j, y).wait_send()

            y_send(wide_out, wide_y, wy_send, wy_recv, head, plane, j, False)

        each(HEADS, sent_wide)
        for j in range(2):
            z_send(wide_sum, wide_z, wz_send, wz_recv, j, False)

            @pl.when(owner_z(j) != z)
            def _():
                stat_z_copy(j, z).wait_send()

            others(PLANES, y, lambda plane: stat_pass(j, plane).wait_send())

        @pl.when(owns)
        def _():
            others(RING, z, lambda d: stat_share(d).wait_send())

    def power_step(step):
        def relay(j):
            pl.when(owner_z(j) != z)(lambda: relay_basis(j, False, True))

        def one_head(index):
            plane, j, head = head_at(index)
            wait_basis(plane, head, False)
            forward(head, plane, j, backward(head).astype(BF16))
            y_send(part_out, part_y, py_send, py_recv, head, plane, j, True)

        each(2, relay)
        each(HEADS, one_head)
        each(2, join_parts)
        pl.when(owns)(lambda: own_parts(step))

        def sent(index):
            plane, j, head = head_at(index)
            y_send(part_out, part_y, py_send, py_recv, head, plane, j, False)

        each(HEADS, sent)
        z_send(part_sum, part_z, pz_send, pz_recv, 0, False)
        z_send(part_sum, part_z, pz_send, pz_recv, 1, False)
        pl.when(step == 0)(settle)

    each(POWER, power_step)

    def store_copy(head):
        rows = pl.ds(pl.multiple_of(head * RANK, RANK), RANK)
        return pltpu.make_async_copy(staged.at[rows], proj_hbm.at[rows], store_sem.at[head])

    def last_relay(j):
        pl.when(owner_z(j) != z)(lambda: relay_basis(j, True, True))

    each(2, last_relay)

    def last_head(index):
        plane, j, head = head_at(index)
        wait_basis(plane, head, True)
        rows = pl.ds(pl.multiple_of(head * RANK, RANK), RANK)
        staged[rows, :] = backward(head)
        store_copy(head).start()

    each(HEADS, last_head)

    row = lax.broadcasted_iota(jnp.int32, (16, QUERIES), 0)
    lane = lax.broadcasted_iota(jnp.int32, (16, QUERIES), 1)
    chosen = lane == s * 16 + 8 * lax.rem(row, 2) + lax.div(row, 2)
    chosen = jnp.where(chosen, 1.0, 0.0).astype(BF16)
    total = jnp.zeros((16, HEADS * RANK), F32)
    for block in range(PLANES):
        total = total + dot(
            chosen[:, block * BLOCK : (block + 1) * BLOCK],
            basis[:, block].reshape(HEADS * RANK, BLOCK),
            LANES,
        )
    chosen_rows[...] = total
    basis_copy = pltpu.make_async_copy(chosen_rows, basis_hbm, local_sem.at[0])
    basis_copy.start()

    each(HEADS, lambda head: store_copy(head).wait())
    basis_copy.wait()
    for j in range(2):
        relay_basis(j, True, False)
    pl.when(owns)(lambda: share_basis(True, False))


def scale_kernel(basis_ref, rows_ref, basis_out, rows_out):
    basis_out[...] = basis_ref[...] * math.sqrt(QUERIES)
    rows_out[...] = rows_ref[...] * math.sqrt(SEQ * KEYS)


def scaled(basis, projection):
    steps = 2
    rows = projection.shape[0] // steps
    whole = pl.BlockSpec(basis.shape, lambda i: (0, 0))
    part = pl.BlockSpec((rows, projection.shape[1]), lambda i: (i, 0))
    return pl.pallas_call(
        scale_kernel,
        out_shape=(
            jax.ShapeDtypeStruct(basis.shape, F32),
            jax.ShapeDtypeStruct(projection.shape, F32),
        ),
        grid=(steps,),
        in_specs=[whole, part],
        out_specs=(whole, part),
        name="scale_results",
    )(basis, projection)


def body(queries, keys, omega, block_offsets):
    vmem = lambda shape, kind: pltpu.VMEM(shape, kind)
    dma = lambda *shape: pltpu.SemaphoreType.DMA(shape)
    panel = (PLANES, RANK, BLOCK)
    basis, projection = pl.pallas_call(
        kernel,
        out_shape=(
            jax.ShapeDtypeStruct((16, HEADS * RANK), F32),
            jax.ShapeDtypeStruct((HEADS * RANK, KEYS), F32),
        ),
        in_specs=[
            pl.BlockSpec(memory_space=pl.ANY),
            pl.BlockSpec(memory_space=pl.ANY),
            pl.BlockSpec(memory_space=pl.ANY),
            pl.BlockSpec(memory_space=pl.ANY),
        ],
        out_specs=(
            pl.BlockSpec(memory_space=pl.ANY),
            pl.BlockSpec(memory_space=pl.ANY),
        ),
        scratch_shapes=[
            vmem((128, HEAD), F32),
            vmem((KVH, 16, HEAD), BF16),
            vmem((KVH, 16, HEAD), BF16),
            vmem((128, HEAD), F32),
            vmem((128, HEAD), F32),
            vmem((HEADS, 16, HEAD), BF16),
            vmem((HEADS, SEQ, 16, HEAD), BF16),
            vmem((KVH, 128, HEAD), BF16),
            vmem((KEYS, HEADS * RANK), BF16),
            vmem((HEADS, RANK, KEYS), BF16),
            vmem((HEADS, KEYS, WIDE), F32),
            vmem((HEADS, BLOCK, BLOCK), F32),
            vmem((HEADS, KEYS, WIDE), BF16),
            vmem((HEADS, BLOCK, BLOCK), BF16),
            vmem((HEADS, 2, QUERIES), F32),
            vmem((PLANES, 2, 2, QUERIES), F32),
            vmem((2, 2, QUERIES), F32),
            vmem((RING, 2, QUERIES), F32),
            vmem((HEADS, 2, QUERIES), F32),
            vmem((HEADS, *panel), F32),
            vmem((PLANES, 2, *panel), F32),
            vmem((2, *panel), F32),
            vmem((RING, *panel), F32),
            vmem((HEADS, *panel), BF16),
            vmem((PLANES, 2, *panel), BF16),
            vmem((2, *panel), BF16),
            vmem((RING, *panel), BF16),
            vmem((HEADS, *panel), BF16),
            vmem((HEADS * RANK, KEYS), F32),
            vmem((16, HEADS * RANK), F32),
            pltpu.SMEM((4,), jnp.int32),
            vmem((2, KVH * HEADS * HEAD), BF16),
            dma(4),
            dma(HEADS),
            dma(KVH), dma(KVH),
            dma(KVH), dma(KVH),
            dma(RING), dma(2, SEQ), dma(SEQ),
            dma(HEADS), dma(PLANES, 2),
            dma(2), dma(RING),
            dma(RING), dma(2, PLANES), dma(HEADS),
            dma(HEADS), dma(PLANES, 2),
            dma(2), dma(RING),
            dma(HEADS), dma(PLANES, 2),
            dma(2), dma(RING),
            dma(RING), dma(2, PLANES), dma(HEADS),
        ],
        compiler_params=pltpu.CompilerParams(
            collective_id=0, has_side_effects=True, vmem_limit_bytes=56 * 2**20
        ),
        cost_estimate=pl.CostEstimate(
            flops=6 * 10**9, bytes_accessed=8 * 2**20, transcendentals=8 * 10**6
        ),
        name="range_finder",
    )(block_offsets, queries, keys, omega)
    return scaled(basis, projection)


def solution(mesh):
    placed = (P(("seq", "kvh"), None), P(("seq", "kvh"), None), P("seq", "kvh"), P())
    return jax.shard_map(
        body,
        mesh=mesh,
        in_specs=placed,
        out_specs=(P("seq", "kvh"), P("kvh", "seq")),
        check_vma=False,
    )
```

```python
import functools
import math

import jax
import jax.numpy as jnp
from jax import lax
from jax.experimental import pallas as pl
from jax.experimental.pallas import tpu as pltpu
from jax.sharding import PartitionSpec as P

MESH = pl.DeviceIdType.MESH
F32 = jnp.float32
BF16 = jnp.bfloat16
HIGHEST = lax.Precision.HIGHEST

SEQ = 32
KVH = 8
PLANES = 4
RING = 8
HEADS = 8
HEAD = 128
RANK = 64
BLOCK = 128
QUERIES = 512
WIDE = QUERIES - BLOCK
KEYS = 1024
POWER = 2
CHUNK = 128

MASKED = -1e30
LOWEST = -1e29
SCALE = math.log2(math.e) / math.sqrt(HEAD)

LANES = (((1,), (1,)), ((), ()))
PLAIN = (((1,), (0,)), ((), ()))


def dot(left, right, dims=PLAIN, precision=None):
    return lax.dot_general(left, right, dims, precision=precision, preferred_element_type=F32)


def each(count, step, start=0):
    def run(index, carry):
        step(index)
        return carry

    lax.fori_loop(start, count, run, 0)


def inverse_factor(gram):
    lanes = lax.broadcasted_iota(jnp.int32, (RANK, RANK), 1)
    rows = lax.broadcasted_iota(jnp.int32, (RANK, RANK), 0)
    start = jnp.concatenate([gram, jnp.where(lanes == rows, 1.0, 0.0)], axis=1)
    sub = lax.broadcasted_iota(jnp.int32, (8, 2 * RANK), 0)

    def spread(tile, lane):
        return jnp.broadcast_to(tile[:, lane : lane + 1], tile.shape)

    def lift(tile, row):
        return jnp.broadcast_to(tile[row : row + 1, :], tile.shape)

    tiles = [start[8 * i : 8 * i + 8] for i in range(8)]
    for step in range(8):
        pivot = tiles[step]
        columns = [spread(pivot, 8 * step + j) for j in range(8)]
        inverses, upper, roots = [], [], jnp.zeros_like(pivot)
        for j in range(8):
            diagonal = lift(columns[j], j)
            inverse = 1.0 / diagonal
            inverses.append(inverse)
            roots = jnp.where(sub == j, lax.rsqrt(diagonal), roots)
            factor = jnp.where(sub > j, columns[j] * inverse, 0.0)
            pivot = pivot - factor * lift(pivot, j)
            across = {}
            for other in range(j + 1, 8):
                across[other] = lift(columns[other], j)
                columns[other] = columns[other] - factor * across[other]
            upper.append(across)
        pivot_rows = [lift(pivot, j) for j in range(8)]
        for index in range(step + 1, 8):
            tile = tiles[index]
            columns = [spread(tile, 8 * step + j) for j in range(8)]
            for j in range(8):
                factor = columns[j] * inverses[j]
                tile = tile - factor * pivot_rows[j]
                for other in range(j + 1, 8):
                    columns[other] = columns[other] - factor * upper[j][other]
            tiles[index] = tile
        tiles[step] = pivot * roots
    return jnp.concatenate(tiles, axis=0)[:, RANK:]


def orthonormal_rows(panel):
    gram = dot(panel, panel, LANES, HIGHEST)
    return dot(inverse_factor(gram), panel, PLAIN, HIGHEST)


def kernel(
    offsets_hbm,
    q_hbm,
    k_hbm,
    omega_hbm,
    basis_hbm,
    proj_hbm,
    q_wide,
    q_tiles,
    q_got,
    q_flat,
    q_turned,
    q_own,
    q_all,
    k_all,
    omega_rows,
    omega_turned,
    scores,
    scores_first,
    probs,
    probs_first,
    stat_out,
    stat_y,
    stat_sum,
    stat_z,
    stat_all,
    wide_out,
    wide_y,
    wide_sum,
    wide_z,
    part_out,
    part_y,
    part_sum,
    part_z,
    basis,
    staged,
    chosen_rows,
    offsets,
    q_ref,
    local_sem,
    store_sem,
    qk_send,
    qk_recv,
    kk_send,
    kk_recv,
    qz_send,
    qf_send,
    q_recv,
    sty_send,
    sty_recv,
    stz_send,
    stz_recv,
    sta_send,
    stb_send,
    st_recv,
    wy_send,
    wy_recv,
    wz_send,
    wz_recv,
    py_send,
    py_recv,
    pz_send,
    pz_recv,
    bz_send,
    by_send,
    b_recv,
):
    s = lax.axis_index("seq")
    k = lax.axis_index("kvh")
    y = lax.div(s, RING)
    z = lax.rem(s, RING)
    core = lax.rem(k, 2)

    def owner_z(j):
        return 2 * (2 * j + core)

    own_j = lax.div(z, 4)
    own_head = 2 * y + own_j
    owns = owner_z(own_j) == z

    def at_seq(plane, place):
        return plane * RING + place

    def remote(src, dst, send, recv, **target):
        return pltpu.make_async_remote_copy(
            src_ref=src, dst_ref=dst, send_sem=send, recv_sem=recv,
            device_id=target, device_id_type=MESH,
        )

    def others(count, me, step):
        def run(d):
            @pl.when(d != me)
            def _():
                step(d)

        each(count, run)

    offsets_copy = pltpu.make_async_copy(offsets_hbm, offsets, local_sem.at[2])
    q_copy_in = pltpu.make_async_copy(q_hbm, q_ref, local_sem.at[3])
    q_copy_in.start()
    offsets_copy.start()
    barrier = pltpu.get_barrier_semaphore()

    def greet(**target):
        pl.semaphore_signal(barrier, inc=1, device_id=target, device_id_type=MESH)

    for hop in (4, 3, 5, 2, 6, 1, 7):
        greet(seq=at_seq(y, lax.rem(z + hop, RING)))
    for hop in (2, 1, 3):
        greet(seq=at_seq(lax.rem(y + hop, PLANES), z))
    others(KVH, k, lambda d: greet(kvh=d))

    omega_copy = pltpu.make_async_copy(omega_hbm, omega_rows, local_sem.at[0])
    omega_copy.start()
    keys_copy = pltpu.make_async_copy(
        k_hbm.at[:, pl.ds(pl.multiple_of(k * HEAD, HEAD), HEAD)], k_all.at[k], local_sem.at[1]
    )
    keys_copy.start()

    q_copy_in.wait()
    offsets_copy.wait()
    q_now = q_ref[...].astype(F32)
    for tile in range(KVH * HEADS):
        q_wide[2 * tile : 2 * tile + 2, :] = q_now[:, tile * HEAD : (tile + 1) * HEAD]
    q_tiles[...] = q_wide[...].astype(BF16).reshape(KVH, 16, HEAD)
    q_got[k] = q_tiles[k]

    basis[...] = jnp.zeros(basis.shape, BF16)
    probs_first[...] = jnp.zeros(probs_first.shape, BF16)
    stat_out[:, 0:1, :] = jnp.full((HEADS, 1, QUERIES), LOWEST, F32)
    stat_out[:, 1:2, :] = jnp.zeros((HEADS, 1, QUERIES), F32)

    @pl.when(y >= 2)
    def _():
        def clear(head):
            probs[head] = jnp.zeros((KEYS, WIDE), BF16)

        each(HEADS, clear)

    pl.semaphore_wait(barrier, KVH - 1 + RING - 1 + PLANES - 1)

    def q_copy(d, slot):
        return remote(q_tiles.at[d], q_got.at[slot], qk_send.at[d], qk_recv.at[slot], kvh=d)

    def k_copy(d, slot):
        columns = pl.ds(pl.multiple_of(d * HEAD, HEAD), HEAD)
        return remote(k_hbm.at[:, columns], k_all.at[slot], kk_send.at[d], kk_recv.at[slot], kvh=d)

    others(KVH, k, lambda d: q_copy(d, k).start())
    others(KVH, k, lambda d: k_copy(d, k).start())
    others(KVH, k, lambda d: q_copy(d, d).wait_recv())

    q_flat[...] = q_got[...].astype(F32).reshape(KVH * 16, HEAD)
    for pair in range(16):
        q_turned[8 * pair : 8 * pair + 8, :] = q_flat[pl.ds(pair, 8, stride=16), :]
    q_own[...] = q_turned[...].astype(BF16).reshape(HEADS, 16, HEAD)
    q_all[:, s] = q_own[...]

    def q_round(d):
        return remote(q_own, q_all.at[:, s], qz_send.at[d], q_recv.at[s], seq=at_seq(y, d))

    def q_pass(piece, way, plane):
        return remote(
            q_all.at[:, piece], q_all.at[:, piece], qf_send.at[way, piece], q_recv.at[piece],
            seq=at_seq(plane, z),
        )

    def q_arrived(piece):
        remote(q_own, q_all.at[:, piece], qz_send.at[0], q_recv.at[piece], seq=piece).wait_recv()

    def q_rounds(step):
        def run(index):
            d = lax.rem(z + index, RING)

            @pl.when((y > 0) | (d == 0))
            def _():
                step(d)

        each(RING, run, 1)

    q_rounds(lambda d: q_round(d).start())

    def pass_block(block, own, step, start):
        def run(index):
            place = lax.rem(z + index, RING)
            piece = at_seq(block, place)
            if start:
                if own:
                    pl.when(index > 0)(lambda: q_arrived(piece))
                else:
                    q_arrived(piece)
            step(piece, lax.rem(place, 2) == 1)

        each(RING, run)

    def pass_all(start):
        def go(piece, way, plane):
            copy = q_pass(piece, way, plane)
            if start:
                copy.start()
            else:
                copy.wait_send()

        @pl.when(y == 3)
        def _():
            def both(piece, odd):
                go(piece, 0, 0)
                go(piece, 1, 2)

            pass_block(3, True, both, start)

            def other(index):
                piece = at_seq(2, 2 * index + 1)
                if start:
                    q_arrived(piece)
                go(piece, 0, 0)

            each(RING // 2, other)

        @pl.when(y == 2)
        def _():
            def both(piece, odd):
                pl.when(odd)(lambda: go(piece, 1, 3))
                go(piece, 0, 1)

            pass_block(2, True, both, start)

        @pl.when(y == 1)
        def _():
            pass_block(1, True, lambda piece, odd: go(piece, 0, 0), start)
            pass_block(
                2, False, lambda piece, odd: pl.when(~odd)(lambda: go(piece, 0, 0)), start
            )

        @pl.when(y == 0)
        def _():
            pass_block(3, False, lambda piece, odd: go(piece, 0, 1), start)

    omega_copy.wait()
    for tile in range(4):
        turned = omega_rows[:, tile * 128 : (tile + 1) * 128].astype(F32).T.astype(BF16)
        omega_turned[2 * tile] = turned[:RANK]
        omega_turned[2 * tile + 1] = turned[RANK:]

    pass_all(True)
    keys_copy.wait()
    others(KVH, k, lambda d: k_copy(d, d).wait_recv())

    lane = lax.broadcasted_iota(jnp.int32, (1, BLOCK), 1)
    place = lax.rem(lane, 16)
    row_in_block = lane - place + 2 * lax.rem(place, 8) + lax.div(place, 8)
    key_row = lax.broadcasted_iota(jnp.int32, (CHUNK, 1), 0)

    def block_of(row, block):
        return row[:, block * BLOCK : (block + 1) * BLOCK]

    def limits(block):
        return offsets[block] * BLOCK + row_in_block - s * KEYS

    def fold(tile, join):
        return join(tile.reshape(CHUNK // 8, 8, tile.shape[1]), axis=0)

    def head_at(index):
        plane = lax.rem(y + lax.div(index, 2), PLANES)
        j = lax.rem(index, 2)
        return plane, j, 2 * plane + j

    def spans(plane, act, everything=False):
        whole = (z == 0) | everything
        if isinstance(plane, int):
            if plane:
                act(plane)
            else:
                pl.when(whole)(lambda: act(0))
                pl.when(~whole)(lambda: act(1))
        else:
            pl.when((plane == 0) & whole)(lambda: act(0))
            pl.when((plane == 1) | ((plane == 0) & ~whole))(lambda: act(1))
            pl.when(plane == 2)(lambda: act(2))
            pl.when(plane == 3)(lambda: act(3))

    def cut(ref, *place, first):
        return ref.at[(*place, pl.ds(first, PLANES - first))]

    def y_send(out, landing, send, recv, head, plane, j, start):
        @pl.when(plane != y)
        def _():
            def act(first):
                copy = remote(
                    cut(out, head, first=first), cut(landing, y, j, first=first),
                    send.at[head], recv.at[y, j], seq=at_seq(plane, z),
                )
                if start:
                    copy.start()
                else:
                    copy.wait_send()

            spans(y, act)

    def y_wait(out, landing, send, recv, j):
        for plane in range(PLANES):
            @pl.when(plane != y)
            def _():
                def act(first):
                    remote(
                        cut(out, 0, first=first), cut(landing, plane, j, first=first),
                        send.at[0], recv.at[plane, j], seq=at_seq(plane, z),
                    ).wait_recv()

                spans(plane, act)

    def z_send(through, landing, send, recv, j, start):
        target = owner_z(j)

        @pl.when(target != z)
        def _():
            def act(first):
                copy = remote(
                    cut(through, j, first=first), cut(landing, z, first=first),
                    send.at[j], recv.at[z], seq=at_seq(y, target),
                )
                if start:
                    copy.start()
                else:
                    copy.wait_send()

            spans(0, act)

    def z_wait(through, landing, send, recv):
        def run(d):
            for first in (0, 1):
                @pl.when((d == 0) if first == 0 else (d != 0))
                def _():
                    remote(
                        cut(through, 0, first=first), cut(landing, d, first=first),
                        send.at[0], recv.at[d], seq=at_seq(y, d),
                    ).wait_recv()

        others(RING, z, run)

    def stat_y_copy(head, plane, j, source):
        return remote(
            stat_out.at[head], stat_y.at[source, j], sty_send.at[head], sty_recv.at[source, j],
            seq=at_seq(plane, z),
        )

    def first_block(block, columns, heads, masked):
        rows = pl.ds(pl.multiple_of(8 * block, 8), 8)
        q_heads = jnp.concatenate([q_all[h, rows].reshape(BLOCK, HEAD) for h in heads], axis=0)
        limit = limits(block)
        limit = jnp.concatenate([limit] * len(heads), axis=1)
        largest = jnp.full((8, len(heads) * BLOCK), LOWEST, F32)
        for chunk in range(KEYS // CHUNK):
            at = slice(chunk * CHUNK, (chunk + 1) * CHUNK)
            piece = dot(k_all[chunk], q_heads, LANES)
            if masked:
                piece = jnp.where(key_row + chunk * CHUNK <= limit, piece, MASKED)
            for n, head in enumerate(heads):
                scores[head, at, columns] = block_of(piece, n)
            largest = jnp.maximum(largest, fold(piece, jnp.max))
        top = jnp.max(largest, axis=0, keepdims=True)
        totals = [jnp.zeros((8, BLOCK), F32) for _ in heads]
        for chunk in range(KEYS // CHUNK):
            at = slice(chunk * CHUNK, (chunk + 1) * CHUNK)
            for n, head in enumerate(heads):
                weight = jnp.exp2((scores[head, at, columns] - block_of(top, n)) * SCALE)
                totals[n] = totals[n] + fold(weight, jnp.sum)
                probs[head, at, columns] = weight.astype(BF16)
        place = pl.ds(pl.multiple_of(block * BLOCK, BLOCK), BLOCK)
        for n, head in enumerate(heads):
            stat_out[head, 0:1, place] = block_of(top, n)
            stat_out[head, 1:2, place] = jnp.sum(totals[n], axis=0, keepdims=True)
            wide_out[head, block] = dot(omega_turned[head], probs[head, :, columns])

    def block_zero(head):
        q_head = q_all[head, 0:8].reshape(BLOCK, HEAD)
        piece = jnp.where(key_row <= limits(0), dot(k_all[0], q_head, LANES), MASKED)
        scores_first[head] = piece
        top = jnp.max(piece, axis=0, keepdims=True)
        weight = jnp.exp2((piece - top) * SCALE)
        probs_first[head] = weight.astype(BF16)
        stat_out[head, 0:1, :BLOCK] = top
        stat_out[head, 1:2, :BLOCK] = jnp.sum(weight, axis=0, keepdims=True)
        wide_out[head, 0] = dot(omega_turned[head, :, :BLOCK], probs_first[head])

    @pl.when(s == 0)
    def _():
        others(RING, z, q_arrived)
        each(HEADS, block_zero)

    steps = jnp.where(y == 0, 3, PLANES - y)

    def one_block(step):
        block = jnp.where(y == 0, jnp.where(step == 0, 3, step), y + step)
        columns = pl.ds(pl.multiple_of((block - 1) * BLOCK, BLOCK), BLOCK)

        @pl.when(jnp.where(y == 0, block != 3, (block == 3) & (y < 3)))
        def _():
            each(RING, lambda d: q_arrived(at_seq(block, d)))

        def run(pair):
            two = [head_at(4 * pair + n) for n in range(4)]
            heads = [head for _, _, head in two]
            pl.when(block == y)(lambda: first_block(block, columns, heads, True))
            pl.when(block != y)(lambda: first_block(block, columns, heads, False))

            @pl.when(step == steps - 1)
            def _():
                for plane, j, head in two:
                    send_first(plane, j, head)

        def send_first(plane, j, head):
            @pl.when(plane != y)
            def _():
                stat_y_copy(head, plane, j, y).start()

            y_send(wide_out, wide_y, wy_send, wy_recv, head, plane, j, True)

            @pl.when(plane == y)
            def _():
                wide_y[y, j] = wide_out[head]
                stat_y[y, j] = stat_out[head]

        each(HEADS // 4, run)

    each(steps, one_block)

    def merge_scale(value, top):
        return jnp.exp2((value - top) * SCALE)

    def join_wide(j):
        for plane in range(PLANES):
            @pl.when(plane != y)
            def _():
                stat_y_copy(0, plane, j, plane).wait_recv()

        tops = [stat_y[p, j, 0:1, :] for p in range(PLANES)]
        top = functools.reduce(jnp.maximum, tops)
        scales = [merge_scale(value, top) for value in tops]
        stat_sum[j, 0:1, :] = top
        stat_sum[j, 1:2, :] = sum(stat_y[p, j, 1:2, :] * scales[p] for p in range(PLANES))

        @pl.when(owner_z(j) == z)
        def _():
            stat_z[z] = stat_sum[j]

        @pl.when(owner_z(j) != z)
        def _():
            stat_z_copy(j, z).start()

        y_wait(wide_out, wide_y, wy_send, wy_recv, j)
        for block in range(1, PLANES):
            wide_sum[j, block] = sum(
                wide_y[p, j, block] * block_of(scales[p], block) for p in range(block + 1)
            )

        @pl.when(z == 0)
        def _():
            wide_sum[j, 0] = wide_y[0, j, 0] * block_of(scales[0], 0)

        @pl.when(owner_z(j) == z)
        def _():
            wide_z[z] = wide_sum[j]

        z_send(wide_sum, wide_z, wz_send, wz_recv, j, True)

    def stat_z_copy(j, source):
        return remote(
            stat_sum.at[j], stat_z.at[source], stz_send.at[j], stz_recv.at[source],
            seq=at_seq(y, owner_z(j)),
        )

    def stat_share(d):
        return remote(
            stat_all.at[own_head], stat_all.at[own_head], sta_send.at[d], st_recv.at[own_head],
            seq=at_seq(y, d),
        )

    def around(d, everything, act):
        whole = (d == 0) | everything
        pl.when(whole)(lambda: act(0))
        pl.when(~whole)(lambda: act(1))

    def share_basis(everything, start):
        def run(d):
            def act(first):
                copy = remote(
                    cut(basis, own_head, first=first), cut(basis, own_head, first=first),
                    bz_send.at[d], b_recv.at[own_head], seq=at_seq(y, d),
                )
                if start:
                    copy.start()
                else:
                    copy.wait_send()

            around(d, everything, act)

        others(RING, z, run)

    def store_basis(rows):
        for block in range(PLANES):
            basis[own_head, block] = block_of(rows, block).astype(BF16)

    def own_wide():
        others(RING, z, lambda d: stat_z_copy(0, d).wait_recv())
        top = functools.reduce(jnp.maximum, [stat_z[d, 0:1, :] for d in range(RING)])
        scales = [merge_scale(stat_z[d, 0:1, :], top) for d in range(RING)]
        inverse = 1.0 / sum(stat_z[d, 1:2, :] * scales[d] for d in range(RING))
        stat_all[own_head, 0:1, :] = top
        stat_all[own_head, 1:2, :] = inverse
        others(RING, z, lambda d: stat_share(d).start())
        z_wait(wide_sum, wide_z, wz_send, wz_recv)
        pieces = [wide_z[0, 0] * block_of(scales[0], 0)]
        for block in range(1, PLANES):
            pieces.append(sum(wide_z[d, block] * block_of(scales[d], block) for d in range(RING)))
        store_basis(orthonormal_rows(jnp.concatenate(pieces, axis=1) * inverse))
        share_basis(False, True)

    each(2, join_wide)
    pl.when(owns)(own_wide)

    def stat_pass(j, plane):
        head = 2 * y + j
        return remote(
            stat_all.at[head], stat_all.at[head], stb_send.at[j, plane], st_recv.at[head],
            seq=at_seq(plane, z),
        )

    def stat_wait(head):
        remote(stat_all.at[head], stat_all.at[head], sta_send.at[0], st_recv.at[head], seq=s).wait_recv()

    def relay_stats(j):
        @pl.when(owner_z(j) != z)
        def _():
            stat_wait(2 * y + j)

        others(PLANES, y, lambda plane: stat_pass(j, plane).start())

    def relay_basis(j, last, start):
        head = 2 * y + j
        if start:
            @pl.when(owner_z(j) != z)
            def _():
                def arrived(first):
                    remote(
                        cut(basis, head, first=first), cut(basis, head, first=first),
                        bz_send.at[0], b_recv.at[head], seq=s,
                    ).wait_recv()

                around(z, last, arrived)

        for plane in range(PLANES):
            @pl.when(plane != y)
            def _():
                def act(first):
                    copy = remote(
                        cut(basis, head, first=first), cut(basis, head, first=first),
                        by_send.at[j, plane], b_recv.at[head], seq=at_seq(plane, z),
                    )
                    if start:
                        copy.start()
                    else:
                        copy.wait_send()

                spans(plane, act, last)

    def wait_basis(plane, head, last):
        @pl.when(plane != y)
        def _():
            def act(first):
                remote(
                    cut(basis, head, first=first), cut(basis, head, first=first),
                    by_send.at[0, 0], b_recv.at[head], seq=at_seq(plane, z),
                ).wait_recv()

            spans(y, act, last)

    relay_stats(0)
    relay_stats(1)

    def normalise(index):
        plane, j, head = head_at(index)

        @pl.when(plane != y)
        def _():
            stat_wait(head)

        def run(block):
            columns = pl.ds(pl.multiple_of((block - 1) * BLOCK, BLOCK), BLOCK)
            place = pl.ds(pl.multiple_of(block * BLOCK, BLOCK), BLOCK)
            top = stat_all[head, 0:1, place]
            inverse = stat_all[head, 1:2, place]
            for chunk in range(KEYS // CHUNK):
                at = slice(chunk * CHUNK, (chunk + 1) * CHUNK)
                weight = merge_scale(scores[head, at, columns], top)
                probs[head, at, columns] = (weight * inverse).astype(BF16)

        each(PLANES, run, jnp.maximum(y, 1))

        @pl.when(s == 0)
        def _():
            weight = merge_scale(scores_first[head], stat_all[head, 0:1, :BLOCK])
            probs_first[head] = (weight * stat_all[head, 1:2, :BLOCK]).astype(BF16)

    @pl.when(owns)
    def _():
        relay_basis(own_j, False, True)

    each(HEADS, normalise)

    def forward(head, plane, j, panel):
        product = dot(panel, probs[head]).astype(BF16)
        for b in range(3):
            part_out[head, b + 1] = product[:, b * BLOCK : (b + 1) * BLOCK]

        @pl.when(s == 0)
        def _():
            part_out[head, 0] = dot(panel[:, :BLOCK], probs_first[head]).astype(BF16)

        @pl.when(plane == y)
        def _():
            part_y[y, j] = part_out[head]

    def backward(head):
        low = jnp.concatenate([basis[head, 1], basis[head, 2], basis[head, 3]], axis=1)
        product = dot(low, probs[head], LANES)
        first = dot(basis[head, 0], probs_first[head], LANES)
        return jnp.concatenate([product[:, :BLOCK] + first, product[:, BLOCK:]], axis=1)

    def join_parts(j):
        y_wait(part_out, part_y, py_send, py_recv, j)
        relay_basis(j, False, False)
        for block in range(1, PLANES):
            part_sum[j, block] = sum(
                part_y[p, j, block].astype(F32) for p in range(block + 1)
            ).astype(BF16)

        @pl.when(z == 0)
        def _():
            part_sum[j, 0] = part_y[0, j, 0]

        @pl.when(owner_z(j) == z)
        def _():
            part_z[z] = part_sum[j]

        z_send(part_sum, part_z, pz_send, pz_recv, j, True)

    def own_parts(step):
        z_wait(part_sum, part_z, pz_send, pz_recv)
        pieces = [part_z[0, 0].astype(F32)]
        for block in range(1, PLANES):
            pieces.append(sum(part_z[d, block].astype(F32) for d in range(RING)))
        rows = orthonormal_rows(jnp.concatenate(pieces, axis=1))
        share_basis(False, False)
        store_basis(rows)
        share_basis(step == POWER - 1, True)
        relay_basis(own_j, step == POWER - 1, True)

    def settle():
        others(KVH, k, lambda d: q_copy(d, k).wait_send())
        others(KVH, k, lambda d: k_copy(d, k).wait_send())
        q_rounds(lambda d: q_round(d).wait_send())
        pass_all(False)

        def sent_wide(index):
            plane, j, head = head_at(index)

            @pl.when(plane != y)
            def _():
                stat_y_copy(head, plane, j, y).wait_send()

            y_send(wide_out, wide_y, wy_send, wy_recv, head, plane, j, False)

        each(HEADS, sent_wide)
        for j in range(2):
            z_send(wide_sum, wide_z, wz_send, wz_recv, j, False)

            @pl.when(owner_z(j) != z)
            def _():
                stat_z_copy(j, z).wait_send()

            others(PLANES, y, lambda plane: stat_pass(j, plane).wait_send())

        @pl.when(owns)
        def _():
            others(RING, z, lambda d: stat_share(d).wait_send())

    def power_step(step):
        def relay(j):
            pl.when(owner_z(j) != z)(lambda: relay_basis(j, False, True))

        def one_head(index):
            plane, j, head = head_at(index)
            wait_basis(plane, head, False)
            forward(head, plane, j, backward(head).astype(BF16))
            y_send(part_out, part_y, py_send, py_recv, head, plane, j, True)

        each(2, relay)
        each(HEADS, one_head)
        each(2, join_parts)
        pl.when(owns)(lambda: own_parts(step))

        def sent(index):
            plane, j, head = head_at(index)
            y_send(part_out, part_y, py_send, py_recv, head, plane, j, False)

        each(HEADS, sent)
        z_send(part_sum, part_z, pz_send, pz_recv, 0, False)
        z_send(part_sum, part_z, pz_send, pz_recv, 1, False)
        pl.when(step == 0)(settle)

    each(POWER, power_step)

    def store_copy(head):
        rows = pl.ds(pl.multiple_of(head * RANK, RANK), RANK)
        return pltpu.make_async_copy(staged.at[rows], proj_hbm.at[rows], store_sem.at[head])

    def last_relay(j):
        pl.when(owner_z(j) != z)(lambda: relay_basis(j, True, True))

    each(2, last_relay)

    def last_head(index):
        plane, j, head = head_at(index)
        wait_basis(plane, head, True)
        rows = pl.ds(pl.multiple_of(head * RANK, RANK), RANK)
        staged[rows, :] = backward(head)
        store_copy(head).start()

    each(HEADS, last_head)

    row = lax.broadcasted_iota(jnp.int32, (16, QUERIES), 0)
    lane = lax.broadcasted_iota(jnp.int32, (16, QUERIES), 1)
    chosen = lane == s * 16 + 8 * lax.rem(row, 2) + lax.div(row, 2)
    chosen = jnp.where(chosen, 1.0, 0.0).astype(BF16)
    total = jnp.zeros((16, HEADS * RANK), F32)
    for block in range(PLANES):
        total = total + dot(
            chosen[:, block * BLOCK : (block + 1) * BLOCK],
            basis[:, block].reshape(HEADS * RANK, BLOCK),
            LANES,
        )
    chosen_rows[...] = total
    basis_copy = pltpu.make_async_copy(chosen_rows, basis_hbm, local_sem.at[0])
    basis_copy.start()

    each(HEADS, lambda head: store_copy(head).wait())
    basis_copy.wait()
    for j in range(2):
        relay_basis(j, True, False)
    pl.when(owns)(lambda: share_basis(True, False))


def scale_kernel(basis_ref, rows_ref, basis_out, rows_out):
    basis_out[...] = basis_ref[...] * math.sqrt(QUERIES)
    rows_out[...] = rows_ref[...] * math.sqrt(SEQ * KEYS)


def scaled(basis, projection):
    steps = 1
    rows = projection.shape[0] // steps
    whole = pl.BlockSpec(basis.shape, lambda i: (0, 0))
    part = pl.BlockSpec((rows, projection.shape[1]), lambda i: (i, 0))
    return pl.pallas_call(
        scale_kernel,
        out_shape=(
            jax.ShapeDtypeStruct(basis.shape, F32),
            jax.ShapeDtypeStruct(projection.shape, F32),
        ),
        grid=(steps,),
        in_specs=[whole, part],
        out_specs=(whole, part),
        name="scale_results",
    )(basis, projection)


def body(queries, keys, omega, block_offsets):
    vmem = lambda shape, kind: pltpu.VMEM(shape, kind)
    dma = lambda *shape: pltpu.SemaphoreType.DMA(shape)
    panel = (PLANES, RANK, BLOCK)
    basis, projection = pl.pallas_call(
        kernel,
        out_shape=(
            jax.ShapeDtypeStruct((16, HEADS * RANK), F32),
            jax.ShapeDtypeStruct((HEADS * RANK, KEYS), F32),
        ),
        in_specs=[
            pl.BlockSpec(memory_space=pl.ANY),
            pl.BlockSpec(memory_space=pl.ANY),
            pl.BlockSpec(memory_space=pl.ANY),
            pl.BlockSpec(memory_space=pl.ANY),
        ],
        out_specs=(
            pl.BlockSpec(memory_space=pl.ANY),
            pl.BlockSpec(memory_space=pl.ANY),
        ),
        scratch_shapes=[
            vmem((128, HEAD), F32),
            vmem((KVH, 16, HEAD), BF16),
            vmem((KVH, 16, HEAD), BF16),
            vmem((128, HEAD), F32),
            vmem((128, HEAD), F32),
            vmem((HEADS, 16, HEAD), BF16),
            vmem((HEADS, SEQ, 16, HEAD), BF16),
            vmem((KVH, 128, HEAD), BF16),
            vmem((KEYS, HEADS * RANK), BF16),
            vmem((HEADS, RANK, KEYS), BF16),
            vmem((HEADS, KEYS, WIDE), F32),
            vmem((HEADS, BLOCK, BLOCK), F32),
            vmem((HEADS, KEYS, WIDE), BF16),
            vmem((HEADS, BLOCK, BLOCK), BF16),
            vmem((HEADS, 2, QUERIES), F32),
            vmem((PLANES, 2, 2, QUERIES), F32),
            vmem((2, 2, QUERIES), F32),
            vmem((RING, 2, QUERIES), F32),
            vmem((HEADS, 2, QUERIES), F32),
            vmem((HEADS, *panel), F32),
            vmem((PLANES, 2, *panel), F32),
            vmem((2, *panel), F32),
            vmem((RING, *panel), F32),
            vmem((HEADS, *panel), BF16),
            vmem((PLANES, 2, *panel), BF16),
            vmem((2, *panel), BF16),
            vmem((RING, *panel), BF16),
            vmem((HEADS, *panel), BF16),
            vmem((HEADS * RANK, KEYS), F32),
            vmem((16, HEADS * RANK), F32),
            pltpu.SMEM((4,), jnp.int32),
            vmem((2, KVH * HEADS * HEAD), BF16),
            dma(4),
            dma(HEADS),
            dma(KVH), dma(KVH),
            dma(KVH), dma(KVH),
            dma(RING), dma(2, SEQ), dma(SEQ),
            dma(HEADS), dma(PLANES, 2),
            dma(2), dma(RING),
            dma(RING), dma(2, PLANES), dma(HEADS),
            dma(HEADS), dma(PLANES, 2),
            dma(2), dma(RING),
            dma(HEADS), dma(PLANES, 2),
            dma(2), dma(RING),
            dma(RING), dma(2, PLANES), dma(HEADS),
        ],
        compiler_params=pltpu.CompilerParams(
            collective_id=0, has_side_effects=True, vmem_limit_bytes=56 * 2**20
        ),
        cost_estimate=pl.CostEstimate(
            flops=6 * 10**9, bytes_accessed=8 * 2**20, transcendentals=8 * 10**6
        ),
        name="range_finder",
    )(block_offsets, queries, keys, omega)
    return scaled(basis, projection)


def solution(mesh):
    placed = (P(("seq", "kvh"), None), P(("seq", "kvh"), None), P("seq", "kvh"), P())
    return jax.shard_map(
        body,
        mesh=mesh,
        in_specs=placed,
        out_specs=(P("seq", "kvh"), P("kvh", "seq")),
        check_vma=False,
    )
```
